512 devices in a mesh: hier: 32 (over y, x), col: 16 (over z, core).
Axes of the slice: x: 4, y: 8, z: 8, core: 2. Of those that a mesh axis runs over, the one named last changes fastest.
Arguments:
- densities: float32 [128, 2, 256, 256], P('hier', None, 'col'), may hold values from -6 to 6
- hamiltonian: float32 [256, 256], replicated, may hold values from -0.35355339 to 0.35355339, as said below
- couplings: float32 [2, 256, 256], replicated, may hold values from -0.088388348 to 0.088388348, as said below
- gamma: float32 [2], replicated, may hold values from 0.005 to 0.05
- coeff: float32 [2, 2], replicated, may hold values from -0.5 to 0.5
- node_count: int32 [32], replicated, may hold values from 2 to 4, as said below
Outputs:
- new_densities: float32 [128, 2, 256, 256], P('hier', None, 'col')
The draws below stay inside these ranges and needn't reach their ends.
Inputs may be any that keep to these rules, and one draw needn't show every extreme that they name: `node_count`: at least one index of hier holds 4 nodes; every index holds 2 or more. `hamiltonian`: symmetric. `couplings`: each of the two matrices is symmetric.
All inputs are finite; a program needn't handle non-finite values.
Results may differ from the reference program's by a relative error of at most 0.00012.
Values sent between devices are 32-bit elements; how exact they have to be, the bound alone decides.
No kernel may reach another device: no remote copies, remote signals or barrier semaphores. Data moves between devices by JAX's collectives and lax.ppermute only.
A program may use at most 64 MiB of HBM per device.

```python
import math
import jax
import jax.numpy as jnp
from jax import lax

D = 256
NODE_DEV = 4
DEPTH2 = 2
SHARDS = 32
SLOTS = 128


def draw_hamiltonian(key, part):
    base = jax.random.truncated_normal(key, -4.0, 4.0, (D, D), jnp.float32)
    return ((base + base.T) / jnp.sqrt(2.0 * D)).astype(jnp.float32)


def draw_couplings(key, part):
    base = jax.random.truncated_normal(jax.random.fold_in(key, 7), -4.0, 4.0, (2, D, D), jnp.float32)
    return (0.25 * (base + jnp.swapaxes(base, 1, 2)) / jnp.sqrt(2.0 * D)).astype(jnp.float32)


def draw_node_count(key, part):
    key_counts, key_full = jax.random.split(jax.random.fold_in(key, 11))
    counts = jax.random.randint(key_counts, (SHARDS,), NODE_DEV // 2, NODE_DEV + 1)
    full_index = jax.random.randint(key_full, (), 0, SHARDS)
    return jnp.where(jnp.arange(SHARDS) == full_index, NODE_DEV, counts).astype(jnp.int32)


def steps_of(rng, extent, cuts, smallest, largest):
    level = 1.0
    for axis_at, blocks in cuts:
        draws = jax.random.uniform(jax.random.fold_in(jax.random.fold_in(rng, 6), axis_at), (blocks,), jnp.float32, smallest / len(cuts), largest / len(cuts))
        level = level * jnp.repeat(jnp.exp(draws), extent[axis_at] // blocks).reshape((-1,) + (1,) * (len(extent) - 1 - axis_at))
    return level


def normal_values(stream_key, extent, width, limit, cuts=(), held_as=jnp.bfloat16):
    loudness = steps_of(stream_key, extent, cuts, -0.22, 0.18) if cuts else 1.0
    entries = jax.random.normal(stream_key, extent, jnp.float32) * width * loudness
    return jnp.minimum(jnp.maximum(entries, -limit), limit).astype(held_as)


def setup_inputs(seed: int = 0) -> dict:
    seeds = jax.random.split(jax.random.key(seed), 7)
    return {
        "densities": normal_values(seeds[0], (SLOTS, 2, D, D), 1.0, 6.0, ((0, 32), (2, 16)), jnp.float32),
        "hamiltonian": draw_hamiltonian(jax.random.fold_in(seeds[6], 71), 0),
        "couplings": draw_couplings(jax.random.fold_in(seeds[6], 71), 0),
        "gamma": jnp.clip(jnp.exp(jax.random.uniform(seeds[3], (2,), jnp.float32, math.log(0.005), math.log(0.05))), 0.005, 0.05),
        "coeff": jnp.clip(jax.random.uniform(seeds[4], (2, 2), jnp.float32, -0.5, 0.5), -0.5, 0.5),
        "node_count": draw_node_count(jax.random.fold_in(seeds[6], 71), 0),
    }


step_size = 0.2

def hierarchy(node_count, device, slot):
    shards = node_count.shape[0]
    columns = jnp.arange(shards, dtype=jnp.int32)
    counts = node_count.astype(jnp.int32)
    offsets = (jnp.cumsum(counts) - counts).astype(jnp.int32)
    live_total = (jnp.sum(counts).astype(jnp.int32) // DEPTH2 * DEPTH2).astype(jnp.int32)

    def lookup(table, which):
        return lax.optimization_barrier(jnp.sum(jnp.where(which[:, None] == columns[None, :], table[None, :], 0), axis=1)).astype(jnp.int32)
    index = (lookup(offsets, device) + slot).astype(jnp.int32)
    live = (slot < lookup(counts, device)) & (index < live_total)
    first = index // DEPTH2
    second = index % DEPTH2
    targets = (index + DEPTH2, index + 1, index - DEPTH2, index - 1)
    allowed = (live & (index + DEPTH2 < live_total), live & (second + 1 < DEPTH2), live & (first > 0), live & (second > 0))
    found = []
    for target, valid in zip(targets, allowed):
        owner = (lax.optimization_barrier(jnp.sum((offsets[None, :] <= target[:, None]).astype(jnp.int32), axis=1)) - 1).astype(jnp.int32)
        within = (target - lookup(offsets, owner)).astype(jnp.int32)
        found.append((owner, within, valid))
    return (live, first, second, found)

def combine(upward, downward, raise_w, lower_w, real, imag):
    rise = raise_w[:, None, None]
    fall = lower_w[:, None, None]
    part_re = rise * upward[:, 0] + fall * (real * downward[:, 0] - imag * downward[:, 1])
    part_im = rise * upward[:, 1] + fall * (real * downward[:, 1] + imag * downward[:, 0])
    return jnp.stack([part_re, part_im], axis=1)

def mixes(linked, levels, coeff, sign):
    result = []
    for mode in range(2):
        result.append(combine(linked[mode], linked[mode + 2], jnp.sqrt(levels[mode] + 1.0), jnp.sqrt(levels[mode]), coeff[mode, 0], sign * coeff[mode, 1]))
    return result

def reference(densities, hamiltonian, couplings, gamma, coeff, node_count):
    device = jnp.repeat(jnp.arange(SHARDS, dtype=jnp.int32), NODE_DEV)
    slot = jnp.tile(jnp.arange(NODE_DEV, dtype=jnp.int32), SHARDS)
    live, first, second, found = hierarchy(node_count, device, slot)
    positions = jnp.stack([jnp.where(v, o * NODE_DEV + w, 0).astype(jnp.int32) for o, w, v in found], axis=1)
    valid = jnp.stack([v.astype(jnp.float32) for o, w, v in found], axis=1)
    levels = jnp.stack([first.astype(jnp.float32), second.astype(jnp.float32)], axis=1)
    alive = live.astype(jnp.float32)
    left_mat = jnp.concatenate([hamiltonian, couplings[0], couplings[1]], axis=1)
    right_mat = jnp.concatenate([hamiltonian, couplings[0], couplings[1]], axis=0)
    high = lax.Precision.HIGHEST

    def slope(state):

        def one(block):
            own, pos, val, lev, keep = block
            linked = [jnp.take(state, pos[:, j], axis=0) * val[:, j][:, None, None, None] for j in range(4)]
            lev_pair = (lev[:, 0], lev[:, 1])
            lefts = mixes(linked, lev_pair, coeff, 1.0)
            rights = mixes(linked, lev_pair, coeff, -1.0)
            left = jnp.einsum('ij,scjk->scik', left_mat, jnp.concatenate([own] + lefts, axis=2), precision=high)
            right = jnp.einsum('scij,jk->scik', jnp.concatenate([own] + rights, axis=3), right_mat, precision=high)
            comm = left - right
            damping = (lev[:, 0] * gamma[0] + lev[:, 1] * gamma[1])[:, None, None]
            out_re = comm[:, 1] - damping * own[:, 0]
            out_im = -comm[:, 0] - damping * own[:, 1]
            return jnp.stack([out_re, out_im], axis=1) * keep[:, None, None, None]
        blocks = (state.reshape(SHARDS, NODE_DEV, 2, D, D), positions.reshape(SHARDS, NODE_DEV, 4), valid.reshape(SHARDS, NODE_DEV, 4), levels.reshape(SHARDS, NODE_DEV, 2), alive.reshape(SHARDS, NODE_DEV))
        return lax.map(one, blocks).reshape(SLOTS, 2, D, D)
    first_slope = slope(densities)
    middle = densities + 0.5 * step_size * first_slope
    second_slope = slope(middle)
    return densities + step_size * second_slope
```

```python
import jax
import jax.numpy as jnp
import numpy as np
from jax import lax
from jax.experimental import pallas as pl
from jax.experimental.pallas import tpu as pltpu
from jax.sharding import Mesh, PartitionSpec as P

STEP = 0.2
HALF2 = 0.5 * STEP * STEP
SLOTS = 4
BF = jnp.bfloat16
F32 = jnp.float32


def split(v):
    hi = v.astype(BF)
    return hi, (v - hi.astype(F32)).astype(BF)


def dot(a, b):
    return jnp.dot(a, b, preferred_element_type=F32)


def granules(vs):
    lane = lax.broadcasted_iota(jnp.int32, vs[0].shape, 1) // 16
    for bit in (4, 2, 1):
        low = (lane & bit) == 0
        out = list(vs)
        for a in range(8):
            if not a & bit:
                b = a | bit
                out[a] = jnp.where(low, vs[a], pltpu.roll(vs[b], 16 * bit, 1))
                out[b] = jnp.where(low, pltpu.roll(vs[a], 128 - 16 * bit, 1), vs[b])
        vs = out
    return vs


class Nodes:
    def __init__(self, count_ref, table_ref, gamma_ref, first, below, above):
        total = jnp.int32(0)
        begin = jnp.int32(0)
        shards = count_ref.shape[0]
        for j in range(shards):
            c = count_ref[j]
            total = total + c
            begin = begin + jnp.where(j < first, c, 0)
        self.live = (total >> 1) << 1
        self.base = begin - 4
        self.begin = begin
        self.table = table_ref
        self.gamma = gamma_ref
        counts = [count_ref[jnp.clip(first + i, 0, shards - 1)] for i in range(-below, above)]
        self.counts = counts
        offs = [begin]
        for i in range(below - 1, -1, -1):
            offs.insert(0, offs[0] - counts[i])
        for i in range(below, len(counts) - 1):
            offs.append(offs[-1] + counts[i])
        self.offs = offs

    def slot(self, p):
        g = self.base + p
        which = jnp.int32(0)
        off = self.offs[0]
        for o in self.offs[1:]:
            inside = g >= o
            which = which + inside.astype(jnp.int32)
            off = jnp.where(inside, o, off)
        return which * SLOTS + jnp.clip(g - off, 0, SLOTS - 1)

    def root(self, n):
        return self.table[jnp.clip(n, 0, self.table.shape[0] - 1)]

    def up(self, p):
        g = self.base + p
        return jnp.where((g >= 0) & (g + 2 < self.live), self.root((g >> 1) + 1), 0.0)

    def down(self, p):
        g = self.base + p
        return jnp.where((g >= 2) & (g < self.live), self.root(g >> 1), 0.0)

    def middle(self, p):
        g = self.base + p
        n = (g >> 1).astype(F32)
        ok = (g >= 0) & (g < self.live)
        upper = jnp.where(ok & (g + 2 < self.live), n + 1.0, 0.0)
        return upper + jnp.where(ok & (g >= 2), n, 0.0)

    def even(self, p):
        g = self.base + p
        return jnp.where((g >= 0) & (g < self.live) & ((g & 1) == 0), 1.0, 0.0).astype(F32)

    def odd(self, p):
        g = self.base + p
        return jnp.where((g >= 0) & (g < self.live) & ((g & 1) == 1), 1.0, 0.0).astype(F32)

    def damp(self, p):
        g = self.base + p
        n0 = (g >> 1).astype(F32)
        n1 = (g & 1).astype(F32)
        return n0 * self.gamma[0] + n1 * self.gamma[1]


def scaled(s, v):
    return (s * v[0], s * v[1])


def plus(a, b):
    return (a[0] + b[0], a[1] + b[1])


def times(re, im, v):
    return (re * v[0] - im * v[1], re * v[1] + im * v[0])


def both(nodes, x, p, re, im):
    r = plus(scaled(nodes.up(p), x[p + 2]), scaled(re * nodes.down(p), x[p - 2]))
    t = scaled(im * nodes.down(p), x[p - 2])
    return (r[0] - t[1], r[1] + t[0]), (r[0] + t[1], r[1] - t[0])


def both1(nodes, x, p, re, im):
    r = plus(scaled(nodes.even(p), x[p + 1]), scaled(re * nodes.odd(p), x[p - 1]))
    t = scaled(im * nodes.odd(p), x[p - 1])
    return (r[0] - t[1], r[1] + t[0]), (r[0] + t[1], r[1] - t[0])


def first_order(nodes, x, p, re, im):
    here = nodes.damp(p)

    def w(q):
        return STEP - HALF2 * (here + nodes.damp(q))

    zero = scaled(w(p), x[p])
    up, down = scaled(w(p + 2) * nodes.up(p), x[p + 2]), scaled(w(p - 2) * nodes.down(p), x[p - 2])
    one = plus(up, times(re[0], im[0], down))
    up, down = scaled(w(p + 1) * nodes.even(p), x[p + 1]), scaled(w(p - 1) * nodes.odd(p), x[p - 1])
    two = plus(up, times(re[1], im[1], down))
    return zero, one, two


def put(hi_ref, lo_ref, block, col, j, rows, v):
    hi, lo = split(jnp.concatenate([v[0], v[1]], axis=0))
    at = pl.ds(block * 128 + j * rows, rows)
    hi_ref[at, 256 * col : 256 * col + 256] = hi
    lo_ref[at, 256 * col : 256 * col + 256] = lo


def times_weights(hi_ref, lo_ref, ghi_ref, glo_ref):
    hi, g = hi_ref[...], ghi_ref[...]
    return dot(hi, g) + dot(lo_ref[...], g) + dot(hi, glo_ref[...])


def weights_kernel(h_ref, q_ref, vhi, vlo, hhi, hlo):
    for b in range(3):
        hi, lo = split(h_ref[...] if b == 0 else q_ref[b - 1])
        vhi[256 * b : 256 * b + 256, :] = hi
        vlo[256 * b : 256 * b + 256, :] = lo
        hhi[:, 256 * b : 256 * b + 256] = hi
        hlo[:, 256 * b : 256 * b + 256] = lo


def pack_kernel(x_ref, near_ref, far_ref, o_ref):
    for g, ref in enumerate((x_ref, near_ref, far_ref)):
        o_ref[:, 8 * g : 8 * g + 8, :] = ref[...].T.reshape(32, 8, 128)


def column_kernel(
    me_ref, count_ref, table_ref, gamma_ref, coeff_ref, got_ref, ghi_ref, glo_ref, o_ref, y_ref, hi_ref, lo_ref, hi2_ref, lo2_ref, z_ref
):
    nodes = Nodes(count_ref, table_ref, gamma_ref, 2 * me_ref[0], 2, 4)
    re = (coeff_ref[0, 0], coeff_ref[1, 0])
    im = (coeff_ref[0, 1], coeff_ref[1, 1])
    places = ((2, 0), (1, 0), (0, 0), (0, 1), (1, 1), (2, 1))
    for i, (g, r) in enumerate(places):
        vs = []
        for low in range(8):
            vs.append(jnp.concatenate([got_ref[(8 * high + low) * 2 + r, 8 * g : 8 * g + 8, :] for high in range(2)], axis=0))
        for m, v in enumerate(granules(vs)):
            y_ref[SLOTS * i + m // 2, m % 2] = jnp.concatenate([v[:8], v[8:]], axis=1)
    x = []
    for p in range(16):
        v = y_ref[nodes.slot(p)]
        x.append((v[0], v[1]))
    a2, b2 = {}, {}
    for p in range(2, 14):
        a2[p], b2[p] = both1(nodes, x, p, re[1], im[1])
    for j in range(8):
        p = j + 4
        a1, b1 = both(nodes, x, p, re[0], im[0])
        a12, b1a2 = both(nodes, a2, p, re[0], im[0])
        a1b2, _ = both(nodes, b2, p, re[0], im[0])
        far = scaled(nodes.up(p) * nodes.up(p + 2), x[p + 4])
        low = scaled(nodes.down(p) * nodes.down(p - 2), x[p - 4])
        mid = nodes.middle(p)
        here = scaled(mid, x[p])
        a11 = plus(plus(far, times(re[0], im[0], here)), times(re[0] * re[0] - im[0] * im[0], 2.0 * re[0] * im[0], low))
        s11 = plus(plus(scaled(2.0, far), scaled(2.0 * re[0], here)), scaled(2.0 * (re[0] * re[0] + im[0] * im[0]), low))
        rows = (
            (x[p], a1, a2[p]),
            (a1, a11, a12),
            (a2[p], a12, times(re[1], im[1], x[p])),
            (scaled(2.0, b1), s11, scaled(2.0, b1a2)),
            (scaled(2.0, b2[p]), scaled(2.0, a1b2), scaled(2.0 * re[1], x[p])),
        )
        for block, row in enumerate(rows):
            for col, v in enumerate(row):
                put(hi_ref, lo_ref, block, col, j, 16, v)
    sums = times_weights(hi_ref, lo_ref, ghi_ref, glo_ref)
    for j in range(8):
        p = j + 4
        for block, v in enumerate(first_order(nodes, x, p, re, im)):
            s = sums[block * 128 + 16 * j : block * 128 + 16 * j + 16]
            put(hi2_ref, lo2_ref, 0, block, j, 16, (v[1] - HALF2 * s[:8], -v[0] - HALF2 * s[8:]))
        z_ref[1, j] = (2.0 * HALF2) * sums[16 * j : 16 * j + 16].reshape(2, 8, 256)
        z_ref[2, j] = HALF2 * sums[384 + 16 * j : 400 + 16 * j].reshape(2, 8, 256)
        z_ref[3, j] = HALF2 * sums[512 + 16 * j : 528 + 16 * j].reshape(2, 8, 256)
    z_ref[0] = times_weights(hi2_ref, lo2_ref, ghi_ref, glo_ref).reshape(8, 2, 8, 256)
    own = nodes.counts[2]
    for z in range(4):
        for r in range(2):
            vs = []
            for m in range(8):
                v = z_ref[z, m // 2 if r == 0 else own + m // 2, m % 2]
                vs.append(jnp.concatenate([v[:, :128], v[:, 128:]], axis=0))
            for low, v in enumerate(granules(vs)):
                for high in range(2):
                    o_ref[(8 * high + low) * 2 + r, 8 * z : 8 * z + 8, :] = v[8 * high : 8 * high + 8]


def row_kernel(
    me_ref, count_ref, table_ref, gamma_ref, coeff_ref, x_ref, p1_ref, p2_ref, p3_ref, p4_ref, ghi_ref, glo_ref, o_ref, w_ref, hi_ref, lo_ref, hi2_ref, lo2_ref
):
    me = me_ref[0] * 2 + me_ref[1]
    nodes = Nodes(count_ref, table_ref, gamma_ref, me, 2, 3)
    re = (coeff_ref[0, 0], coeff_ref[1, 0])
    im = (-coeff_ref[0, 1], -coeff_ref[1, 1])
    up = me_ref[1]
    w_ref[pl.ds(2 * SLOTS, SLOTS)] = x_ref[...]
    w_ref[pl.ds((1 + 2 * up) * SLOTS, SLOTS)] = p1_ref[...]
    w_ref[pl.ds(4 * up * SLOTS, SLOTS)] = p2_ref[...]
    w_ref[pl.ds((3 - 2 * up) * SLOTS, SLOTS)] = p3_ref[...]
    w_ref[pl.ds((4 - 4 * up) * SLOTS, SLOTS)] = p4_ref[...]
    x = []
    for p in range(12):
        v = w_ref[nodes.slot(p)]
        x.append((v[0], v[1]))
    b2 = {}
    for p in range(2, 10):
        b2[p], _ = both1(nodes, x, p, re[1], im[1])
    for j in range(4):
        p = j + 4
        b1, _ = both(nodes, x, p, re[0], im[0])
        b12, _ = both(nodes, b2, p, re[0], im[0])
        far = scaled(nodes.up(p) * nodes.up(p + 2), x[p + 4])
        low = scaled(nodes.down(p) * nodes.down(p - 2), x[p - 4])
        here = scaled(nodes.middle(p), x[p])
        b11 = plus(plus(far, times(re[0], im[0], here)), times(re[0] * re[0] - im[0] * im[0], 2.0 * re[0] * im[0], low))
        rows = ((x[p], b1, b2[p]), (b1, b11, b12), (b2[p], b12, times(re[1], im[1], x[p])))
        for block, row in enumerate(rows):
            for col, v in enumerate(row):
                put(hi_ref, lo_ref, block, col, j, 32, v)
    sums = times_weights(hi_ref, lo_ref, ghi_ref, glo_ref)
    for j in range(4):
        p = j + 4
        for block, v in enumerate(first_order(nodes, x, p, re, im)):
            s = sums[block * 128 + 32 * j : block * 128 + 32 * j + 32]
            put(hi2_ref, lo2_ref, 0, block, j, 32, (-v[1] - HALF2 * s[:16], v[0] - HALF2 * s[16:]))
    right = times_weights(hi2_ref, lo2_ref, ghi_ref, glo_ref)
    for j in range(4):
        d = nodes.damp(j + 4)
        keep = 1.0 - STEP * d + HALF2 * d * d
        old = x_ref[j].reshape(32, 256)
        live = (j < nodes.counts[2]) & (nodes.begin + j < nodes.live)
        o_ref[32 * j : 32 * j + 32, :] = jnp.where(live, keep * old + right[32 * j : 32 * j + 32], old)


def finish_kernel(me_ref, count_ref, got_ref, base_ref, ghi_ref, glo_ref, o_ref):
    me = me_ref[0] * 2 + me_ref[1]
    total = jnp.int32(0)
    begin = jnp.int32(0)
    for j in range(count_ref.shape[0]):
        c = count_ref[j]
        total = total + c
        begin = begin + jnp.where(j < me, c, 0)
    limit = (total >> 1) << 1
    his, los = [], []
    for z in range(1, 4):
        hi, lo = split(got_ref[:, 8 * z : 8 * z + 8, :].reshape(256, 128))
        his.append(hi)
        los.append(lo)
    hi, lo = jnp.concatenate(his, axis=0), jnp.concatenate(los, axis=0)
    g = ghi_ref[...]
    out = dot(g, hi) + dot(g, lo) + dot(glo_ref[...], hi) + got_ref[:, :8, :].reshape(256, 128)
    out = out.T
    for j in range(4):
        live = (j < count_ref[me]) & (begin + j < limit)
        rows = slice(32 * j, 32 * j + 32)
        o_ref[rows, :] = base_ref[rows, :] + jnp.where(live, out[rows], 0.0)


SMEM = pl.BlockSpec(memory_space=pltpu.SMEM)
VMEM = pl.BlockSpec(memory_space=pltpu.VMEM)


def call(kernel, outs, specs, scratch=(), flops=1_000_000, name=None):
    return pl.pallas_call(
        kernel,
        out_shape=outs,
        in_specs=specs,
        out_specs=jax.tree.map(lambda _: VMEM, outs),
        scratch_shapes=list(scratch),
        compiler_params=pltpu.CompilerParams(vmem_limit_bytes=48 * 1024 * 1024),
        cost_estimate=pl.CostEstimate(flops=flops, bytes_accessed=4_000_000, transcendentals=0),
        name=name,
    )


def struct(shape, dtype=F32):
    return jax.ShapeDtypeStruct(shape, dtype)


weights_call = call(
    weights_kernel,
    (struct((768, 256), BF), struct((768, 256), BF), struct((256, 768), BF), struct((256, 768), BF)),
    [VMEM] * 2,
    name="weights",
)
pack_call = call(pack_kernel, struct((32, 24, 128)), [VMEM] * 3, name="pack")
column_call = call(
    column_kernel,
    struct((32, 32, 128)),
    [SMEM] * 5 + [VMEM] * 3,
    [
        pltpu.VMEM((24, 2, 8, 256), F32),
        pltpu.VMEM((640, 768), BF),
        pltpu.VMEM((640, 768), BF),
        pltpu.VMEM((128, 768), BF),
        pltpu.VMEM((128, 768), BF),
        pltpu.VMEM((4, 8, 2, 8, 256), F32),
    ],
    flops=1_000_000_000,
    name="columns",
)
row_call = call(
    row_kernel,
    struct((128, 256)),
    [SMEM] * 5 + [VMEM] * 7,
    [
        pltpu.VMEM((20, 2, 16, 256), F32),
        pltpu.VMEM((384, 768), BF),
        pltpu.VMEM((384, 768), BF),
        pltpu.VMEM((128, 768), BF),
        pltpu.VMEM((128, 768), BF),
    ],
    flops=1_000_000_000,
    name="rows",
)
finish_call = call(finish_kernel, struct((128, 256)), [SMEM] * 2 + [VMEM] * 4, flops=300_000_000, name="finish")


def swap_routes(shards):
    pairs = [(i, i + 1) for i in range(1, shards - 1, 2)]
    near = pairs + [(b, a) for a, b in pairs]
    far = [(i, i + 2) for i in range(0, shards - 2, 2)] + [(i, i - 2) for i in range(3, shards, 2)]
    pairs = [(i, i + 1) for i in range(0, shards, 2)]
    inner = pairs + [(b, a) for a, b in pairs]
    back = [(i, i - 2) for i in range(2, shards, 2)] + [(i, i + 2) for i in range(1, shards - 2, 2)]
    return near, far, inner, back


def on_device(densities, hamiltonian, couplings, gamma, coeff, node_count):
    hier = ("team", "r")
    group = ("col", "r")
    table = jnp.asarray(np.sqrt(np.arange(72, dtype=np.float32)))
    me = jnp.stack([lax.axis_index("team"), lax.axis_index("r")]).astype(jnp.int32)
    near, far, inner, back = swap_routes(node_count.shape[0])
    flat = densities.reshape(128, 256)
    p1 = lax.ppermute(densities, hier, near)
    p2 = lax.ppermute(densities, hier, far)
    vhi, vlo, hhi, hlo = weights_call(hamiltonian, couplings)
    sent = pack_call(flat, p1.reshape(128, 256), p2.reshape(128, 256))
    got = lax.all_to_all(sent, group, 0, 0, tiled=True)
    back_sent = column_call(me, node_count, table, gamma, coeff, got, vhi, vlo)
    back_sent, again = lax.optimization_barrier((back_sent, densities))
    p3 = lax.ppermute(again, hier, inner)
    p4 = lax.ppermute(again, hier, back)
    back_got = lax.all_to_all(back_sent, group, 0, 0, tiled=True)
    base = row_call(me, node_count, table, gamma, coeff, densities, p1, p2, p3, p4, vhi, vlo)
    out = finish_call(me, node_count, back_got, base, hhi, hlo)
    return out.reshape(4, 2, 16, 256)


def solution(mesh):
    devices = mesh.devices
    inside = Mesh(devices.reshape(devices.shape[0] // 2, 2, devices.shape[1]), ("team", "r", "col"))
    spec = P(("team", "r"), None, "col", None)
    return jax.shard_map(
        on_device,
        mesh=inside,
        in_specs=(spec, P(), P(), P(), P(), P()),
        out_specs=spec,
        check_vma=False,
    )
```

```python
import jax
import jax.numpy as jnp
from jax import lax
from jax.experimental import pallas as pl
from jax.experimental.pallas import tpu as pltpu
from jax.sharding import Mesh, PartitionSpec as P

STEP = 0.2
HALF2 = 0.5 * STEP * STEP
SLOTS = 4
TOTAL, TEAM_BEGIN, HERE_BEGIN, SIDE, COUNTS = 0, 1, 2, 3, 4
ROOTS = 72
BF = jnp.bfloat16
F32 = jnp.float32


def split(v):
    hi = v.astype(BF)
    return hi, (v - hi.astype(F32)).astype(BF)


def dot(a, b):
    return jnp.dot(a, b, preferred_element_type=F32)


def granules(vs):
    lane = lax.broadcasted_iota(jnp.int32, vs[0].shape, 1) // 16
    for bit in (4, 2, 1):
        low = (lane & bit) == 0
        out = list(vs)
        for a in range(8):
            if not a & bit:
                b = a | bit
                out[a] = jnp.where(low, vs[a], pltpu.roll(vs[b], 16 * bit, 1))
                out[b] = jnp.where(low, pltpu.roll(vs[a], 128 - 16 * bit, 1), vs[b])
        vs = out
    return vs


class Nodes:
    def __init__(self, ints_ref, reals_ref, begin):
        self.live = (ints_ref[TOTAL] >> 1) << 1
        self.begin = begin
        self.base = begin - 4
        self.reals = reals_ref
        self.gamma = (reals_ref[0], reals_ref[1])
        self.re = (reals_ref[2], reals_ref[4])
        self.im = (reals_ref[3], reals_ref[5])

    def root(self, n):
        return self.reals[jnp.clip(n, 0, ROOTS - 1) + 6]

    def up(self, p):
        g = self.base + p
        return jnp.where((g >= 0) & (g + 2 < self.live), self.root((g >> 1) + 1), 0.0)

    def down(self, p):
        g = self.base + p
        return jnp.where((g >= 2) & (g < self.live), self.root(g >> 1), 0.0)

    def middle(self, p):
        g = self.base + p
        n = (g >> 1).astype(F32)
        ok = (g >= 0) & (g < self.live)
        upper = jnp.where(ok & (g + 2 < self.live), n + 1.0, 0.0)
        return upper + jnp.where(ok & (g >= 2), n, 0.0)

    def even(self, p):
        g = self.base + p
        return jnp.where((g >= 0) & (g < self.live) & ((g & 1) == 0), 1.0, 0.0).astype(F32)

    def odd(self, p):
        g = self.base + p
        return jnp.where((g >= 0) & (g < self.live) & ((g & 1) == 1), 1.0, 0.0).astype(F32)

    def damp(self, p):
        g = self.base + p
        n0 = (g >> 1).astype(F32)
        n1 = (g & 1).astype(F32)
        return n0 * self.gamma[0] + n1 * self.gamma[1]


def scaled(s, v):
    return (s * v[0], s * v[1])


def plus(a, b):
    return (a[0] + b[0], a[1] + b[1])


def times(re, im, v):
    return (re * v[0] - im * v[1], re * v[1] + im * v[0])


def both(nodes, x, p, re, im):
    r = plus(scaled(nodes.up(p), x[p + 2]), scaled(re * nodes.down(p), x[p - 2]))
    t = scaled(im * nodes.down(p), x[p - 2])
    return (r[0] - t[1], r[1] + t[0]), (r[0] + t[1], r[1] - t[0])


def both1(nodes, x, p, re, im):
    r = plus(scaled(nodes.even(p), x[p + 1]), scaled(re * nodes.odd(p), x[p - 1]))
    t = scaled(im * nodes.odd(p), x[p - 1])
    return (r[0] - t[1], r[1] + t[0]), (r[0] + t[1], r[1] - t[0])


def first_order(nodes, x, p, re, im):
    here = nodes.damp(p)

    def w(q):
        return STEP - HALF2 * (here + nodes.damp(q))

    zero = scaled(w(p), x[p])
    up, down = scaled(w(p + 2) * nodes.up(p), x[p + 2]), scaled(w(p - 2) * nodes.down(p), x[p - 2])
    one = plus(up, times(re[0], im[0], down))
    up, down = scaled(w(p + 1) * nodes.even(p), x[p + 1]), scaled(w(p - 1) * nodes.odd(p), x[p - 1])
    two = plus(up, times(re[1], im[1], down))
    return zero, one, two


def put(hi_ref, lo_ref, block, col, j, rows, v):
    hi, lo = split(jnp.concatenate([v[0], v[1]], axis=0))
    at = pl.ds(block * 128 + j * rows, rows)
    hi_ref[at, 256 * col : 256 * col + 256] = hi
    lo_ref[at, 256 * col : 256 * col + 256] = lo


def times_weights(hi_ref, lo_ref, ghi_ref, glo_ref):
    hi, g = hi_ref[...], ghi_ref[...]
    return dot(hi, g) + dot(lo_ref[...], g) + dot(hi, glo_ref[...])


def weights_kernel(h_ref, q_ref, vhi, vlo, hhi, hlo):
    for b in range(3):
        hi, lo = split(h_ref[...] if b == 0 else q_ref[b - 1])
        vhi[256 * b : 256 * b + 256, :] = hi
        vlo[256 * b : 256 * b + 256, :] = lo
        hhi[:, 256 * b : 256 * b + 256] = hi
        hlo[:, 256 * b : 256 * b + 256] = lo


def own_kernel(x_ref, o_ref, t_ref, sem):
    t_ref[...] = x_ref[...].T.reshape(32, 8, 128)
    copy = pltpu.make_async_copy(t_ref, o_ref.at[:, 0:8], sem)
    copy.start()
    copy.wait()


def halo_kernel(ints_ref, near_ref, far_ref, _, o_ref, s_ref, t_ref, sem):
    side = ints_ref[SIDE]
    count = jnp.where(side == 0, ints_ref[COUNTS + 1], ints_ref[COUNTS + 3])
    for i in range(4):
        at = i + jnp.where(side == 0, count - 4, 0)
        inside = jnp.where(side == 0, at >= 0, i < count)
        other = jnp.where(side == 0, at + 2, i - count)
        near = near_ref[jnp.clip(at, 0, 3)]
        far = far_ref[jnp.clip(other, 0, 1)]
        s_ref[32 * i : 32 * i + 32, :] = jnp.where(inside, near, far).reshape(32, 256)
    t_ref[...] = s_ref[...].T.reshape(32, 8, 128)
    copy = pltpu.make_async_copy(t_ref, o_ref.at[:, 8:16], sem)
    copy.start()
    copy.wait()


def column_kernel(ints_ref, reals_ref, got_ref, ghi_ref, glo_ref, o_ref, y_ref, hi_ref, lo_ref, hi2_ref, lo2_ref, z_ref):
    nodes = Nodes(ints_ref, reals_ref, ints_ref[TEAM_BEGIN])
    own, other = ints_ref[COUNTS + 2 - ints_ref[SIDE]], ints_ref[COUNTS + 3 - ints_ref[SIDE]]
    re, im = nodes.re, nodes.im
    places = ((1, 0), (0, 0), (0, 1), (1, 1))
    for i, (g, r) in enumerate(places):
        vs = []
        for low in range(8):
            vs.append(jnp.concatenate([got_ref[(8 * high + low) * 2 + r, 8 * g : 8 * g + 8, :] for high in range(2)], axis=0))
        for m, v in enumerate(granules(vs)):
            y_ref[SLOTS * i + m // 2, m % 2] = jnp.concatenate([v[:8], v[8:]], axis=1)

    def slot(p):
        j = p - 4
        if j < 0:
            return p
        return jnp.where(j < own, 4 + j, jnp.where(j < own + other, 8 + j - own, jnp.minimum(12 + j - own - other, 15)))

    x = []
    for p in range(16):
        v = y_ref[slot(p)]
        x.append((v[0], v[1]))
    a2, b2 = {}, {}
    for p in range(2, 14):
        a2[p], b2[p] = both1(nodes, x, p, re[1], im[1])
    for j in range(8):
        p = j + 4
        a1, b1 = both(nodes, x, p, re[0], im[0])
        a12, b1a2 = both(nodes, a2, p, re[0], im[0])
        a1b2, _ = both(nodes, b2, p, re[0], im[0])
        far = scaled(nodes.up(p) * nodes.up(p + 2), x[p + 4])
        low = scaled(nodes.down(p) * nodes.down(p - 2), x[p - 4])
        mid = nodes.middle(p)
        here = scaled(mid, x[p])
        a11 = plus(plus(far, times(re[0], im[0], here)), times(re[0] * re[0] - im[0] * im[0], 2.0 * re[0] * im[0], low))
        s11 = plus(plus(scaled(2.0, far), scaled(2.0 * re[0], here)), scaled(2.0 * (re[0] * re[0] + im[0] * im[0]), low))
        rows = (
            (x[p], a1, a2[p]),
            (a1, a11, a12),
            (a2[p], a12, times(re[1], im[1], x[p])),
            (scaled(2.0, b1), s11, scaled(2.0, b1a2)),
            (scaled(2.0, b2[p]), scaled(2.0, a1b2), scaled(2.0 * re[1], x[p])),
        )
        for block, row in enumerate(rows):
            for col, v in enumerate(row):
                put(hi_ref, lo_ref, block, col, j, 16, v)
    sums = times_weights(hi_ref, lo_ref, ghi_ref, glo_ref)
    for j in range(8):
        p = j + 4
        for block, v in enumerate(first_order(nodes, x, p, re, im)):
            s = sums[block * 128 + 16 * j : block * 128 + 16 * j + 16]
            put(hi2_ref, lo2_ref, 0, block, j, 16, (v[1] - HALF2 * s[:8], -v[0] - HALF2 * s[8:]))
        z_ref[1, j] = (2.0 * HALF2) * sums[16 * j : 16 * j + 16].reshape(2, 8, 256)
        z_ref[2, j] = HALF2 * sums[384 + 16 * j : 400 + 16 * j].reshape(2, 8, 256)
        z_ref[3, j] = HALF2 * sums[512 + 16 * j : 528 + 16 * j].reshape(2, 8, 256)
    z_ref[0] = times_weights(hi2_ref, lo2_ref, ghi_ref, glo_ref).reshape(8, 2, 8, 256)
    for z in range(4):
        for r in range(2):
            vs = []
            for m in range(8):
                v = z_ref[z, m // 2 if r == 0 else own + m // 2, m % 2]
                vs.append(jnp.concatenate([v[:, :128], v[:, 128:]], axis=0))
            for low, v in enumerate(granules(vs)):
                for high in range(2):
                    o_ref[(8 * high + low) * 2 + r, 8 * z : 8 * z + 8, :] = v[8 * high : 8 * high + 8]


def row_kernel(
    ints_ref, reals_ref, x_ref, p1_ref, p2_ref, p3_ref, p4_ref, ghi_ref, glo_ref, o_ref, w_ref, hi_ref, lo_ref, hi2_ref, lo2_ref
):
    nodes = Nodes(ints_ref, reals_ref, ints_ref[HERE_BEGIN])
    re, im = nodes.re, (-nodes.im[0], -nodes.im[1])
    up = ints_ref[SIDE]
    below, own, above = ints_ref[COUNTS + 1], ints_ref[COUNTS + 2], ints_ref[COUNTS + 3]
    w_ref[8:12] = x_ref[...]
    w_ref[pl.ds(4 + 8 * up, 4)] = p1_ref[...]
    w_ref[pl.ds(2 + 14 * up, 2)] = p2_ref[...]
    w_ref[pl.ds(12 - 8 * up, 4)] = p3_ref[...]
    w_ref[pl.ds(16 - 14 * up, 2)] = p4_ref[...]

    def slot(p):
        j = p - 4
        if j < 0:
            return 4 + j + below
        return jnp.where(j < own, 8 + j, jnp.where(j < own + above, 12 + j - own, jnp.minimum(16 + j - own - above, 17)))

    x = []
    for p in range(12):
        v = w_ref[slot(p)]
        x.append((v[0], v[1]))
    b2 = {}
    for p in range(2, 10):
        b2[p], _ = both1(nodes, x, p, re[1], im[1])
    for j in range(4):
        p = j + 4
        b1, _ = both(nodes, x, p, re[0], im[0])
        b12, _ = both(nodes, b2, p, re[0], im[0])
        far = scaled(nodes.up(p) * nodes.up(p + 2), x[p + 4])
        low = scaled(nodes.down(p) * nodes.down(p - 2), x[p - 4])
        here = scaled(nodes.middle(p), x[p])
        b11 = plus(plus(far, times(re[0], im[0], here)), times(re[0] * re[0] - im[0] * im[0], 2.0 * re[0] * im[0], low))
        rows = ((x[p], b1, b2[p]), (b1, b11, b12), (b2[p], b12, times(re[1], im[1], x[p])))
        for block, row in enumerate(rows):
            for col, v in enumerate(row):
                put(hi_ref, lo_ref, block, col, j, 32, v)
    sums = times_weights(hi_ref, lo_ref, ghi_ref, glo_ref)
    for j in range(4):
        p = j + 4
        for block, v in enumerate(first_order(nodes, x, p, re, im)):
            s = sums[block * 128 + 32 * j : block * 128 + 32 * j + 32]
            put(hi2_ref, lo2_ref, 0, block, j, 32, (-v[1] - HALF2 * s[:16], v[0] - HALF2 * s[16:]))
    right = times_weights(hi2_ref, lo2_ref, ghi_ref, glo_ref)
    for j in range(4):
        d = nodes.damp(j + 4)
        keep = 1.0 - STEP * d + HALF2 * d * d
        old = x_ref[j].reshape(32, 256)
        live = (j < own) & (nodes.begin + j < nodes.live)
        o_ref[32 * j : 32 * j + 32, :] = jnp.where(live, keep * old + right[32 * j : 32 * j + 32], old)


def finish_kernel(ints_ref, got_ref, base_ref, ghi_ref, glo_ref, o_ref):
    own, begin, limit = ints_ref[COUNTS + 2], ints_ref[HERE_BEGIN], (ints_ref[TOTAL] >> 1) << 1
    his, los = [], []
    for z in range(1, 4):
        hi, lo = split(got_ref[:, 8 * z : 8 * z + 8, :].reshape(256, 128))
        his.append(hi)
        los.append(lo)
    hi, lo = jnp.concatenate(his, axis=0), jnp.concatenate(los, axis=0)
    g = ghi_ref[...]
    out = dot(g, hi) + dot(g, lo) + dot(glo_ref[...], hi) + got_ref[:, :8, :].reshape(256, 128)
    out = out.T
    for j in range(4):
        live = (j < own) & (begin + j < limit)
        rows = slice(32 * j, 32 * j + 32)
        o_ref[rows, :] = base_ref[rows, :] + jnp.where(live, out[rows], 0.0)


SMEM = pl.BlockSpec(memory_space=pltpu.SMEM)
VMEM = pl.BlockSpec(memory_space=pltpu.VMEM)
ANY = pl.BlockSpec(memory_space=pl.ANY)


def call(kernel, outs, specs, scratch=(), flops=1_000_000, name=None, out_specs=None, aliases=None):
    return pl.pallas_call(
        kernel,
        out_shape=outs,
        in_specs=specs,
        out_specs=out_specs or jax.tree.map(lambda _: VMEM, outs),
        input_output_aliases=aliases or {},
        scratch_shapes=list(scratch),
        compiler_params=pltpu.CompilerParams(vmem_limit_bytes=48 * 1024 * 1024),
        cost_estimate=pl.CostEstimate(flops=flops, bytes_accessed=4_000_000, transcendentals=0),
        name=name,
    )


def struct(shape, dtype=F32):
    return jax.ShapeDtypeStruct(shape, dtype)


weights_call = call(
    weights_kernel,
    (struct((768, 256), BF), struct((768, 256), BF), struct((256, 768), BF), struct((256, 768), BF)),
    [VMEM] * 2,
    name="weights",
)
own_call = call(
    own_kernel, struct((32, 16, 128)), [VMEM], [pltpu.VMEM((32, 8, 128), F32), pltpu.SemaphoreType.DMA], out_specs=ANY, name="own"
)
halo_call = call(
    halo_kernel,
    struct((32, 16, 128)),
    [SMEM] + [VMEM] * 2 + [ANY],
    [pltpu.VMEM((128, 256), F32), pltpu.VMEM((32, 8, 128), F32), pltpu.SemaphoreType.DMA],
    out_specs=ANY,
    aliases={3: 0},
    name="halo",
)
column_call = call(
    column_kernel,
    struct((32, 32, 128)),
    [SMEM] * 2 + [VMEM] * 3,
    [
        pltpu.VMEM((16, 2, 8, 256), F32),
        pltpu.VMEM((640, 768), BF),
        pltpu.VMEM((640, 768), BF),
        pltpu.VMEM((128, 768), BF),
        pltpu.VMEM((128, 768), BF),
        pltpu.VMEM((4, 8, 2, 8, 256), F32),
    ],
    flops=1_000_000_000,
    name="columns",
)
row_call = call(
    row_kernel,
    struct((128, 256)),
    [SMEM] * 2 + [VMEM] * 7,
    [
        pltpu.VMEM((18, 2, 16, 256), F32),
        pltpu.VMEM((384, 768), BF),
        pltpu.VMEM((384, 768), BF),
        pltpu.VMEM((128, 768), BF),
        pltpu.VMEM((128, 768), BF),
    ],
    flops=1_000_000_000,
    name="rows",
)
finish_call = call(finish_kernel, struct((128, 256)), [SMEM] + [VMEM] * 4, flops=300_000_000, name="finish")


def swap_routes(shards):
    pairs = [(i, i + 1) for i in range(1, shards - 1, 2)]
    near = pairs + [(b, a) for a, b in pairs]
    far = [(i, i + 2) for i in range(0, shards - 2, 2)] + [(i, i - 2) for i in range(3, shards, 2)]
    pairs = [(i, i + 1) for i in range(0, shards, 2)]
    inner = pairs + [(b, a) for a, b in pairs]
    back = [(i, i - 2) for i in range(2, shards, 2)] + [(i, i + 2) for i in range(1, shards - 2, 2)]
    return near, far, inner, back


def integers(node_count):
    shards = node_count.shape[0]
    team, side = lax.axis_index("team"), lax.axis_index("r")
    here = 2 * team + side
    row = jnp.arange(16, dtype=jnp.int32)[:, None]
    column = jnp.arange(shards, dtype=jnp.int32)[None, :]
    near = jnp.clip(here + row - (COUNTS + 2), 0, shards - 1)
    wanted = (
        (row == TOTAL)
        | ((row == TEAM_BEGIN) & (column < 2 * team))
        | ((row == HERE_BEGIN) & (column < here))
        | ((row >= COUNTS) & (column == near))
    )
    sums = jnp.sum(jnp.where(wanted, node_count[None, :], 0), axis=1)
    return sums + jnp.where(row[:, 0] == SIDE, side, 0)


def on_device(densities, hamiltonian, couplings, gamma, coeff, node_count):
    hier = ("team", "r")
    group = ("col", "r")
    ints = integers(node_count)
    reals = jnp.concatenate([gamma, coeff.reshape(4), jnp.sqrt(jnp.arange(ROOTS, dtype=F32))])
    near, far, inner, back = swap_routes(node_count.shape[0])
    p1 = lax.ppermute(densities, hier, near)
    tail = ints[COUNTS + 2] - 2
    side = lax.axis_index("r")
    p2 = lax.ppermute(lax.dynamic_slice_in_dim(densities, jnp.where(side == 0, tail, 0), 2, 0), hier, far)
    part = own_call(densities.reshape(128, 256))
    vhi, vlo, hhi, hlo = weights_call(hamiltonian, couplings)
    sent = halo_call(ints, p1, p2, part)
    sent, again = lax.optimization_barrier((sent, densities))
    got = lax.all_to_all(sent, group, 0, 0, tiled=True)
    p3 = lax.ppermute(again, hier, inner)
    p4 = lax.ppermute(lax.dynamic_slice_in_dim(again, jnp.where(side == 0, 0, tail), 2, 0), hier, back)
    back_sent = column_call(ints, reals, got, vhi, vlo)
    back_sent, p3, p4 = lax.optimization_barrier((back_sent, p3, p4))
    back_got = lax.all_to_all(back_sent, group, 0, 0, tiled=True)
    base = row_call(ints, reals, densities, p1, p2, p3, p4, vhi, vlo)
    out = finish_call(ints, back_got, base, hhi, hlo)
    return out.reshape(4, 2, 16, 256)


def solution(mesh):
    devices = mesh.devices
    inside = Mesh(devices.reshape(devices.shape[0] // 2, 2, devices.shape[1]), ("team", "r", "col"))
    spec = P(("team", "r"), None, "col", None)
    return jax.shard_map(
        on_device,
        mesh=inside,
        in_specs=(spec, P(), P(), P(), P(), P()),
        out_specs=spec,
        check_vma=False,
    )
```

```python
import jax
import jax.numpy as jnp
from jax import lax
from jax.experimental import pallas as pl
from jax.experimental.pallas import tpu as pltpu
from jax.sharding import Mesh, PartitionSpec as P

STEP = 0.2
HALF2 = 0.5 * STEP * STEP
SLOTS = 4
TOTAL, TEAM_BEGIN, HERE_BEGIN, SIDE, COUNTS = 0, 1, 2, 3, 4
ROOTS = 72
BF = jnp.bfloat16
F32 = jnp.float32


def split(v):
    hi = v.astype(BF)
    return hi, (v - hi.astype(F32)).astype(BF)


def dot(a, b):
    return jnp.dot(a, b, preferred_element_type=F32)


def granules(vs):
    lane = lax.broadcasted_iota(jnp.int32, vs[0].shape, 1) // 16
    for bit in (4, 2, 1):
        low = (lane & bit) == 0
        out = list(vs)
        for a in range(8):
            if not a & bit:
                b = a | bit
                out[a] = jnp.where(low, vs[a], pltpu.roll(vs[b], 16 * bit, 1))
                out[b] = jnp.where(low, pltpu.roll(vs[a], 128 - 16 * bit, 1), vs[b])
        vs = out
    return vs


class Nodes:
    def __init__(self, ints_ref, reals_ref, begin):
        self.live = (ints_ref[TOTAL] >> 1) << 1
        self.begin = begin
        self.base = begin - 4
        self.reals = reals_ref
        self.gamma = (reals_ref[0], reals_ref[1])
        self.re = (reals_ref[2], reals_ref[4])
        self.im = (reals_ref[3], reals_ref[5])

    def root(self, n):
        return self.reals[jnp.clip(n, 0, ROOTS - 1) + 6]

    def up(self, p):
        g = self.base + p
        return jnp.where((g >= 0) & (g + 2 < self.live), self.root((g >> 1) + 1), 0.0)

    def down(self, p):
        g = self.base + p
        return jnp.where((g >= 2) & (g < self.live), self.root(g >> 1), 0.0)

    def middle(self, p):
        g = self.base + p
        n = (g >> 1).astype(F32)
        ok = (g >= 0) & (g < self.live)
        upper = jnp.where(ok & (g + 2 < self.live), n + 1.0, 0.0)
        return upper + jnp.where(ok & (g >= 2), n, 0.0)

    def even(self, p):
        g = self.base + p
        return jnp.where((g >= 0) & (g < self.live) & ((g & 1) == 0), 1.0, 0.0).astype(F32)

    def odd(self, p):
        g = self.base + p
        return jnp.where((g >= 0) & (g < self.live) & ((g & 1) == 1), 1.0, 0.0).astype(F32)

    def damp(self, p):
        g = self.base + p
        n0 = (g >> 1).astype(F32)
        n1 = (g & 1).astype(F32)
        return n0 * self.gamma[0] + n1 * self.gamma[1]


def scaled(s, v):
    return (s * v[0], s * v[1])


def plus(a, b):
    return (a[0] + b[0], a[1] + b[1])


def times(re, im, v):
    return (re * v[0] - im * v[1], re * v[1] + im * v[0])


def both(nodes, x, p, re, im):
    r = plus(scaled(nodes.up(p), x[p + 2]), scaled(re * nodes.down(p), x[p - 2]))
    t = scaled(im * nodes.down(p), x[p - 2])
    return (r[0] - t[1], r[1] + t[0]), (r[0] + t[1], r[1] - t[0])


def both1(nodes, x, p, re, im):
    r = plus(scaled(nodes.even(p), x[p + 1]), scaled(re * nodes.odd(p), x[p - 1]))
    t = scaled(im * nodes.odd(p), x[p - 1])
    return (r[0] - t[1], r[1] + t[0]), (r[0] + t[1], r[1] - t[0])


def first_order(nodes, x, p, re, im):
    here = nodes.damp(p)

    def w(q):
        return STEP - HALF2 * (here + nodes.damp(q))

    zero = scaled(w(p), x[p])
    up, down = scaled(w(p + 2) * nodes.up(p), x[p + 2]), scaled(w(p - 2) * nodes.down(p), x[p - 2])
    one = plus(up, times(re[0], im[0], down))
    up, down = scaled(w(p + 1) * nodes.even(p), x[p + 1]), scaled(w(p - 1) * nodes.odd(p), x[p - 1])
    two = plus(up, times(re[1], im[1], down))
    return zero, one, two


def put(hi_ref, lo_ref, block, col, j, rows, v):
    hi, lo = split(jnp.concatenate([v[0], v[1]], axis=0))
    at = pl.ds(block * 128 + j * rows, rows)
    hi_ref[at, 256 * col : 256 * col + 256] = hi
    lo_ref[at, 256 * col : 256 * col + 256] = lo


def times_weights(hi_ref, lo_ref, ghi_ref, glo_ref):
    hi, g = hi_ref[...], ghi_ref[...]
    return dot(hi, g) + dot(lo_ref[...], g) + dot(hi, glo_ref[...])


def weights_kernel(h_ref, q_ref, vhi, vlo, hhi, hlo):
    for b in range(3):
        hi, lo = split(h_ref[...] if b == 0 else q_ref[b - 1])
        vhi[256 * b : 256 * b + 256, :] = hi
        vlo[256 * b : 256 * b + 256, :] = lo
        hhi[:, 256 * b : 256 * b + 256] = hi
        hlo[:, 256 * b : 256 * b + 256] = lo


def own_kernel(x_ref, o_ref, t_ref, sem):
    t_ref[...] = x_ref[...].T.reshape(32, 8, 128)
    copy = pltpu.make_async_copy(t_ref, o_ref.at[:, 0:8], sem)
    copy.start()
    copy.wait()


def halo_kernel(ints_ref, near_ref, far_ref, _, o_ref, s_ref, t_ref, sem):
    side = ints_ref[SIDE]
    count = jnp.where(side == 0, ints_ref[COUNTS + 1], ints_ref[COUNTS + 3])
    farther = ints_ref[COUNTS]
    for i in range(4):
        at = i + jnp.where(side == 0, count - 4, 0)
        inside = jnp.where(side == 0, at >= 0, i < count)
        other = jnp.where(side == 0, at + farther, i - count)
        near = near_ref[jnp.clip(at, 0, 3)]
        far = far_ref[jnp.clip(other, 0, 3)]
        s_ref[32 * i : 32 * i + 32, :] = jnp.where(inside, near, far).reshape(32, 256)
    t_ref[...] = s_ref[...].T.reshape(32, 8, 128)
    copy = pltpu.make_async_copy(t_ref, o_ref.at[:, 8:16], sem)
    copy.start()
    copy.wait()


def column_kernel(ints_ref, reals_ref, got_ref, ghi_ref, glo_ref, o_ref, y_ref, hi_ref, lo_ref, hi2_ref, lo2_ref, z_ref):
    nodes = Nodes(ints_ref, reals_ref, ints_ref[TEAM_BEGIN])
    own, other = ints_ref[COUNTS + 2 - ints_ref[SIDE]], ints_ref[COUNTS + 3 - ints_ref[SIDE]]
    re, im = nodes.re, nodes.im
    places = ((1, 0), (0, 0), (0, 1), (1, 1))
    for i, (g, r) in enumerate(places):
        vs = []
        for low in range(8):
            vs.append(jnp.concatenate([got_ref[(8 * high + low) * 2 + r, 8 * g : 8 * g + 8, :] for high in range(2)], axis=0))
        for m, v in enumerate(granules(vs)):
            y_ref[SLOTS * i + m // 2, m % 2] = jnp.concatenate([v[:8], v[8:]], axis=1)

    def slot(p):
        j = p - 4
        if j < 0:
            return p
        return jnp.where(j < own, 4 + j, jnp.where(j < own + other, 8 + j - own, jnp.minimum(12 + j - own - other, 15)))

    x = []
    for p in range(16):
        v = y_ref[slot(p)]
        x.append((v[0], v[1]))
    a2, b2 = {}, {}
    for p in range(2, 14):
        a2[p], b2[p] = both1(nodes, x, p, re[1], im[1])
    for j in range(8):
        p = j + 4
        a1, b1 = both(nodes, x, p, re[0], im[0])
        a12, b1a2 = both(nodes, a2, p, re[0], im[0])
        a1b2, _ = both(nodes, b2, p, re[0], im[0])
        far = scaled(nodes.up(p) * nodes.up(p + 2), x[p + 4])
        low = scaled(nodes.down(p) * nodes.down(p - 2), x[p - 4])
        mid = nodes.middle(p)
        here = scaled(mid, x[p])
        a11 = plus(plus(far, times(re[0], im[0], here)), times(re[0] * re[0] - im[0] * im[0], 2.0 * re[0] * im[0], low))
        s11 = plus(plus(scaled(2.0, far), scaled(2.0 * re[0], here)), scaled(2.0 * (re[0] * re[0] + im[0] * im[0]), low))
        rows = (
            (x[p], a1, a2[p]),
            (a1, a11, a12),
            (a2[p], a12, times(re[1], im[1], x[p])),
            (scaled(2.0, b1), s11, scaled(2.0, b1a2)),
            (scaled(2.0, b2[p]), scaled(2.0, a1b2), scaled(2.0 * re[1], x[p])),
        )
        for block, row in enumerate(rows):
            for col, v in enumerate(row):
                put(hi_ref, lo_ref, block, col, j, 16, v)
    sums = times_weights(hi_ref, lo_ref, ghi_ref, glo_ref)
    for j in range(8):
        p = j + 4
        for block, v in enumerate(first_order(nodes, x, p, re, im)):
            s = sums[block * 128 + 16 * j : block * 128 + 16 * j + 16]
            put(hi2_ref, lo2_ref, 0, block, j, 16, (v[1] - HALF2 * s[:8], -v[0] - HALF2 * s[8:]))
        z_ref[1, j] = (2.0 * HALF2) * sums[16 * j : 16 * j + 16].reshape(2, 8, 256)
        z_ref[2, j] = HALF2 * sums[384 + 16 * j : 400 + 16 * j].reshape(2, 8, 256)
        z_ref[3, j] = HALF2 * sums[512 + 16 * j : 528 + 16 * j].reshape(2, 8, 256)
    z_ref[0] = times_weights(hi2_ref, lo2_ref, ghi_ref, glo_ref).reshape(8, 2, 8, 256)
    for z in range(4):
        for r in range(2):
            vs = []
            for m in range(8):
                v = z_ref[z, m // 2 if r == 0 else own + m // 2, m % 2]
                vs.append(jnp.concatenate([v[:, :128], v[:, 128:]], axis=0))
            for low, v in enumerate(granules(vs)):
                for high in range(2):
                    o_ref[(8 * high + low) * 2 + r, 8 * z : 8 * z + 8, :] = v[8 * high : 8 * high + 8]


def row_kernel(
    ints_ref, reals_ref, x_ref, p1_ref, p2_ref, p3_ref, p4_ref, ghi_ref, glo_ref, o_ref, w_ref, hi_ref, lo_ref, hi2_ref, lo2_ref
):
    nodes = Nodes(ints_ref, reals_ref, ints_ref[HERE_BEGIN])
    re, im = nodes.re, (-nodes.im[0], -nodes.im[1])
    up = ints_ref[SIDE]
    farther, below, own, above = (ints_ref[COUNTS + i] for i in range(4))
    w_ref[8:12] = x_ref[...]
    w_ref[pl.ds(4 + 8 * up, 4)] = p1_ref[...]
    w_ref[pl.ds(16 * up, 4)] = p2_ref[...]
    w_ref[pl.ds(12 - 8 * up, 4)] = p3_ref[...]
    w_ref[pl.ds(16 - 16 * up, 4)] = p4_ref[...]

    def slot(p):
        j = p - 4
        if j < 0:
            return jnp.where(j + below >= 0, 4 + j + below, farther + j + below)
        return jnp.where(j < own, 8 + j, jnp.where(j < own + above, 12 + j - own, jnp.minimum(16 + j - own - above, 19)))

    x = []
    for p in range(12):
        v = w_ref[slot(p)]
        x.append((v[0], v[1]))
    b2 = {}
    for p in range(2, 10):
        b2[p], _ = both1(nodes, x, p, re[1], im[1])
    for j in range(4):
        p = j + 4
        b1, _ = both(nodes, x, p, re[0], im[0])
        b12, _ = both(nodes, b2, p, re[0], im[0])
        far = scaled(nodes.up(p) * nodes.up(p + 2), x[p + 4])
        low = scaled(nodes.down(p) * nodes.down(p - 2), x[p - 4])
        here = scaled(nodes.middle(p), x[p])
        b11 = plus(plus(far, times(re[0], im[0], here)), times(re[0] * re[0] - im[0] * im[0], 2.0 * re[0] * im[0], low))
        rows = ((x[p], b1, b2[p]), (b1, b11, b12), (b2[p], b12, times(re[1], im[1], x[p])))
        for block, row in enumerate(rows):
            for col, v in enumerate(row):
                put(hi_ref, lo_ref, block, col, j, 32, v)
    sums = times_weights(hi_ref, lo_ref, ghi_ref, glo_ref)
    for j in range(4):
        p = j + 4
        for block, v in enumerate(first_order(nodes, x, p, re, im)):
            s = sums[block * 128 + 32 * j : block * 128 + 32 * j + 32]
            put(hi2_ref, lo2_ref, 0, block, j, 32, (-v[1] - HALF2 * s[:16], v[0] - HALF2 * s[16:]))
    right = times_weights(hi2_ref, lo2_ref, ghi_ref, glo_ref)
    for j in range(4):
        d = nodes.damp(j + 4)
        keep = 1.0 - STEP * d + HALF2 * d * d
        old = x_ref[j].reshape(32, 256)
        live = (j < own) & (nodes.begin + j < nodes.live)
        o_ref[32 * j : 32 * j + 32, :] = jnp.where(live, keep * old + right[32 * j : 32 * j + 32], old)


def finish_kernel(ints_ref, got_ref, base_ref, ghi_ref, glo_ref, o_ref):
    own, begin, limit = ints_ref[COUNTS + 2], ints_ref[HERE_BEGIN], (ints_ref[TOTAL] >> 1) << 1
    his, los = [], []
    for z in range(1, 4):
        hi, lo = split(got_ref[:, 8 * z : 8 * z + 8, :].reshape(256, 128))
        his.append(hi)
        los.append(lo)
    hi, lo = jnp.concatenate(his, axis=0), jnp.concatenate(los, axis=0)
    g = ghi_ref[...]
    out = dot(g, hi) + dot(g, lo) + dot(glo_ref[...], hi) + got_ref[:, :8, :].reshape(256, 128)
    out = out.T
    for j in range(4):
        live = (j < own) & (begin + j < limit)
        rows = slice(32 * j, 32 * j + 32)
        o_ref[rows, :] = base_ref[rows, :] + jnp.where(live, out[rows], 0.0)


SMEM = pl.BlockSpec(memory_space=pltpu.SMEM)
VMEM = pl.BlockSpec(memory_space=pltpu.VMEM)
ANY = pl.BlockSpec(memory_space=pl.ANY)


def call(kernel, outs, specs, scratch=(), flops=1_000_000, name=None, out_specs=None, aliases=None):
    return pl.pallas_call(
        kernel,
        out_shape=outs,
        in_specs=specs,
        out_specs=out_specs or jax.tree.map(lambda _: VMEM, outs),
        input_output_aliases=aliases or {},
        scratch_shapes=list(scratch),
        compiler_params=pltpu.CompilerParams(vmem_limit_bytes=48 * 1024 * 1024),
        cost_estimate=pl.CostEstimate(flops=flops, bytes_accessed=4_000_000, transcendentals=0),
        name=name,
    )


def struct(shape, dtype=F32):
    return jax.ShapeDtypeStruct(shape, dtype)


weights_call = call(
    weights_kernel,
    (struct((768, 256), BF), struct((768, 256), BF), struct((256, 768), BF), struct((256, 768), BF)),
    [VMEM] * 2,
    name="weights",
)
own_call = call(
    own_kernel, struct((32, 16, 128)), [VMEM], [pltpu.VMEM((32, 8, 128), F32), pltpu.SemaphoreType.DMA], out_specs=ANY, name="own"
)
halo_call = call(
    halo_kernel,
    struct((32, 16, 128)),
    [SMEM] + [VMEM] * 2 + [ANY],
    [pltpu.VMEM((128, 256), F32), pltpu.VMEM((32, 8, 128), F32), pltpu.SemaphoreType.DMA],
    out_specs=ANY,
    aliases={3: 0},
    name="halo",
)
column_call = call(
    column_kernel,
    struct((32, 32, 128)),
    [SMEM] * 2 + [VMEM] * 3,
    [
        pltpu.VMEM((16, 2, 8, 256), F32),
        pltpu.VMEM((640, 768), BF),
        pltpu.VMEM((640, 768), BF),
        pltpu.VMEM((128, 768), BF),
        pltpu.VMEM((128, 768), BF),
        pltpu.VMEM((4, 8, 2, 8, 256), F32),
    ],
    flops=1_000_000_000,
    name="columns",
)
row_call = call(
    row_kernel,
    struct((128, 256)),
    [SMEM] * 2 + [VMEM] * 7,
    [
        pltpu.VMEM((20, 2, 16, 256), F32),
        pltpu.VMEM((384, 768), BF),
        pltpu.VMEM((384, 768), BF),
        pltpu.VMEM((128, 768), BF),
        pltpu.VMEM((128, 768), BF),
    ],
    flops=1_000_000_000,
    name="rows",
)
finish_call = call(finish_kernel, struct((128, 256)), [SMEM] + [VMEM] * 4, flops=300_000_000, name="finish")


def swap_routes(shards):
    pairs = [(i, i + 1) for i in range(1, shards - 1, 2)]
    near = pairs + [(b, a) for a, b in pairs]
    far = [(i, i + 2) for i in range(0, shards - 2, 2)] + [(i, i - 2) for i in range(3, shards, 2)]
    pairs = [(i, i + 1) for i in range(0, shards, 2)]
    inner = pairs + [(b, a) for a, b in pairs]
    back = [(i, i - 2) for i in range(2, shards, 2)] + [(i, i + 2) for i in range(1, shards - 2, 2)]
    return near, far, inner, back


def integers(node_count):
    shards = node_count.shape[0]
    team, side = lax.axis_index("team"), lax.axis_index("r")
    here = 2 * team + side
    row = jnp.arange(16, dtype=jnp.int32)[:, None]
    column = jnp.arange(shards, dtype=jnp.int32)[None, :]
    near = jnp.clip(here + row - (COUNTS + 2), 0, shards - 1)
    wanted = (
        (row == TOTAL)
        | ((row == TEAM_BEGIN) & (column < 2 * team))
        | ((row == HERE_BEGIN) & (column < here))
        | ((row >= COUNTS) & (column == near))
    )
    sums = jnp.sum(jnp.where(wanted, node_count[None, :], 0), axis=1)
    return sums + jnp.where(row[:, 0] == SIDE, side, 0)


def on_device(densities, hamiltonian, couplings, gamma, coeff, node_count):
    hier = ("team", "r")
    group = ("col", "r")
    ints = integers(node_count)
    reals = jnp.concatenate([gamma, coeff.reshape(4), jnp.sqrt(jnp.arange(ROOTS, dtype=F32))])
    near, far, inner, back = swap_routes(node_count.shape[0])
    p1 = lax.ppermute(densities, hier, near)
    p2 = lax.ppermute(densities, hier, far)
    part = own_call(densities.reshape(128, 256))
    vhi, vlo, hhi, hlo = weights_call(hamiltonian, couplings)
    sent = halo_call(ints, p1, p2, part)
    sent, again = lax.optimization_barrier((sent, densities))
    got = lax.all_to_all(sent, group, 0, 0, tiled=True)
    p3 = lax.ppermute(again, hier, inner)
    back_sent = column_call(ints, reals, got, vhi, vlo)
    back_sent, p3, again = lax.optimization_barrier((back_sent, p3, densities))
    back_got = lax.all_to_all(back_sent, group, 0, 0, tiled=True)
    p4 = lax.ppermute(again, hier, back)
    base = row_call(ints, reals, densities, p1, p2, p3, p4, vhi, vlo)
    out = finish_call(ints, back_got, base, hhi, hlo)
    return out.reshape(4, 2, 16, 256)


def solution(mesh):
    devices = mesh.devices
    inside = Mesh(devices.reshape(devices.shape[0] // 2, 2, devices.shape[1]), ("team", "r", "col"))
    spec = P(("team", "r"), None, "col", None)
    return jax.shard_map(
        on_device,
        mesh=inside,
        in_specs=(spec, P(), P(), P(), P(), P()),
        out_specs=spec,
        check_vma=False,
    )
```

```python
import jax
import jax.numpy as jnp
from jax import lax
from jax.experimental import pallas as pl
from jax.experimental.pallas import tpu as pltpu
from jax.sharding import Mesh, PartitionSpec as P

STEP = 0.2
HALF2 = 0.5 * STEP * STEP
SLOTS = 4
TOTAL, TEAM_BEGIN, HERE_BEGIN, SIDE, COUNTS = 0, 1, 2, 3, 4
ROOTS = 72
BF = jnp.bfloat16
F32 = jnp.float32


def split(v):
    hi = v.astype(BF)
    return hi, (v - hi.astype(F32)).astype(BF)


def dot(a, b):
    return jnp.dot(a, b, preferred_element_type=F32)


def granules(vs):
    lane = lax.broadcasted_iota(jnp.int32, vs[0].shape, 1) // 16
    turned = [vs[0]] + [pltpu.roll(vs[k], 16 * k, 1) for k in range(1, 8)]
    cur = [turned[-k % 8] for k in range(8)]
    for bit in (1, 2, 4):
        pick = (lane & bit) != 0
        cur = [jnp.where(pick, cur[(m - bit) % 8], cur[m]) for m in range(8)]
    return [cur[0]] + [pltpu.roll(cur[m], 128 - 16 * m, 1) for m in range(1, 8)]


def once(method):
    def cached(self, p):
        key = (method.__name__, p)
        if key not in self.memo:
            self.memo[key] = method(self, p)
        return self.memo[key]

    return cached


class Nodes:
    def __init__(self, ints_ref, reals_ref, begin):
        self.memo = {}
        self.live = (ints_ref[TOTAL] >> 1) << 1
        self.begin = begin
        self.base = begin - 4
        self.reals = reals_ref
        self.gamma = (reals_ref[0], reals_ref[1])
        self.re = (reals_ref[2], reals_ref[4])
        self.im = (reals_ref[3], reals_ref[5])

    def root(self, n):
        return self.reals[jnp.clip(n, 0, ROOTS - 1) + 6]

    @once
    def up(self, p):
        g = self.base + p
        return jnp.where((g >= 0) & (g + 2 < self.live), self.root((g >> 1) + 1), 0.0)

    @once
    def down(self, p):
        g = self.base + p
        return jnp.where((g >= 2) & (g < self.live), self.root(g >> 1), 0.0)

    @once
    def middle(self, p):
        g = self.base + p
        n = (g >> 1).astype(F32)
        ok = (g >= 0) & (g < self.live)
        upper = jnp.where(ok & (g + 2 < self.live), n + 1.0, 0.0)
        return upper + jnp.where(ok & (g >= 2), n, 0.0)

    @once
    def even(self, p):
        g = self.base + p
        return jnp.where((g >= 0) & (g < self.live) & ((g & 1) == 0), 1.0, 0.0).astype(F32)

    @once
    def odd(self, p):
        g = self.base + p
        return jnp.where((g >= 0) & (g < self.live) & ((g & 1) == 1), 1.0, 0.0).astype(F32)

    @once
    def damp(self, p):
        g = self.base + p
        n0 = (g >> 1).astype(F32)
        n1 = (g & 1).astype(F32)
        return n0 * self.gamma[0] + n1 * self.gamma[1]


def scaled(s, v):
    return (s * v[0], s * v[1])


def plus(a, b):
    return (a[0] + b[0], a[1] + b[1])


def times(re, im, v):
    return (re * v[0] - im * v[1], re * v[1] + im * v[0])


def both(nodes, x, p, re, im):
    r = plus(scaled(nodes.up(p), x[p + 2]), scaled(re * nodes.down(p), x[p - 2]))
    t = scaled(im * nodes.down(p), x[p - 2])
    return (r[0] - t[1], r[1] + t[0]), (r[0] + t[1], r[1] - t[0])


def both1(nodes, x, p, re, im):
    r = plus(scaled(nodes.even(p), x[p + 1]), scaled(re * nodes.odd(p), x[p - 1]))
    t = scaled(im * nodes.odd(p), x[p - 1])
    return (r[0] - t[1], r[1] + t[0]), (r[0] + t[1], r[1] - t[0])


def first_order(nodes, x, p, re, im):
    here = nodes.damp(p)

    def w(q):
        return STEP - HALF2 * (here + nodes.damp(q))

    zero = scaled(w(p), x[p])
    up, down = scaled(w(p + 2) * nodes.up(p), x[p + 2]), scaled(w(p - 2) * nodes.down(p), x[p - 2])
    one = plus(up, times(re[0], im[0], down))
    up, down = scaled(w(p + 1) * nodes.even(p), x[p + 1]), scaled(w(p - 1) * nodes.odd(p), x[p - 1])
    two = plus(up, times(re[1], im[1], down))
    return zero, one, two


def put(hi_ref, lo_ref, block, col, j, rows, v):
    hi, lo = split(jnp.concatenate([v[0], v[1]], axis=0))
    at = pl.ds(block * 128 + j * rows, rows)
    hi_ref[at, 256 * col : 256 * col + 256] = hi
    lo_ref[at, 256 * col : 256 * col + 256] = lo


def times_weights(hi_ref, lo_ref, ghi_ref, glo_ref):
    hi, g = hi_ref[...], ghi_ref[...]
    return dot(hi, g) + dot(lo_ref[...], g) + dot(hi, glo_ref[...])


def weights_kernel(h_ref, q_ref, vhi, vlo, hhi, hlo):
    for b in range(3):
        hi, lo = split(h_ref[...] if b == 0 else q_ref[b - 1])
        vhi[256 * b : 256 * b + 256, :] = hi
        vlo[256 * b : 256 * b + 256, :] = lo
        hhi[:, 256 * b : 256 * b + 256] = hi
        hlo[:, 256 * b : 256 * b + 256] = lo


def own_kernel(x_ref, o_ref, t_ref, sem):
    t_ref[...] = x_ref[...].T.reshape(32, 8, 128)
    copy = pltpu.make_async_copy(t_ref, o_ref.at[:, 0:8], sem)
    copy.start()
    copy.wait()


def fetch(pairs, sem):
    copies = [pltpu.make_async_copy(source, target, sem.at[i]) for i, (source, target) in enumerate(pairs)]
    for copy in copies:
        copy.start()
    return copies


def halo_kernel(ints_in, far_ref, near_ref, _, o_ref, t_ref, ints_ref, sem, out_sem):
    fetched = fetch([(ints_in, ints_ref)], sem)
    near = near_ref[...].reshape(128, 256).T
    far = far_ref[...].reshape(128, 256).T
    lane = lax.broadcasted_iota(jnp.int32, near.shape, 1)
    for copy in fetched:
        copy.wait()
    lower = ints_ref[SIDE] == 0
    count = jnp.where(lower, ints_ref[COUNTS + 1], ints_ref[COUNTS + 3])
    near = pltpu.roll(near, jnp.where(lower, 4 - count, 0) * 32, 1)
    far = pltpu.roll(far, ((jnp.where(lower, 8 - count - ints_ref[COUNTS], count)) & 3) * 32, 1)
    inside = (lane >= jnp.where(lower, 4 - count, 0) * 32) & (lane < jnp.where(lower, 4, count) * 32)
    t_ref[...] = jnp.where(inside, near, far).reshape(32, 8, 128)
    copy = pltpu.make_async_copy(t_ref, o_ref.at[:, 8:16], out_sem)
    copy.start()
    copy.wait()


def column_kernel(
    ints_in, reals_in, got_ref, ghi_ref, glo_ref, o_ref, y_ref, hi_ref, lo_ref, hi2_ref, lo2_ref, z_ref, send_ref, ints_ref, reals_ref, sem, out_sem
):
    fetched = fetch([(ints_in, ints_ref), (reals_in, reals_ref)], sem)
    places = ((1, 0), (0, 0), (0, 1), (1, 1))
    for i, (g, r) in enumerate(places):
        vs = []
        for low in range(8):
            vs.append(jnp.concatenate([got_ref[(8 * high + low) * 2 + r, 8 * g : 8 * g + 8, :] for high in range(2)], axis=0))
        for m, v in enumerate(granules(vs)):
            y_ref[SLOTS * i + m // 2, m % 2] = jnp.concatenate([v[:8], v[8:]], axis=1)
    for copy in fetched:
        copy.wait()
    nodes = Nodes(ints_ref, reals_ref, ints_ref[TEAM_BEGIN])
    own, other = ints_ref[COUNTS + 2 - ints_ref[SIDE]], ints_ref[COUNTS + 3 - ints_ref[SIDE]]
    re, im = nodes.re, nodes.im

    def slot(p):
        j = p - 4
        if j < 0:
            return p
        return jnp.where(j < own, 4 + j, jnp.where(j < own + other, 8 + j - own, jnp.minimum(12 + j - own - other, 15)))

    x = []
    for p in range(16):
        v = y_ref[slot(p)]
        x.append((v[0], v[1]))
    a2, b2 = {}, {}
    for p in range(2, 14):
        a2[p], b2[p] = both1(nodes, x, p, re[1], im[1])
    for j in range(8):
        p = j + 4
        a1, b1 = both(nodes, x, p, re[0], im[0])
        a12, b1a2 = both(nodes, a2, p, re[0], im[0])
        a1b2, _ = both(nodes, b2, p, re[0], im[0])
        far = scaled(nodes.up(p) * nodes.up(p + 2), x[p + 4])
        low = scaled(nodes.down(p) * nodes.down(p - 2), x[p - 4])
        mid = nodes.middle(p)
        here = scaled(mid, x[p])
        a11 = plus(plus(far, times(re[0], im[0], here)), times(re[0] * re[0] - im[0] * im[0], 2.0 * re[0] * im[0], low))
        s11 = plus(plus(scaled(2.0, far), scaled(2.0 * re[0], here)), scaled(2.0 * (re[0] * re[0] + im[0] * im[0]), low))
        rows = (
            (x[p], a1, a2[p]),
            (a1, a11, a12),
            (a2[p], a12, times(re[1], im[1], x[p])),
            (scaled(2.0, b1), s11, scaled(2.0, b1a2)),
            (scaled(2.0, b2[p]), scaled(2.0, a1b2), scaled(2.0 * re[1], x[p])),
        )
        for block, row in enumerate(rows):
            for col, v in enumerate(row):
                put(hi_ref, lo_ref, block, col, j, 16, v)
    sums = times_weights(hi_ref, lo_ref, ghi_ref, glo_ref)
    for j in range(8):
        p = j + 4
        for block, v in enumerate(first_order(nodes, x, p, re, im)):
            s = sums[block * 128 + 16 * j : block * 128 + 16 * j + 16]
            put(hi2_ref, lo2_ref, 0, block, j, 16, (v[1] - HALF2 * s[:8], -v[0] - HALF2 * s[8:]))
        z_ref[1, j] = (2.0 * HALF2) * sums[16 * j : 16 * j + 16].reshape(2, 8, 256)
        z_ref[2, j] = HALF2 * sums[384 + 16 * j : 400 + 16 * j].reshape(2, 8, 256)
        z_ref[3, j] = HALF2 * sums[512 + 16 * j : 528 + 16 * j].reshape(2, 8, 256)

    def send(z):
        for r in range(2):
            vs = []
            for m in range(8):
                v = z_ref[z, m // 2 if r == 0 else own + m // 2, m % 2]
                vs.append(jnp.concatenate([v[:, :128], v[:, 128:]], axis=0))
            for low, v in enumerate(granules(vs)):
                for high in range(2):
                    send_ref[z, (8 * high + low) * 2 + r] = v[8 * high : 8 * high + 8]
        copy = pltpu.make_async_copy(send_ref.at[z], o_ref.at[:, 8 * z : 8 * z + 8], out_sem.at[z])
        copy.start()
        return copy

    last = times_weights(hi2_ref, lo2_ref, ghi_ref, glo_ref)
    copies = [send(z) for z in range(1, 4)]
    z_ref[0] = last.reshape(8, 2, 8, 256)
    for copy in [*copies, send(0)]:
        copy.wait()


def row_kernel(
    ints_ref, reals_ref, x_ref, p1_ref, p2_ref, p3_ref, p4_ref, ghi_ref, glo_ref, o_ref, w_ref, hi_ref, lo_ref, hi2_ref, lo2_ref
):
    nodes = Nodes(ints_ref, reals_ref, ints_ref[HERE_BEGIN])
    re, im = nodes.re, (-nodes.im[0], -nodes.im[1])
    up = ints_ref[SIDE]
    farther, below, own, above = (ints_ref[COUNTS + i] for i in range(4))
    w_ref[8:12] = x_ref[...]
    w_ref[pl.ds(4 + 8 * up, 4)] = p1_ref[...]
    w_ref[pl.ds(16 * up, 4)] = p2_ref[...]
    w_ref[pl.ds(12 - 8 * up, 4)] = p3_ref[...]
    w_ref[pl.ds(16 - 16 * up, 4)] = p4_ref[...]

    def slot(p):
        j = p - 4
        if j < 0:
            return jnp.where(j + below >= 0, 4 + j + below, farther + j + below)
        return jnp.where(j < own, 8 + j, jnp.where(j < own + above, 12 + j - own, jnp.minimum(16 + j - own - above, 19)))

    x = []
    for p in range(12):
        v = w_ref[slot(p)]
        x.append((v[0], v[1]))
    b2 = {}
    for p in range(2, 10):
        b2[p], _ = both1(nodes, x, p, re[1], im[1])
    for j in range(4):
        p = j + 4
        b1, _ = both(nodes, x, p, re[0], im[0])
        b12, _ = both(nodes, b2, p, re[0], im[0])
        far = scaled(nodes.up(p) * nodes.up(p + 2), x[p + 4])
        low = scaled(nodes.down(p) * nodes.down(p - 2), x[p - 4])
        here = scaled(nodes.middle(p), x[p])
        b11 = plus(plus(far, times(re[0], im[0], here)), times(re[0] * re[0] - im[0] * im[0], 2.0 * re[0] * im[0], low))
        rows = ((x[p], b1, b2[p]), (b1, b11, b12), (b2[p], b12, times(re[1], im[1], x[p])))
        for block, row in enumerate(rows):
            for col, v in enumerate(row):
                put(hi_ref, lo_ref, block, col, j, 32, v)
    sums = times_weights(hi_ref, lo_ref, ghi_ref, glo_ref)
    for j in range(4):
        p = j + 4
        for block, v in enumerate(first_order(nodes, x, p, re, im)):
            s = sums[block * 128 + 32 * j : block * 128 + 32 * j + 32]
            put(hi2_ref, lo2_ref, 0, block, j, 32, (-v[1] - HALF2 * s[:16], v[0] - HALF2 * s[16:]))
    right = times_weights(hi2_ref, lo2_ref, ghi_ref, glo_ref)
    for j in range(4):
        d = nodes.damp(j + 4)
        keep = 1.0 - STEP * d + HALF2 * d * d
        old = x_ref[j].reshape(32, 256)
        live = (j < own) & (nodes.begin + j < nodes.live)
        o_ref[32 * j : 32 * j + 32, :] = jnp.where(live, keep * old + right[32 * j : 32 * j + 32], old)


def finish_kernel(ints_in, got_ref, base_ref, ghi_ref, glo_ref, o_ref, ints_ref, sem):
    fetched = fetch([(ints_in, ints_ref)], sem)
    his, los = [], []
    for z in range(1, 4):
        hi, lo = split(got_ref[:, 8 * z : 8 * z + 8, :].reshape(256, 128))
        his.append(hi)
        los.append(lo)
    hi, lo = jnp.concatenate(his, axis=0), jnp.concatenate(los, axis=0)
    g = ghi_ref[...]
    out = dot(g, hi) + dot(g, lo) + dot(glo_ref[...], hi) + got_ref[:, :8, :].reshape(256, 128)
    out = out.T
    for copy in fetched:
        copy.wait()
    own, begin, limit = ints_ref[COUNTS + 2], ints_ref[HERE_BEGIN], (ints_ref[TOTAL] >> 1) << 1
    for j in range(4):
        live = (j < own) & (begin + j < limit)
        rows = slice(32 * j, 32 * j + 32)
        o_ref[rows, :] = base_ref[rows, :] + jnp.where(live, out[rows], 0.0)


SMEM = pl.BlockSpec(memory_space=pltpu.SMEM)
VMEM = pl.BlockSpec(memory_space=pltpu.VMEM)
ANY = pl.BlockSpec(memory_space=pl.ANY)


def call(kernel, outs, specs, scratch=(), flops=1_000_000, name=None, out_specs=None, aliases=None):
    return pl.pallas_call(
        kernel,
        out_shape=outs,
        in_specs=specs,
        out_specs=out_specs or jax.tree.map(lambda _: VMEM, outs),
        input_output_aliases=aliases or {},
        scratch_shapes=list(scratch),
        compiler_params=pltpu.CompilerParams(vmem_limit_bytes=48 * 1024 * 1024),
        cost_estimate=pl.CostEstimate(flops=flops, bytes_accessed=4_000_000, transcendentals=0),
        name=name,
    )


def struct(shape, dtype=F32):
    return jax.ShapeDtypeStruct(shape, dtype)


weights_call = call(
    weights_kernel,
    (struct((768, 256), BF), struct((768, 256), BF), struct((256, 768), BF), struct((256, 768), BF)),
    [VMEM] * 2,
    name="weights",
)
own_call = call(
    own_kernel, struct((32, 16, 128)), [VMEM], [pltpu.VMEM((32, 8, 128), F32), pltpu.SemaphoreType.DMA], out_specs=ANY, name="own"
)
INTS = pltpu.SMEM((16,), jnp.int32)
halo_call = call(
    halo_kernel,
    struct((32, 16, 128)),
    [ANY] + [VMEM] * 2 + [ANY],
    [pltpu.VMEM((32, 8, 128), F32), INTS, pltpu.SemaphoreType.DMA((1,)), pltpu.SemaphoreType.DMA],
    out_specs=ANY,
    aliases={3: 0},
    name="halo",
)
column_call = call(
    column_kernel,
    struct((32, 32, 128)),
    [ANY] * 2 + [VMEM] * 3,
    [
        pltpu.VMEM((16, 2, 8, 256), F32),
        pltpu.VMEM((640, 768), BF),
        pltpu.VMEM((640, 768), BF),
        pltpu.VMEM((128, 768), BF),
        pltpu.VMEM((128, 768), BF),
        pltpu.VMEM((4, 8, 2, 8, 256), F32),
        pltpu.VMEM((4, 32, 8, 128), F32),
        INTS,
        pltpu.SMEM((6 + ROOTS,), F32),
        pltpu.SemaphoreType.DMA((2,)),
        pltpu.SemaphoreType.DMA((4,)),
    ],
    flops=1_000_000_000,
    out_specs=ANY,
    name="columns",
)
row_call = call(
    row_kernel,
    struct((128, 256)),
    [SMEM] * 2 + [VMEM] * 7,
    [
        pltpu.VMEM((20, 2, 16, 256), F32),
        pltpu.VMEM((384, 768), BF),
        pltpu.VMEM((384, 768), BF),
        pltpu.VMEM((128, 768), BF),
        pltpu.VMEM((128, 768), BF),
    ],
    flops=1_000_000_000,
    name="rows",
)
finish_call = call(
    finish_kernel, struct((128, 256)), [ANY] + [VMEM] * 4, [INTS, pltpu.SemaphoreType.DMA((1,))], flops=300_000_000, name="finish"
)


def swap_routes(shards):
    pairs = [(i, i + 1) for i in range(1, shards - 1, 2)]
    near = pairs + [(b, a) for a, b in pairs]
    far = [(i, i + 2) for i in range(0, shards - 2, 2)] + [(i, i - 2) for i in range(3, shards, 2)]
    pairs = [(i, i + 1) for i in range(0, shards, 2)]
    inner = pairs + [(b, a) for a, b in pairs]
    back = [(i, i - 2) for i in range(2, shards, 2)] + [(i, i + 2) for i in range(1, shards - 2, 2)]
    return near, far, inner, back


def integers(node_count):
    shards = node_count.shape[0]
    team, side = lax.axis_index("team"), lax.axis_index("r")
    here = 2 * team + side
    row = jnp.arange(16, dtype=jnp.int32)[:, None]
    column = jnp.arange(shards, dtype=jnp.int32)[None, :]
    near = jnp.clip(here + row - (COUNTS + 2), 0, shards - 1)
    wanted = (
        (row == TOTAL)
        | ((row == TEAM_BEGIN) & (column < 2 * team))
        | ((row == HERE_BEGIN) & (column < here))
        | ((row >= COUNTS) & (column == near))
    )
    sums = jnp.sum(jnp.where(wanted, node_count[None, :], 0), axis=1)
    return sums + jnp.where(row[:, 0] == SIDE, side, 0)


def on_device(densities, hamiltonian, couplings, gamma, coeff, node_count):
    hier = ("team", "r")
    group = ("col", "r")
    ints = integers(node_count)
    reals = jnp.concatenate([gamma, coeff.reshape(4), jnp.sqrt(jnp.arange(ROOTS, dtype=F32))])
    near, far, inner, back = swap_routes(node_count.shape[0])
    p2 = lax.ppermute(densities, hier, far)
    p1 = lax.ppermute(densities, hier, near)
    part = own_call(densities.reshape(128, 256))
    vhi, vlo, hhi, hlo = weights_call(hamiltonian, couplings)
    sent = halo_call(ints, p2, p1, part)
    sent, again = lax.optimization_barrier((sent, densities))
    got = lax.all_to_all(sent, group, 0, 0, tiled=True)
    p3 = lax.ppermute(again, hier, inner)
    back_sent = column_call(ints, reals, got, vhi, vlo)
    back_sent, p3, again = lax.optimization_barrier((back_sent, p3, densities))
    back_got = lax.all_to_all(back_sent, group, 0, 0, tiled=True)
    p4 = lax.ppermute(again, hier, back)
    base = row_call(ints, reals, densities, p1, p2, p3, p4, vhi, vlo)
    out = finish_call(ints, back_got, base, hhi, hlo)
    return out.reshape(4, 2, 16, 256)


def solution(mesh):
    devices = mesh.devices
    inside = Mesh(devices.reshape(devices.shape[0] // 2, 2, devices.shape[1]), ("team", "r", "col"))
    spec = P(("team", "r"), None, "col", None)
    return jax.shard_map(
        on_device,
        mesh=inside,
        in_specs=(spec, P(), P(), P(), P(), P()),
        out_specs=spec,
        check_vma=False,
    )
```

```python
import jax
import jax.numpy as jnp
from jax import lax
from jax.experimental import pallas as pl
from jax.experimental.pallas import tpu as pltpu
from jax.sharding import Mesh, PartitionSpec as P

STEP = 0.2
HALF2 = 0.5 * STEP * STEP
SLOTS = 4
TOTAL, TEAM_BEGIN, HERE_BEGIN, SIDE, COUNTS = 0, 1, 2, 3, 4
ROOTS = 72
BF = jnp.bfloat16
F32 = jnp.float32


def split(v):
    hi = v.astype(BF)
    return hi, (v - hi.astype(F32)).astype(BF)


def dot(a, b):
    return jnp.dot(a, b, preferred_element_type=F32)


def granules(vs):
    lane = lax.broadcasted_iota(jnp.int32, vs[0].shape, 1) // 16
    turned = [vs[0]] + [pltpu.roll(vs[k], 16 * k, 1) for k in range(1, 8)]
    cur = [turned[-k % 8] for k in range(8)]
    for bit in (1, 2, 4):
        pick = (lane & bit) != 0
        cur = [jnp.where(pick, cur[(m - bit) % 8], cur[m]) for m in range(8)]
    return [cur[0]] + [pltpu.roll(cur[m], 128 - 16 * m, 1) for m in range(1, 8)]


def once(method):
    def cached(self, p):
        key = (method.__name__, p)
        if key not in self.memo:
            self.memo[key] = method(self, p)
        return self.memo[key]

    return cached


class Nodes:
    def __init__(self, ints_ref, reals_ref, begin):
        self.memo = {}
        self.live = (ints_ref[TOTAL] >> 1) << 1
        self.begin = begin
        self.base = begin - 4
        self.reals = reals_ref
        self.gamma = (reals_ref[0], reals_ref[1])
        self.re = (reals_ref[2], reals_ref[4])
        self.im = (reals_ref[3], reals_ref[5])

    def root(self, n):
        return self.reals[jnp.clip(n, 0, ROOTS - 1) + 6]

    @once
    def up(self, p):
        g = self.base + p
        return jnp.where((g >= 0) & (g + 2 < self.live), self.root((g >> 1) + 1), 0.0)

    @once
    def down(self, p):
        g = self.base + p
        return jnp.where((g >= 2) & (g < self.live), self.root(g >> 1), 0.0)

    @once
    def middle(self, p):
        g = self.base + p
        n = (g >> 1).astype(F32)
        ok = (g >= 0) & (g < self.live)
        upper = jnp.where(ok & (g + 2 < self.live), n + 1.0, 0.0)
        return upper + jnp.where(ok & (g >= 2), n, 0.0)

    @once
    def even(self, p):
        g = self.base + p
        return jnp.where((g >= 0) & (g < self.live) & ((g & 1) == 0), 1.0, 0.0).astype(F32)

    @once
    def odd(self, p):
        g = self.base + p
        return jnp.where((g >= 0) & (g < self.live) & ((g & 1) == 1), 1.0, 0.0).astype(F32)

    @once
    def damp(self, p):
        g = self.base + p
        n0 = (g >> 1).astype(F32)
        n1 = (g & 1).astype(F32)
        return n0 * self.gamma[0] + n1 * self.gamma[1]


def scaled(s, v):
    return (s * v[0], s * v[1])


def plus(a, b):
    return (a[0] + b[0], a[1] + b[1])


def times(re, im, v):
    return (re * v[0] - im * v[1], re * v[1] + im * v[0])


def both(nodes, x, p, re, im):
    r = plus(scaled(nodes.up(p), x[p + 2]), scaled(re * nodes.down(p), x[p - 2]))
    t = scaled(im * nodes.down(p), x[p - 2])
    return (r[0] - t[1], r[1] + t[0]), (r[0] + t[1], r[1] - t[0])


def both1(nodes, x, p, re, im):
    r = plus(scaled(nodes.even(p), x[p + 1]), scaled(re * nodes.odd(p), x[p - 1]))
    t = scaled(im * nodes.odd(p), x[p - 1])
    return (r[0] - t[1], r[1] + t[0]), (r[0] + t[1], r[1] - t[0])


def first_order(nodes, x, p, re, im):
    here = nodes.damp(p)

    def w(q):
        return STEP - HALF2 * (here + nodes.damp(q))

    zero = scaled(w(p), x[p])
    up, down = scaled(w(p + 2) * nodes.up(p), x[p + 2]), scaled(w(p - 2) * nodes.down(p), x[p - 2])
    one = plus(up, times(re[0], im[0], down))
    up, down = scaled(w(p + 1) * nodes.even(p), x[p + 1]), scaled(w(p - 1) * nodes.odd(p), x[p - 1])
    two = plus(up, times(re[1], im[1], down))
    return zero, one, two


def put(hi_ref, lo_ref, block, col, j, rows, v):
    hi, lo = split(jnp.concatenate([v[0], v[1]], axis=0))
    at = pl.ds(block * 128 + j * rows, rows)
    hi_ref[at, 256 * col : 256 * col + 256] = hi
    lo_ref[at, 256 * col : 256 * col + 256] = lo


def times_weights(hi_ref, lo_ref, ghi_ref, glo_ref):
    hi, g = hi_ref[...], ghi_ref[...]
    return dot(hi, g) + dot(lo_ref[...], g) + dot(hi, glo_ref[...])


def weights_kernel(h_ref, q_ref, vhi, vlo, hhi, hlo):
    for b in range(3):
        hi, lo = split(h_ref[...] if b == 0 else q_ref[b - 1])
        vhi[256 * b : 256 * b + 256, :] = hi
        vlo[256 * b : 256 * b + 256, :] = lo
        hhi[:, 256 * b : 256 * b + 256] = hi
        hlo[:, 256 * b : 256 * b + 256] = lo


def own_kernel(x_ref, o_ref, t_ref, sem):
    t_ref[...] = x_ref[...].T.reshape(32, 8, 128)
    copy = pltpu.make_async_copy(t_ref, o_ref.at[:, 0:8], sem)
    copy.start()
    copy.wait()


def fetch(pairs, sem):
    copies = [pltpu.make_async_copy(source, target, sem.at[i]) for i, (source, target) in enumerate(pairs)]
    for copy in copies:
        copy.start()
    return copies


def halo_kernel(wide_ref, far_ref, near_ref, _, o_ref, t_ref, sem):
    def row(i):
        return wide_ref[i : i + 1, :]

    def turned(v, by, choices):
        out = v
        for k in range(1, choices):
            out = jnp.where(by == k, pltpu.roll(v, 32 * k, 1), out)
        return out

    side = row(SIDE)
    lower = 1 - side
    count = lower * row(COUNTS + 1) + side * row(COUNTS + 3)
    by_near = jnp.broadcast_to(lower * (4 - count), (256, 128))
    by_far = jnp.broadcast_to((lower * (8 - count - row(COUNTS)) + side * count) & 3, (256, 128))
    begin = jnp.broadcast_to(lower * (4 - count), (256, 128))
    end = jnp.broadcast_to(lower * 4 + side * count, (256, 128))
    near = turned(near_ref[...].reshape(128, 256).T, by_near, 3)
    far = turned(far_ref[...].reshape(128, 256).T, by_far, 4)
    node = lax.broadcasted_iota(jnp.int32, (256, 128), 1) // 32
    t_ref[...] = jnp.where(node >= begin, jnp.where(node < end, near, far), far).reshape(32, 8, 128)
    copy = pltpu.make_async_copy(t_ref, o_ref.at[:, 8:16], sem)
    copy.start()
    copy.wait()


def pair_kernel(ints_ref, x_ref, near_ref, o_ref):
    o_ref[0:4] = x_ref[...]
    o_ref[4:6] = near_ref[pl.ds(jnp.where(ints_ref[SIDE] == 0, ints_ref[COUNTS + 1] - 2, 0), 2)]


def column_kernel(
    ints_in, reals_in, got_ref, ghi_ref, glo_ref, o_ref, y_ref, hi_ref, lo_ref, hi2_ref, lo2_ref, z_ref, send_ref, ints_ref, reals_ref, sem, out_sem
):
    fetched = fetch([(ints_in, ints_ref), (reals_in, reals_ref)], sem)
    places = ((1, 0), (0, 0), (0, 1), (1, 1))
    for i, (g, r) in enumerate(places):
        vs = []
        for low in range(8):
            vs.append(jnp.concatenate([got_ref[(8 * high + low) * 2 + r, 8 * g : 8 * g + 8, :] for high in range(2)], axis=0))
        for m, v in enumerate(granules(vs)):
            y_ref[SLOTS * i + m // 2, m % 2] = jnp.concatenate([v[:8], v[8:]], axis=1)
    for copy in fetched:
        copy.wait()
    nodes = Nodes(ints_ref, reals_ref, ints_ref[TEAM_BEGIN])
    own, other = ints_ref[COUNTS + 2 - ints_ref[SIDE]], ints_ref[COUNTS + 3 - ints_ref[SIDE]]
    re, im = nodes.re, nodes.im

    def slot(p):
        j = p - 4
        if j < 0:
            return p
        return jnp.where(j < own, 4 + j, jnp.where(j < own + other, 8 + j - own, jnp.minimum(12 + j - own - other, 15)))

    x = []
    for p in range(16):
        v = y_ref[slot(p)]
        x.append((v[0], v[1]))
    a2, b2 = {}, {}
    for p in range(2, 14):
        a2[p], b2[p] = both1(nodes, x, p, re[1], im[1])
    for j in range(8):
        p = j + 4
        a1, b1 = both(nodes, x, p, re[0], im[0])
        a12, b1a2 = both(nodes, a2, p, re[0], im[0])
        a1b2, _ = both(nodes, b2, p, re[0], im[0])
        far = scaled(nodes.up(p) * nodes.up(p + 2), x[p + 4])
        low = scaled(nodes.down(p) * nodes.down(p - 2), x[p - 4])
        mid = nodes.middle(p)
        here = scaled(mid, x[p])
        a11 = plus(plus(far, times(re[0], im[0], here)), times(re[0] * re[0] - im[0] * im[0], 2.0 * re[0] * im[0], low))
        s11 = plus(plus(scaled(2.0, far), scaled(2.0 * re[0], here)), scaled(2.0 * (re[0] * re[0] + im[0] * im[0]), low))
        rows = (
            (x[p], a1, a2[p]),
            (a1, a11, a12),
            (a2[p], a12, times(re[1], im[1], x[p])),
            (scaled(2.0, b1), s11, scaled(2.0, b1a2)),
            (scaled(2.0, b2[p]), scaled(2.0, a1b2), scaled(2.0 * re[1], x[p])),
        )
        for block, row in enumerate(rows):
            for col, v in enumerate(row):
                put(hi_ref, lo_ref, block, col, j, 16, v)
    sums = times_weights(hi_ref, lo_ref, ghi_ref, glo_ref)
    for j in range(8):
        p = j + 4
        for block, v in enumerate(first_order(nodes, x, p, re, im)):
            s = sums[block * 128 + 16 * j : block * 128 + 16 * j + 16]
            put(hi2_ref, lo2_ref, 0, block, j, 16, (v[1] - HALF2 * s[:8], -v[0] - HALF2 * s[8:]))
        z_ref[1, j] = (2.0 * HALF2) * sums[16 * j : 16 * j + 16].reshape(2, 8, 256)
        z_ref[2, j] = HALF2 * sums[384 + 16 * j : 400 + 16 * j].reshape(2, 8, 256)
        z_ref[3, j] = HALF2 * sums[512 + 16 * j : 528 + 16 * j].reshape(2, 8, 256)

    def send(z):
        for r in range(2):
            vs = []
            for m in range(8):
                v = z_ref[z, m // 2 if r == 0 else own + m // 2, m % 2]
                vs.append(jnp.concatenate([v[:, :128], v[:, 128:]], axis=0))
            for low, v in enumerate(granules(vs)):
                for high in range(2):
                    send_ref[z, (8 * high + low) * 2 + r] = v[8 * high : 8 * high + 8]
        copy = pltpu.make_async_copy(send_ref.at[z], o_ref.at[:, 8 * z : 8 * z + 8], out_sem.at[z])
        copy.start()
        return copy

    last = times_weights(hi2_ref, lo2_ref, ghi_ref, glo_ref)
    copies = [send(z) for z in range(1, 4)]
    z_ref[0] = last.reshape(8, 2, 8, 256)
    for copy in [*copies, send(0)]:
        copy.wait()


def row_kernel(
    ints_ref, reals_ref, x_ref, p1_ref, p2_ref, pair_ref, ghi_ref, glo_ref, o_ref, w_ref, hi_ref, lo_ref, hi2_ref, lo2_ref
):
    nodes = Nodes(ints_ref, reals_ref, ints_ref[HERE_BEGIN])
    re, im = nodes.re, (-nodes.im[0], -nodes.im[1])
    up = ints_ref[SIDE]
    farther, below, own, above = (ints_ref[COUNTS + i] for i in range(4))
    w_ref[8:12] = x_ref[...]
    w_ref[pl.ds(4 + 8 * up, 4)] = p1_ref[...]
    w_ref[pl.ds(16 * up, 4)] = p2_ref[...]
    w_ref[pl.ds(12 - 8 * up, 4)] = pair_ref[0:4]
    w_ref[pl.ds(jnp.where(up == 0, 16, farther - 2), 2)] = pair_ref[4:6]

    def slot(p):
        j = p - 4
        if j < 0:
            return jnp.where(j + below >= 0, 4 + j + below, farther + j + below)
        return jnp.where(j < own, 8 + j, jnp.where(j < own + above, 12 + j - own, jnp.minimum(16 + j - own - above, 19)))

    x = []
    for p in range(12):
        v = w_ref[slot(p)]
        x.append((v[0], v[1]))
    b2 = {}
    for p in range(2, 10):
        b2[p], _ = both1(nodes, x, p, re[1], im[1])
    for j in range(4):
        p = j + 4
        b1, _ = both(nodes, x, p, re[0], im[0])
        b12, _ = both(nodes, b2, p, re[0], im[0])
        far = scaled(nodes.up(p) * nodes.up(p + 2), x[p + 4])
        low = scaled(nodes.down(p) * nodes.down(p - 2), x[p - 4])
        here = scaled(nodes.middle(p), x[p])
        b11 = plus(plus(far, times(re[0], im[0], here)), times(re[0] * re[0] - im[0] * im[0], 2.0 * re[0] * im[0], low))
        rows = ((x[p], b1, b2[p]), (b1, b11, b12), (b2[p], b12, times(re[1], im[1], x[p])))
        for block, row in enumerate(rows):
            for col, v in enumerate(row):
                put(hi_ref, lo_ref, block, col, j, 32, v)
    sums = times_weights(hi_ref, lo_ref, ghi_ref, glo_ref)
    for j in range(4):
        p = j + 4
        for block, v in enumerate(first_order(nodes, x, p, re, im)):
            s = sums[block * 128 + 32 * j : block * 128 + 32 * j + 32]
            put(hi2_ref, lo2_ref, 0, block, j, 32, (-v[1] - HALF2 * s[:16], v[0] - HALF2 * s[16:]))
    right = times_weights(hi2_ref, lo2_ref, ghi_ref, glo_ref)
    for j in range(4):
        d = nodes.damp(j + 4)
        keep = 1.0 - STEP * d + HALF2 * d * d
        old = x_ref[j].reshape(32, 256)
        live = (j < own) & (nodes.begin + j < nodes.live)
        o_ref[32 * j : 32 * j + 32, :] = jnp.where(live, keep * old + right[32 * j : 32 * j + 32], old)


def finish_kernel(ints_in, got_ref, base_ref, ghi_ref, glo_ref, o_ref, ints_ref, sem):
    fetched = fetch([(ints_in, ints_ref)], sem)
    his, los = [], []
    for z in range(1, 4):
        hi, lo = split(got_ref[:, 8 * z : 8 * z + 8, :].reshape(256, 128))
        his.append(hi)
        los.append(lo)
    hi, lo = jnp.concatenate(his, axis=0), jnp.concatenate(los, axis=0)
    g = ghi_ref[...]
    out = dot(g, hi) + dot(g, lo) + dot(glo_ref[...], hi) + got_ref[:, :8, :].reshape(256, 128)
    out = out.T
    for copy in fetched:
        copy.wait()
    own, begin, limit = ints_ref[COUNTS + 2], ints_ref[HERE_BEGIN], (ints_ref[TOTAL] >> 1) << 1
    for j in range(4):
        live = (j < own) & (begin + j < limit)
        rows = slice(32 * j, 32 * j + 32)
        o_ref[rows, :] = base_ref[rows, :] + jnp.where(live, out[rows], 0.0)


SMEM = pl.BlockSpec(memory_space=pltpu.SMEM)
VMEM = pl.BlockSpec(memory_space=pltpu.VMEM)
ANY = pl.BlockSpec(memory_space=pl.ANY)


def call(kernel, outs, specs, scratch=(), flops=1_000_000, name=None, out_specs=None, aliases=None):
    return pl.pallas_call(
        kernel,
        out_shape=outs,
        in_specs=specs,
        out_specs=out_specs or jax.tree.map(lambda _: VMEM, outs),
        input_output_aliases=aliases or {},
        scratch_shapes=list(scratch),
        compiler_params=pltpu.CompilerParams(vmem_limit_bytes=48 * 1024 * 1024),
        cost_estimate=pl.CostEstimate(flops=flops, bytes_accessed=4_000_000, transcendentals=0),
        name=name,
    )


def struct(shape, dtype=F32):
    return jax.ShapeDtypeStruct(shape, dtype)


weights_call = call(
    weights_kernel,
    (struct((768, 256), BF), struct((768, 256), BF), struct((256, 768), BF), struct((256, 768), BF)),
    [VMEM] * 2,
    name="weights",
)
own_call = call(
    own_kernel, struct((32, 16, 128)), [VMEM], [pltpu.VMEM((32, 8, 128), F32), pltpu.SemaphoreType.DMA], out_specs=ANY, name="own"
)
INTS = pltpu.SMEM((16,), jnp.int32)
halo_call = call(
    halo_kernel,
    struct((32, 16, 128)),
    [VMEM] * 3 + [ANY],
    [pltpu.VMEM((32, 8, 128), F32), pltpu.SemaphoreType.DMA],
    out_specs=ANY,
    aliases={3: 0},
    name="halo",
)
pair_call = call(pair_kernel, struct((6, 2, 16, 256)), [SMEM] + [VMEM] * 2, name="pair")
column_call = call(
    column_kernel,
    struct((32, 32, 128)),
    [ANY] * 2 + [VMEM] * 3,
    [
        pltpu.VMEM((16, 2, 8, 256), F32),
        pltpu.VMEM((640, 768), BF),
        pltpu.VMEM((640, 768), BF),
        pltpu.VMEM((128, 768), BF),
        pltpu.VMEM((128, 768), BF),
        pltpu.VMEM((4, 8, 2, 8, 256), F32),
        pltpu.VMEM((4, 32, 8, 128), F32),
        INTS,
        pltpu.SMEM((6 + ROOTS,), F32),
        pltpu.SemaphoreType.DMA((2,)),
        pltpu.SemaphoreType.DMA((4,)),
    ],
    flops=1_000_000_000,
    out_specs=ANY,
    name="columns",
)
row_call = call(
    row_kernel,
    struct((128, 256)),
    [SMEM] * 2 + [VMEM] * 6,
    [
        pltpu.VMEM((20, 2, 16, 256), F32),
        pltpu.VMEM((384, 768), BF),
        pltpu.VMEM((384, 768), BF),
        pltpu.VMEM((128, 768), BF),
        pltpu.VMEM((128, 768), BF),
    ],
    flops=1_000_000_000,
    name="rows",
)
finish_call = call(
    finish_kernel, struct((128, 256)), [ANY] + [VMEM] * 4, [INTS, pltpu.SemaphoreType.DMA((1,))], flops=300_000_000, name="finish"
)


def routes(shards):
    pairs = [(i, i + 1) for i in range(1, shards - 1, 2)]
    near = pairs + [(b, a) for a, b in pairs]
    far = [(i, i + 2) for i in range(0, shards - 2, 2)] + [(i, i - 2) for i in range(3, shards, 2)]
    pairs = [(i, i + 1) for i in range(0, shards, 2)]
    return near, far, pairs + [(b, a) for a, b in pairs]


def integers(node_count):
    shards = node_count.shape[0]
    team, side = lax.axis_index("team"), lax.axis_index("r")
    here = 2 * team + side
    row = jnp.arange(16, dtype=jnp.int32)[:, None]
    column = jnp.arange(shards, dtype=jnp.int32)[None, :]
    near = jnp.clip(here + row - (COUNTS + 2), 0, shards - 1)
    wanted = (
        (row == TOTAL)
        | ((row == TEAM_BEGIN) & (column < 2 * team))
        | ((row == HERE_BEGIN) & (column < here))
        | ((row >= COUNTS) & (column == near))
    )
    sums = jnp.sum(jnp.where(wanted, node_count[None, :], 0), axis=1)
    return sums + jnp.where(row[:, 0] == SIDE, side, 0)


def on_device(densities, hamiltonian, couplings, gamma, coeff, node_count):
    hier = ("team", "r")
    group = ("col", "r")
    ints = integers(node_count)
    reals = jnp.concatenate([gamma, coeff.reshape(4), jnp.sqrt(jnp.arange(ROOTS, dtype=F32))])
    near, far, inner = routes(node_count.shape[0])
    p2 = lax.ppermute(densities, hier, far)
    p1 = lax.ppermute(densities, hier, near)
    part = own_call(densities.reshape(128, 256))
    vhi, vlo, hhi, hlo = weights_call(hamiltonian, couplings)
    sent = halo_call(jnp.broadcast_to(ints[:, None], (16, 128)), p2, p1, part)
    sent, x, p1 = lax.optimization_barrier((sent, densities, p1))
    got = lax.all_to_all(sent, group, 0, 0, tiled=True)
    pair = pair_call(ints, x, p1)
    back_sent = column_call(ints, reals, got, vhi, vlo)
    back_sent, pair = lax.optimization_barrier((back_sent, pair))
    back_got = lax.all_to_all(back_sent, group, 0, 0, tiled=True)
    pair = lax.ppermute(pair, hier, inner)
    base = row_call(ints, reals, x, p1, p2, pair, vhi, vlo)
    out = finish_call(ints, back_got, base, hhi, hlo)
    return out.reshape(4, 2, 16, 256)


def solution(mesh):
    devices = mesh.devices
    inside = Mesh(devices.reshape(devices.shape[0] // 2, 2, devices.shape[1]), ("team", "r", "col"))
    spec = P(("team", "r"), None, "col", None)
    return jax.shard_map(
        on_device,
        mesh=inside,
        in_specs=(spec, P(), P(), P(), P(), P()),
        out_specs=spec,
        check_vma=False,
    )
```

```python
import jax
import jax.numpy as jnp
from jax import lax
from jax.experimental import pallas as pl
from jax.experimental.pallas import tpu as pltpu
from jax.sharding import Mesh, PartitionSpec as P

STEP = 0.2
HALF2 = 0.5 * STEP * STEP
SLOTS = 4
TOTAL, TEAM_BEGIN, HERE_BEGIN, SIDE, COUNTS, ODD = 0, 1, 2, 3, 4, 9
ROOTS = 72
BF = jnp.bfloat16
F32 = jnp.float32


def split(v):
    hi = v.astype(BF)
    return hi, (v - hi.astype(F32)).astype(BF)


def dot(a, b):
    return jnp.dot(a, b, preferred_element_type=F32)


def granules(vs):
    lane = lax.broadcasted_iota(jnp.int32, vs[0].shape, 1) // 16
    turned = [vs[0]] + [pltpu.roll(vs[k], 16 * k, 1) for k in range(1, 8)]
    cur = [turned[-k % 8] for k in range(8)]
    for bit in (1, 2, 4):
        pick = (lane & bit) != 0
        cur = [jnp.where(pick, cur[(m - bit) % 8], cur[m]) for m in range(8)]
    return [cur[0]] + [pltpu.roll(cur[m], 128 - 16 * m, 1) for m in range(1, 8)]


def once(method):
    def cached(self, p):
        key = (method.__name__, p)
        if key not in self.memo:
            self.memo[key] = method(self, p)
        return self.memo[key]

    return cached


class Nodes:
    def __init__(self, ints_ref, reals_ref, begin):
        self.memo = {}
        self.live = (ints_ref[TOTAL] >> 1) << 1
        self.begin = begin
        self.base = begin - 4
        self.reals = reals_ref
        self.gamma = (reals_ref[0], reals_ref[1])
        self.re = (reals_ref[2], reals_ref[4])
        self.im = (reals_ref[3], reals_ref[5])

    def root(self, n):
        return self.reals[jnp.clip(n, 0, ROOTS - 1) + 6]

    @once
    def up(self, p):
        g = self.base + p
        return jnp.where((g >= 0) & (g + 2 < self.live), self.root((g >> 1) + 1), 0.0)

    @once
    def down(self, p):
        g = self.base + p
        return jnp.where((g >= 2) & (g < self.live), self.root(g >> 1), 0.0)

    @once
    def middle(self, p):
        g = self.base + p
        n = (g >> 1).astype(F32)
        ok = (g >= 0) & (g < self.live)
        upper = jnp.where(ok & (g + 2 < self.live), n + 1.0, 0.0)
        return upper + jnp.where(ok & (g >= 2), n, 0.0)

    @once
    def even(self, p):
        g = self.base + p
        return jnp.where((g >= 0) & (g < self.live) & ((g & 1) == 0), 1.0, 0.0).astype(F32)

    @once
    def odd(self, p):
        g = self.base + p
        return jnp.where((g >= 0) & (g < self.live) & ((g & 1) == 1), 1.0, 0.0).astype(F32)

    @once
    def damp(self, p):
        g = self.base + p
        n0 = (g >> 1).astype(F32)
        n1 = (g & 1).astype(F32)
        return n0 * self.gamma[0] + n1 * self.gamma[1]


def scaled(s, v):
    return (s * v[0], s * v[1])


def plus(a, b):
    return (a[0] + b[0], a[1] + b[1])


def times(re, im, v):
    return (re * v[0] - im * v[1], re * v[1] + im * v[0])


def both(nodes, x, p, re, im):
    r = plus(scaled(nodes.up(p), x[p + 2]), scaled(re * nodes.down(p), x[p - 2]))
    t = scaled(im * nodes.down(p), x[p - 2])
    return (r[0] - t[1], r[1] + t[0]), (r[0] + t[1], r[1] - t[0])


def both1(nodes, x, p, re, im):
    r = plus(scaled(nodes.even(p), x[p + 1]), scaled(re * nodes.odd(p), x[p - 1]))
    t = scaled(im * nodes.odd(p), x[p - 1])
    return (r[0] - t[1], r[1] + t[0]), (r[0] + t[1], r[1] - t[0])


def first_order(nodes, x, p, re, im):
    here = nodes.damp(p)

    def w(q):
        return STEP - HALF2 * (here + nodes.damp(q))

    zero = scaled(w(p), x[p])
    up, down = scaled(w(p + 2) * nodes.up(p), x[p + 2]), scaled(w(p - 2) * nodes.down(p), x[p - 2])
    one = plus(up, times(re[0], im[0], down))
    up, down = scaled(w(p + 1) * nodes.even(p), x[p + 1]), scaled(w(p - 1) * nodes.odd(p), x[p - 1])
    two = plus(up, times(re[1], im[1], down))
    return zero, one, two


def put(hi_ref, lo_ref, block, col, j, rows, v):
    hi, lo = split(jnp.concatenate([v[0], v[1]], axis=0))
    at = pl.ds(block * 128 + j * rows, rows)
    hi_ref[at, 256 * col : 256 * col + 256] = hi
    lo_ref[at, 256 * col : 256 * col + 256] = lo


def times_weights(hi_ref, lo_ref, ghi_ref, glo_ref):
    hi, g = hi_ref[...], ghi_ref[...]
    return dot(hi, g) + dot(lo_ref[...], g) + dot(hi, glo_ref[...])


def weights_kernel(h_ref, q_ref, vhi, vlo, hhi, hlo):
    for b in range(3):
        hi, lo = split(h_ref[...] if b == 0 else q_ref[b - 1])
        vhi[256 * b : 256 * b + 256, :] = hi
        vlo[256 * b : 256 * b + 256, :] = lo
        hhi[:, 256 * b : 256 * b + 256] = hi
        hlo[:, 256 * b : 256 * b + 256] = lo


def own_kernel(x_ref, o_ref):
    o_ref[...] = x_ref[...].T.reshape(32, 8, 128)


def fetch(pairs, sem):
    copies = [pltpu.make_async_copy(source, target, sem.at[i]) for i, (source, target) in enumerate(pairs)]
    for copy in copies:
        copy.start()
    return copies


def team_counts(ints_ref):
    side = ints_ref[SIDE]
    return ints_ref[COUNTS + 2 - side], ints_ref[COUNTS + 3 - side]


def edge_kernel(ints_in, got_ref, own_ref, first_ref, last_ref, y_ref, ints_ref, sem):
    fetched = fetch([(ints_in, ints_ref)], sem)
    for place in range(2):
        vs = []
        for low in range(8):
            vs.append(jnp.concatenate([got_ref[(8 * high + low) * 2 + place] for high in range(2)], axis=0))
        for m, v in enumerate(granules(vs)):
            y_ref[SLOTS * place + m // 2, m % 2] = jnp.concatenate([v[:8], v[8:]], axis=1)
    for copy in fetched:
        copy.wait()
    own, other = team_counts(ints_ref)
    odd = ints_ref[ODD]

    def node(j):
        return y_ref[jnp.where(j < own, SLOTS * odd + j, SLOTS * (1 - odd) + jnp.minimum(j - own, SLOTS - 1))]

    for j in range(8):
        own_ref[j] = node(j)
    for j in range(4):
        first_ref[j] = own_ref[j]
        last_ref[j] = own_ref[own + other - 4 + j]


def pair_kernel(ints_ref, x_ref, near_ref, o_ref):
    o_ref[0:4] = x_ref[...]
    o_ref[4:6] = near_ref[pl.ds(jnp.where(ints_ref[SIDE] == 0, ints_ref[COUNTS + 1] - 2, 0), 2)]


def column_kernel(
    ints_in, reals_in, own_ref, below_ref, above_ref, ghi_ref, glo_ref, o_ref, y_ref, hi_ref, lo_ref, hi2_ref, lo2_ref, z_ref, send_ref, ints_ref, reals_ref, sem, out_sem
):
    fetched = fetch([(ints_in, ints_ref), (reals_in, reals_ref)], sem)
    y_ref[0:4] = below_ref[...]
    y_ref[4:12] = own_ref[...]
    y_ref[12:16] = above_ref[...]
    for copy in fetched:
        copy.wait()
    nodes = Nodes(ints_ref, reals_ref, ints_ref[TEAM_BEGIN])
    own, other = team_counts(ints_ref)
    odd = ints_ref[ODD]
    re, im = nodes.re, nodes.im
    y_ref[pl.ds(4 + own + other, 4)] = above_ref[...]
    x = []
    for p in range(16):
        v = y_ref[p]
        x.append((v[0], v[1]))
    a2, b2 = {}, {}
    for p in range(2, 14):
        a2[p], b2[p] = both1(nodes, x, p, re[1], im[1])
    for j in range(8):
        p = j + 4
        a1, b1 = both(nodes, x, p, re[0], im[0])
        a12, b1a2 = both(nodes, a2, p, re[0], im[0])
        a1b2, _ = both(nodes, b2, p, re[0], im[0])
        far = scaled(nodes.up(p) * nodes.up(p + 2), x[p + 4])
        low = scaled(nodes.down(p) * nodes.down(p - 2), x[p - 4])
        mid = nodes.middle(p)
        here = scaled(mid, x[p])
        a11 = plus(plus(far, times(re[0], im[0], here)), times(re[0] * re[0] - im[0] * im[0], 2.0 * re[0] * im[0], low))
        s11 = plus(plus(scaled(2.0, far), scaled(2.0 * re[0], here)), scaled(2.0 * (re[0] * re[0] + im[0] * im[0]), low))
        rows = (
            (x[p], a1, a2[p]),
            (a1, a11, a12),
            (a2[p], a12, times(re[1], im[1], x[p])),
            (scaled(2.0, b1), s11, scaled(2.0, b1a2)),
            (scaled(2.0, b2[p]), scaled(2.0, a1b2), scaled(2.0 * re[1], x[p])),
        )
        for block, row in enumerate(rows):
            for col, v in enumerate(row):
                put(hi_ref, lo_ref, block, col, j, 16, v)
    sums = times_weights(hi_ref, lo_ref, ghi_ref, glo_ref)
    for j in range(8):
        p = j + 4
        for block, v in enumerate(first_order(nodes, x, p, re, im)):
            s = sums[block * 128 + 16 * j : block * 128 + 16 * j + 16]
            put(hi2_ref, lo2_ref, 0, block, j, 16, (v[1] - HALF2 * s[:8], -v[0] - HALF2 * s[8:]))
        z_ref[1, j] = (2.0 * HALF2) * sums[16 * j : 16 * j + 16].reshape(2, 8, 256)
        z_ref[2, j] = HALF2 * sums[384 + 16 * j : 400 + 16 * j].reshape(2, 8, 256)
        z_ref[3, j] = HALF2 * sums[512 + 16 * j : 528 + 16 * j].reshape(2, 8, 256)

    def send(z):
        for r in range(2):
            vs = []
            for m in range(8):
                v = z_ref[z, m // 2 if r == 0 else own + m // 2, m % 2]
                vs.append(jnp.concatenate([v[:, :128], v[:, 128:]], axis=0))
            for low, v in enumerate(granules(vs)):
                for high in range(2):
                    send_ref[z, (8 * high + low) * 2 + (odd if r == 0 else 1 - odd)] = v[8 * high : 8 * high + 8]
        copy = pltpu.make_async_copy(send_ref.at[z], o_ref.at[:, 8 * z : 8 * z + 8], out_sem.at[z])
        copy.start()
        return copy

    last = times_weights(hi2_ref, lo2_ref, ghi_ref, glo_ref)
    copies = [send(z) for z in range(1, 4)]
    z_ref[0] = last.reshape(8, 2, 8, 256)
    for copy in [*copies, send(0)]:
        copy.wait()


def row_kernel(
    ints_ref, reals_ref, x_ref, p1_ref, p2_ref, pair_ref, ghi_ref, glo_ref, o_ref, w_ref, hi_ref, lo_ref, hi2_ref, lo2_ref
):
    nodes = Nodes(ints_ref, reals_ref, ints_ref[HERE_BEGIN])
    re, im = nodes.re, (-nodes.im[0], -nodes.im[1])
    up = ints_ref[SIDE]
    farther, below, own, above = (ints_ref[COUNTS + i] for i in range(4))
    w_ref[8:12] = x_ref[...]
    w_ref[pl.ds(4 + 8 * up, 4)] = p1_ref[...]
    w_ref[pl.ds(16 * up, 4)] = p2_ref[...]
    w_ref[pl.ds(12 - 8 * up, 4)] = pair_ref[0:4]
    w_ref[pl.ds(jnp.where(up == 0, 16, farther - 2), 2)] = pair_ref[4:6]

    def slot(p):
        j = p - 4
        if j < 0:
            return jnp.where(j + below >= 0, 4 + j + below, farther + j + below)
        return jnp.where(j < own, 8 + j, jnp.where(j < own + above, 12 + j - own, jnp.minimum(16 + j - own - above, 19)))

    x = []
    for p in range(12):
        v = w_ref[slot(p)]
        x.append((v[0], v[1]))
    b2 = {}
    for p in range(2, 10):
        b2[p], _ = both1(nodes, x, p, re[1], im[1])
    for j in range(4):
        p = j + 4
        b1, _ = both(nodes, x, p, re[0], im[0])
        b12, _ = both(nodes, b2, p, re[0], im[0])
        far = scaled(nodes.up(p) * nodes.up(p + 2), x[p + 4])
        low = scaled(nodes.down(p) * nodes.down(p - 2), x[p - 4])
        here = scaled(nodes.middle(p), x[p])
        b11 = plus(plus(far, times(re[0], im[0], here)), times(re[0] * re[0] - im[0] * im[0], 2.0 * re[0] * im[0], low))
        rows = ((x[p], b1, b2[p]), (b1, b11, b12), (b2[p], b12, times(re[1], im[1], x[p])))
        for block, row in enumerate(rows):
            for col, v in enumerate(row):
                put(hi_ref, lo_ref, block, col, j, 32, v)
    sums = times_weights(hi_ref, lo_ref, ghi_ref, glo_ref)
    for j in range(4):
        p = j + 4
        for block, v in enumerate(first_order(nodes, x, p, re, im)):
            s = sums[block * 128 + 32 * j : block * 128 + 32 * j + 32]
            put(hi2_ref, lo2_ref, 0, block, j, 32, (-v[1] - HALF2 * s[:16], v[0] - HALF2 * s[16:]))
    right = times_weights(hi2_ref, lo2_ref, ghi_ref, glo_ref)
    for j in range(4):
        d = nodes.damp(j + 4)
        keep = 1.0 - STEP * d + HALF2 * d * d
        old = x_ref[j].reshape(32, 256)
        live = (j < own) & (nodes.begin + j < nodes.live)
        o_ref[32 * j : 32 * j + 32, :] = jnp.where(live, keep * old + right[32 * j : 32 * j + 32], old)


def finish_kernel(ints_in, got_ref, base_ref, ghi_ref, glo_ref, o_ref, ints_ref, sem):
    fetched = fetch([(ints_in, ints_ref)], sem)
    his, los = [], []
    for z in range(1, 4):
        hi, lo = split(got_ref[:, 8 * z : 8 * z + 8, :].reshape(256, 128))
        his.append(hi)
        los.append(lo)
    hi, lo = jnp.concatenate(his, axis=0), jnp.concatenate(los, axis=0)
    g = ghi_ref[...]
    out = dot(g, hi) + dot(g, lo) + dot(glo_ref[...], hi) + got_ref[:, :8, :].reshape(256, 128)
    out = out.T
    for copy in fetched:
        copy.wait()
    own, begin, limit = ints_ref[COUNTS + 2], ints_ref[HERE_BEGIN], (ints_ref[TOTAL] >> 1) << 1
    for j in range(4):
        live = (j < own) & (begin + j < limit)
        rows = slice(32 * j, 32 * j + 32)
        o_ref[rows, :] = base_ref[rows, :] + jnp.where(live, out[rows], 0.0)


SMEM = pl.BlockSpec(memory_space=pltpu.SMEM)
VMEM = pl.BlockSpec(memory_space=pltpu.VMEM)
ANY = pl.BlockSpec(memory_space=pl.ANY)


def call(kernel, outs, specs, scratch=(), flops=1_000_000, name=None, out_specs=None, aliases=None):
    return pl.pallas_call(
        kernel,
        out_shape=outs,
        in_specs=specs,
        out_specs=out_specs or jax.tree.map(lambda _: VMEM, outs),
        input_output_aliases=aliases or {},
        scratch_shapes=list(scratch),
        compiler_params=pltpu.CompilerParams(vmem_limit_bytes=48 * 1024 * 1024),
        cost_estimate=pl.CostEstimate(flops=flops, bytes_accessed=4_000_000, transcendentals=0),
        name=name,
    )


def struct(shape, dtype=F32):
    return jax.ShapeDtypeStruct(shape, dtype)


weights_call = call(
    weights_kernel,
    (struct((768, 256), BF), struct((768, 256), BF), struct((256, 768), BF), struct((256, 768), BF)),
    [VMEM] * 2,
    name="weights",
)
own_call = call(own_kernel, struct((32, 8, 128)), [VMEM], name="own")
INTS = pltpu.SMEM((16,), jnp.int32)
edge_call = call(
    edge_kernel,
    (struct((8, 2, 8, 256)), struct((4, 2, 8, 256)), struct((4, 2, 8, 256))),
    [ANY, VMEM],
    [pltpu.VMEM((8, 2, 8, 256), F32), INTS, pltpu.SemaphoreType.DMA((1,))],
    name="edge",
)
pair_call = call(pair_kernel, struct((6, 2, 16, 256)), [SMEM] + [VMEM] * 2, name="pair")
column_call = call(
    column_kernel,
    struct((32, 32, 128)),
    [ANY] * 2 + [VMEM] * 5,
    [
        pltpu.VMEM((16, 2, 8, 256), F32),
        pltpu.VMEM((640, 768), BF),
        pltpu.VMEM((640, 768), BF),
        pltpu.VMEM((128, 768), BF),
        pltpu.VMEM((128, 768), BF),
        pltpu.VMEM((4, 8, 2, 8, 256), F32),
        pltpu.VMEM((4, 32, 8, 128), F32),
        INTS,
        pltpu.SMEM((6 + ROOTS,), F32),
        pltpu.SemaphoreType.DMA((2,)),
        pltpu.SemaphoreType.DMA((4,)),
    ],
    flops=1_000_000_000,
    out_specs=ANY,
    name="columns",
)
row_call = call(
    row_kernel,
    struct((128, 256)),
    [SMEM] * 2 + [VMEM] * 6,
    [
        pltpu.VMEM((20, 2, 16, 256), F32),
        pltpu.VMEM((384, 768), BF),
        pltpu.VMEM((384, 768), BF),
        pltpu.VMEM((128, 768), BF),
        pltpu.VMEM((128, 768), BF),
    ],
    flops=1_000_000_000,
    name="rows",
)
finish_call = call(
    finish_kernel, struct((128, 256)), [ANY] + [VMEM] * 4, [INTS, pltpu.SemaphoreType.DMA((1,))], flops=300_000_000, name="finish"
)


def routes(shards):
    pairs = [(i, i + 1) for i in range(1, shards - 1, 2)]
    near = pairs + [(b, a) for a, b in pairs]
    far = [(i, i + 2) for i in range(0, shards - 2, 2)] + [(i, i - 2) for i in range(3, shards, 2)]
    pairs = [(i, i + 1) for i in range(0, shards, 2)]
    inner = pairs + [(b, a) for a, b in pairs]
    onward = [(i, (i // 2 + 1) * 2 + 1 - i % 2) for i in range(shards - 2)]
    return near, far, inner, onward, [(b, a) for a, b in onward]


def groups(shards, columns):
    return [
        [(2 * team + (side ^ team % 2)) * columns + c for c in range(columns) for side in range(2)] for team in range(shards // 2)
    ]


def integers(node_count):
    shards = node_count.shape[0]
    team, side = lax.axis_index("team"), lax.axis_index("r")
    here = 2 * team + side
    row = jnp.arange(16, dtype=jnp.int32)[:, None]
    column = jnp.arange(shards, dtype=jnp.int32)[None, :]
    near = jnp.clip(here + row - (COUNTS + 2), 0, shards - 1)
    wanted = (
        (row == TOTAL)
        | ((row == TEAM_BEGIN) & (column < 2 * team))
        | ((row == HERE_BEGIN) & (column < here))
        | ((row >= COUNTS) & (row < ODD) & (column == near))
    )
    sums = jnp.sum(jnp.where(wanted, node_count[None, :], 0), axis=1)
    return sums + jnp.where(row[:, 0] == SIDE, side, 0) + jnp.where(row[:, 0] == ODD, team & 1, 0)


def on_device(densities, hamiltonian, couplings, gamma, coeff, node_count):
    hier = ("team", "r")
    shards = node_count.shape[0]
    everyone = ("team", "r", "col")
    lists = groups(shards, lax.axis_size("col"))
    near, far, inner, onward, backward = routes(shards)

    def exchange(v):
        return lax.all_to_all(v, everyone, 0, 0, axis_index_groups=lists, tiled=True)

    ints = integers(node_count)
    reals = jnp.concatenate([gamma, coeff.reshape(4), jnp.sqrt(jnp.arange(ROOTS, dtype=F32))])
    vhi, vlo, hhi, hlo = weights_call(hamiltonian, couplings)
    sent, x = lax.optimization_barrier((own_call(densities.reshape(128, 256)), densities))
    got = exchange(sent)
    p1 = lax.ppermute(x, hier, near)
    p2 = lax.ppermute(x, hier, far)
    own, first, last = edge_call(ints, got)
    below = lax.ppermute(last, hier, onward)
    above = lax.ppermute(first, hier, backward)
    own, p1, p2, x = lax.optimization_barrier((own, p1, p2, x))
    pair = pair_call(ints, x, p1)
    own, pair = lax.optimization_barrier((own, pair))
    back_sent = column_call(ints, reals, own, below, above, vhi, vlo)
    back_sent, pair = lax.optimization_barrier((back_sent, pair))
    back_got = exchange(back_sent)
    pair = lax.ppermute(pair, hier, inner)
    base = row_call(ints, reals, x, p1, p2, pair, vhi, vlo)
    out = finish_call(ints, back_got, base, hhi, hlo)
    return out.reshape(4, 2, 16, 256)


def solution(mesh):
    devices = mesh.devices
    inside = Mesh(devices.reshape(devices.shape[0] // 2, 2, devices.shape[1]), ("team", "r", "col"))
    spec = P(("team", "r"), None, "col", None)
    return jax.shard_map(
        on_device,
        mesh=inside,
        in_specs=(spec, P(), P(), P(), P(), P()),
        out_specs=spec,
        check_vma=False,
    )
```

```python
import jax
import jax.numpy as jnp
from jax import lax
from jax.experimental import pallas as pl
from jax.experimental.pallas import tpu as pltpu
from jax.sharding import Mesh, PartitionSpec as P

STEP = 0.2
HALF2 = 0.5 * STEP * STEP
SLOTS = 4
TOTAL, TEAM_BEGIN, HERE_BEGIN, SIDE, COUNTS, ODD = 0, 1, 2, 3, 4, 9
ROOTS = 72
BF = jnp.bfloat16
F32 = jnp.float32


def split(v):
    hi = v.astype(BF)
    return hi, (v - hi.astype(F32)).astype(BF)


def dot(a, b):
    return jnp.dot(a, b, preferred_element_type=F32)


def granules(vs):
    lane = lax.broadcasted_iota(jnp.int32, vs[0].shape, 1) // 16
    turned = [vs[0]] + [pltpu.roll(vs[k], 16 * k, 1) for k in range(1, 8)]
    cur = [turned[-k % 8] for k in range(8)]
    for bit in (1, 2, 4):
        pick = (lane & bit) != 0
        cur = [jnp.where(pick, cur[(m - bit) % 8], cur[m]) for m in range(8)]
    return [cur[0]] + [pltpu.roll(cur[m], 128 - 16 * m, 1) for m in range(1, 8)]


def once(method):
    def cached(self, p):
        key = (method.__name__, p)
        if key not in self.memo:
            self.memo[key] = method(self, p)
        return self.memo[key]

    return cached


class Nodes:
    def __init__(self, ints_ref, reals_ref, begin):
        self.memo = {}
        self.live = (ints_ref[TOTAL] >> 1) << 1
        self.begin = begin
        self.base = begin - 4
        self.reals = reals_ref
        self.gamma = (reals_ref[0], reals_ref[1])
        self.re = (reals_ref[2], reals_ref[4])
        self.im = (reals_ref[3], reals_ref[5])

    def root(self, n):
        return self.reals[jnp.clip(n, 0, ROOTS - 1) + 6]

    @once
    def up(self, p):
        g = self.base + p
        return jnp.where((g >= 0) & (g + 2 < self.live), self.root((g >> 1) + 1), 0.0)

    @once
    def down(self, p):
        g = self.base + p
        return jnp.where((g >= 2) & (g < self.live), self.root(g >> 1), 0.0)

    @once
    def middle(self, p):
        g = self.base + p
        n = (g >> 1).astype(F32)
        ok = (g >= 0) & (g < self.live)
        upper = jnp.where(ok & (g + 2 < self.live), n + 1.0, 0.0)
        return upper + jnp.where(ok & (g >= 2), n, 0.0)

    @once
    def even(self, p):
        g = self.base + p
        return jnp.where((g >= 0) & (g < self.live) & ((g & 1) == 0), 1.0, 0.0).astype(F32)

    @once
    def odd(self, p):
        g = self.base + p
        return jnp.where((g >= 0) & (g < self.live) & ((g & 1) == 1), 1.0, 0.0).astype(F32)

    @once
    def damp(self, p):
        g = self.base + p
        n0 = (g >> 1).astype(F32)
        n1 = (g & 1).astype(F32)
        return n0 * self.gamma[0] + n1 * self.gamma[1]


def scaled(s, v):
    return (s * v[0], s * v[1])


def plus(a, b):
    return (a[0] + b[0], a[1] + b[1])


def times(re, im, v):
    return (re * v[0] - im * v[1], re * v[1] + im * v[0])


def both(nodes, x, p, re, im):
    r = plus(scaled(nodes.up(p), x[p + 2]), scaled(re * nodes.down(p), x[p - 2]))
    t = scaled(im * nodes.down(p), x[p - 2])
    return (r[0] - t[1], r[1] + t[0]), (r[0] + t[1], r[1] - t[0])


def both1(nodes, x, p, re, im):
    r = plus(scaled(nodes.even(p), x[p + 1]), scaled(re * nodes.odd(p), x[p - 1]))
    t = scaled(im * nodes.odd(p), x[p - 1])
    return (r[0] - t[1], r[1] + t[0]), (r[0] + t[1], r[1] - t[0])


def first_order(nodes, x, p, re, im):
    here = nodes.damp(p)

    def w(q):
        return STEP - HALF2 * (here + nodes.damp(q))

    zero = scaled(w(p), x[p])
    up, down = scaled(w(p + 2) * nodes.up(p), x[p + 2]), scaled(w(p - 2) * nodes.down(p), x[p - 2])
    one = plus(up, times(re[0], im[0], down))
    up, down = scaled(w(p + 1) * nodes.even(p), x[p + 1]), scaled(w(p - 1) * nodes.odd(p), x[p - 1])
    two = plus(up, times(re[1], im[1], down))
    return zero, one, two


def put(hi_ref, lo_ref, block, col, j, rows, v):
    hi, lo = split(jnp.concatenate([v[0], v[1]], axis=0))
    at = pl.ds(block * 128 + j * rows, rows)
    hi_ref[at, 256 * col : 256 * col + 256] = hi
    lo_ref[at, 256 * col : 256 * col + 256] = lo


def times_weights(hi_ref, lo_ref, ghi_ref, glo_ref):
    hi, g = hi_ref[...], ghi_ref[...]
    return dot(hi, g) + dot(lo_ref[...], g) + dot(hi, glo_ref[...])


def weights_kernel(h_ref, q_ref, vhi, vlo, hhi, hlo):
    for b in range(3):
        hi, lo = split(h_ref[...] if b == 0 else q_ref[b - 1])
        vhi[256 * b : 256 * b + 256, :] = hi
        vlo[256 * b : 256 * b + 256, :] = lo
        hhi[:, 256 * b : 256 * b + 256] = hi
        hlo[:, 256 * b : 256 * b + 256] = lo


def own_kernel(x_ref, o_ref):
    o_ref[...] = x_ref[...].T.reshape(32, 8, 128)


def fetch(pairs, sem):
    copies = [pltpu.make_async_copy(source, target, sem.at[i]) for i, (source, target) in enumerate(pairs)]
    for copy in copies:
        copy.start()
    return copies


def team_counts(ints_ref):
    side = ints_ref[SIDE]
    return ints_ref[COUNTS + 2 - side], ints_ref[COUNTS + 3 - side]


def edge_kernel(ints_in, got_ref, own_ref, first_ref, last_ref, y_ref, ints_ref, sem):
    fetched = fetch([(ints_in, ints_ref)], sem)
    for place in range(2):
        vs = []
        for low in range(8):
            vs.append(jnp.concatenate([got_ref[(8 * high + low) * 2 + place] for high in range(2)], axis=0))
        for m, v in enumerate(granules(vs)):
            y_ref[SLOTS * place + m // 2, m % 2] = jnp.concatenate([v[:8], v[8:]], axis=1)
    for copy in fetched:
        copy.wait()
    own, other = team_counts(ints_ref)
    odd = ints_ref[ODD]

    def node(j):
        return y_ref[jnp.where(j < own, SLOTS * odd + j, SLOTS * (1 - odd) + jnp.minimum(j - own, SLOTS - 1))]

    for j in range(8):
        own_ref[j] = node(j)
    for j in range(4):
        first_ref[j] = own_ref[j]
        last_ref[j] = own_ref[own + other - 4 + j]


def pair_kernel(ints_ref, x_ref, near_ref, o_ref, far_ref):
    far_ref[...] = x_ref[pl.ds(jnp.where(ints_ref[SIDE] == 0, ints_ref[COUNTS + 2] - 2, 0), 2)]
    o_ref[0:4] = x_ref[...]
    o_ref[4:6] = near_ref[pl.ds(jnp.where(ints_ref[SIDE] == 0, ints_ref[COUNTS + 1] - 2, 0), 2)]


def column_kernel(
    ints_in, reals_in, own_ref, below_ref, above_ref, ghi_ref, glo_ref, o_ref, y_ref, hi_ref, lo_ref, hi2_ref, lo2_ref, z_ref, send_ref, ints_ref, reals_ref, sem, out_sem
):
    fetched = fetch([(ints_in, ints_ref), (reals_in, reals_ref)], sem)
    y_ref[0:4] = below_ref[...]
    y_ref[4:12] = own_ref[...]
    y_ref[12:16] = above_ref[...]
    for copy in fetched:
        copy.wait()
    nodes = Nodes(ints_ref, reals_ref, ints_ref[TEAM_BEGIN])
    own, other = team_counts(ints_ref)
    odd = ints_ref[ODD]
    re, im = nodes.re, nodes.im
    y_ref[pl.ds(4 + own + other, 4)] = above_ref[...]
    x = []
    for p in range(16):
        v = y_ref[p]
        x.append((v[0], v[1]))
    a2, b2 = {}, {}
    for p in range(2, 14):
        a2[p], b2[p] = both1(nodes, x, p, re[1], im[1])
    for j in range(8):
        p = j + 4
        a1, b1 = both(nodes, x, p, re[0], im[0])
        a12, b1a2 = both(nodes, a2, p, re[0], im[0])
        a1b2, _ = both(nodes, b2, p, re[0], im[0])
        far = scaled(nodes.up(p) * nodes.up(p + 2), x[p + 4])
        low = scaled(nodes.down(p) * nodes.down(p - 2), x[p - 4])
        mid = nodes.middle(p)
        here = scaled(mid, x[p])
        a11 = plus(plus(far, times(re[0], im[0], here)), times(re[0] * re[0] - im[0] * im[0], 2.0 * re[0] * im[0], low))
        s11 = plus(plus(scaled(2.0, far), scaled(2.0 * re[0], here)), scaled(2.0 * (re[0] * re[0] + im[0] * im[0]), low))
        rows = (
            (x[p], a1, a2[p]),
            (a1, a11, a12),
            (a2[p], a12, times(re[1], im[1], x[p])),
            (scaled(2.0, b1), s11, scaled(2.0, b1a2)),
            (scaled(2.0, b2[p]), scaled(2.0, a1b2), scaled(2.0 * re[1], x[p])),
        )
        for block, row in enumerate(rows):
            for col, v in enumerate(row):
                put(hi_ref, lo_ref, block, col, j, 16, v)
    sums = times_weights(hi_ref, lo_ref, ghi_ref, glo_ref)
    for j in range(8):
        p = j + 4
        for block, v in enumerate(first_order(nodes, x, p, re, im)):
            s = sums[block * 128 + 16 * j : block * 128 + 16 * j + 16]
            put(hi2_ref, lo2_ref, 0, block, j, 16, (v[1] - HALF2 * s[:8], -v[0] - HALF2 * s[8:]))
        z_ref[1, j] = (2.0 * HALF2) * sums[16 * j : 16 * j + 16].reshape(2, 8, 256)
        z_ref[2, j] = HALF2 * sums[384 + 16 * j : 400 + 16 * j].reshape(2, 8, 256)
        z_ref[3, j] = HALF2 * sums[512 + 16 * j : 528 + 16 * j].reshape(2, 8, 256)

    def send(z):
        for r in range(2):
            vs = []
            for m in range(8):
                v = z_ref[z, m // 2 if r == 0 else own + m // 2, m % 2]
                vs.append(jnp.concatenate([v[:, :128], v[:, 128:]], axis=0))
            for low, v in enumerate(granules(vs)):
                for high in range(2):
                    send_ref[z, (8 * high + low) * 2 + (odd if r == 0 else 1 - odd)] = v[8 * high : 8 * high + 8]
        copy = pltpu.make_async_copy(send_ref.at[z], o_ref.at[:, 8 * z : 8 * z + 8], out_sem.at[z])
        copy.start()
        return copy

    last = times_weights(hi2_ref, lo2_ref, ghi_ref, glo_ref)
    copies = [send(z) for z in range(1, 4)]
    z_ref[0] = last.reshape(8, 2, 8, 256)
    for copy in [*copies, send(0)]:
        copy.wait()


def row_kernel(
    ints_ref, reals_ref, x_ref, p1_ref, p2_ref, pair_ref, ghi_ref, glo_ref, o_ref, w_ref, hi_ref, lo_ref, hi2_ref, lo2_ref
):
    nodes = Nodes(ints_ref, reals_ref, ints_ref[HERE_BEGIN])
    re, im = nodes.re, (-nodes.im[0], -nodes.im[1])
    up = ints_ref[SIDE]
    farther, below, own, above = (ints_ref[COUNTS + i] for i in range(4))
    w_ref[8:12] = x_ref[...]
    w_ref[pl.ds(4 + 8 * up, 4)] = p1_ref[...]
    w_ref[pl.ds(jnp.where(up == 0, farther - 2, 16), 2)] = p2_ref[...]
    w_ref[pl.ds(12 - 8 * up, 4)] = pair_ref[0:4]
    w_ref[pl.ds(jnp.where(up == 0, 16, farther - 2), 2)] = pair_ref[4:6]

    def slot(p):
        j = p - 4
        if j < 0:
            return jnp.where(j + below >= 0, 4 + j + below, farther + j + below)
        return jnp.where(j < own, 8 + j, jnp.where(j < own + above, 12 + j - own, jnp.minimum(16 + j - own - above, 19)))

    x = []
    for p in range(12):
        v = w_ref[slot(p)]
        x.append((v[0], v[1]))
    b2 = {}
    for p in range(2, 10):
        b2[p], _ = both1(nodes, x, p, re[1], im[1])
    for j in range(4):
        p = j + 4
        b1, _ = both(nodes, x, p, re[0], im[0])
        b12, _ = both(nodes, b2, p, re[0], im[0])
        far = scaled(nodes.up(p) * nodes.up(p + 2), x[p + 4])
        low = scaled(nodes.down(p) * nodes.down(p - 2), x[p - 4])
        here = scaled(nodes.middle(p), x[p])
        b11 = plus(plus(far, times(re[0], im[0], here)), times(re[0] * re[0] - im[0] * im[0], 2.0 * re[0] * im[0], low))
        rows = ((x[p], b1, b2[p]), (b1, b11, b12), (b2[p], b12, times(re[1], im[1], x[p])))
        for block, row in enumerate(rows):
            for col, v in enumerate(row):
                put(hi_ref, lo_ref, block, col, j, 32, v)
    sums = times_weights(hi_ref, lo_ref, ghi_ref, glo_ref)
    for j in range(4):
        p = j + 4
        for block, v in enumerate(first_order(nodes, x, p, re, im)):
            s = sums[block * 128 + 32 * j : block * 128 + 32 * j + 32]
            put(hi2_ref, lo2_ref, 0, block, j, 32, (-v[1] - HALF2 * s[:16], v[0] - HALF2 * s[16:]))
    right = times_weights(hi2_ref, lo2_ref, ghi_ref, glo_ref)
    for j in range(4):
        d = nodes.damp(j + 4)
        keep = 1.0 - STEP * d + HALF2 * d * d
        old = x_ref[j].reshape(32, 256)
        live = (j < own) & (nodes.begin + j < nodes.live)
        o_ref[32 * j : 32 * j + 32, :] = jnp.where(live, keep * old + right[32 * j : 32 * j + 32], old)


def finish_kernel(ints_in, got_ref, base_ref, ghi_ref, glo_ref, o_ref, ints_ref, sem):
    fetched = fetch([(ints_in, ints_ref)], sem)
    his, los = [], []
    for z in range(1, 4):
        hi, lo = split(got_ref[:, 8 * z : 8 * z + 8, :].reshape(256, 128))
        his.append(hi)
        los.append(lo)
    hi, lo = jnp.concatenate(his, axis=0), jnp.concatenate(los, axis=0)
    g = ghi_ref[...]
    out = dot(g, hi) + dot(g, lo) + dot(glo_ref[...], hi) + got_ref[:, :8, :].reshape(256, 128)
    out = out.T
    for copy in fetched:
        copy.wait()
    own, begin, limit = ints_ref[COUNTS + 2], ints_ref[HERE_BEGIN], (ints_ref[TOTAL] >> 1) << 1
    for j in range(4):
        live = (j < own) & (begin + j < limit)
        rows = slice(32 * j, 32 * j + 32)
        o_ref[rows, :] = base_ref[rows, :] + jnp.where(live, out[rows], 0.0)


SMEM = pl.BlockSpec(memory_space=pltpu.SMEM)
VMEM = pl.BlockSpec(memory_space=pltpu.VMEM)
ANY = pl.BlockSpec(memory_space=pl.ANY)


def call(kernel, outs, specs, scratch=(), flops=1_000_000, name=None, out_specs=None, aliases=None):
    return pl.pallas_call(
        kernel,
        out_shape=outs,
        in_specs=specs,
        out_specs=out_specs or jax.tree.map(lambda _: VMEM, outs),
        input_output_aliases=aliases or {},
        scratch_shapes=list(scratch),
        compiler_params=pltpu.CompilerParams(vmem_limit_bytes=48 * 1024 * 1024),
        cost_estimate=pl.CostEstimate(flops=flops, bytes_accessed=4_000_000, transcendentals=0),
        name=name,
    )


def struct(shape, dtype=F32):
    return jax.ShapeDtypeStruct(shape, dtype)


weights_call = call(
    weights_kernel,
    (struct((768, 256), BF), struct((768, 256), BF), struct((256, 768), BF), struct((256, 768), BF)),
    [VMEM] * 2,
    name="weights",
)
own_call = call(own_kernel, struct((32, 8, 128)), [VMEM], name="own")
INTS = pltpu.SMEM((16,), jnp.int32)
edge_call = call(
    edge_kernel,
    (struct((8, 2, 8, 256)), struct((4, 2, 8, 256)), struct((4, 2, 8, 256))),
    [ANY, VMEM],
    [pltpu.VMEM((8, 2, 8, 256), F32), INTS, pltpu.SemaphoreType.DMA((1,))],
    name="edge",
)
pair_call = call(pair_kernel, (struct((6, 2, 16, 256)), struct((2, 2, 16, 256))), [SMEM] + [VMEM] * 2, name="pair")
column_call = call(
    column_kernel,
    struct((32, 32, 128)),
    [ANY] * 2 + [VMEM] * 5,
    [
        pltpu.VMEM((16, 2, 8, 256), F32),
        pltpu.VMEM((640, 768), BF),
        pltpu.VMEM((640, 768), BF),
        pltpu.VMEM((128, 768), BF),
        pltpu.VMEM((128, 768), BF),
        pltpu.VMEM((4, 8, 2, 8, 256), F32),
        pltpu.VMEM((4, 32, 8, 128), F32),
        INTS,
        pltpu.SMEM((6 + ROOTS,), F32),
        pltpu.SemaphoreType.DMA((2,)),
        pltpu.SemaphoreType.DMA((4,)),
    ],
    flops=1_000_000_000,
    out_specs=ANY,
    name="columns",
)
row_call = call(
    row_kernel,
    struct((128, 256)),
    [SMEM] * 2 + [VMEM] * 6,
    [
        pltpu.VMEM((20, 2, 16, 256), F32),
        pltpu.VMEM((384, 768), BF),
        pltpu.VMEM((384, 768), BF),
        pltpu.VMEM((128, 768), BF),
        pltpu.VMEM((128, 768), BF),
    ],
    flops=1_000_000_000,
    name="rows",
)
finish_call = call(
    finish_kernel, struct((128, 256)), [ANY] + [VMEM] * 4, [INTS, pltpu.SemaphoreType.DMA((1,))], flops=300_000_000, name="finish"
)


def routes(shards):
    pairs = [(i, i + 1) for i in range(1, shards - 1, 2)]
    near = pairs + [(b, a) for a, b in pairs]
    far = [(i, i + 2) for i in range(0, shards - 2, 2)] + [(i, i - 2) for i in range(3, shards, 2)]
    pairs = [(i, i + 1) for i in range(0, shards, 2)]
    inner = pairs + [(b, a) for a, b in pairs]
    onward = [(i, (i // 2 + 1) * 2 + 1 - i % 2) for i in range(shards - 2)]
    return near, far, inner, onward, [(b, a) for a, b in onward]


def groups(shards, columns):
    return [
        [(2 * team + (side ^ team % 2)) * columns + c for c in range(columns) for side in range(2)] for team in range(shards // 2)
    ]


def integers(node_count):
    shards = node_count.shape[0]
    team, side = lax.axis_index("team"), lax.axis_index("r")
    here = 2 * team + side
    row = jnp.arange(16, dtype=jnp.int32)[:, None]
    column = jnp.arange(shards, dtype=jnp.int32)[None, :]
    near = jnp.clip(here + row - (COUNTS + 2), 0, shards - 1)
    wanted = (
        (row == TOTAL)
        | ((row == TEAM_BEGIN) & (column < 2 * team))
        | ((row == HERE_BEGIN) & (column < here))
        | ((row >= COUNTS) & (row < ODD) & (column == near))
    )
    sums = jnp.sum(jnp.where(wanted, node_count[None, :], 0), axis=1)
    return sums + jnp.where(row[:, 0] == SIDE, side, 0) + jnp.where(row[:, 0] == ODD, team & 1, 0)


def on_device(densities, hamiltonian, couplings, gamma, coeff, node_count):
    hier = ("team", "r")
    shards = node_count.shape[0]
    everyone = ("team", "r", "col")
    lists = groups(shards, lax.axis_size("col"))
    near, far, inner, onward, backward = routes(shards)

    def exchange(v):
        return lax.all_to_all(v, everyone, 0, 0, axis_index_groups=lists, tiled=True)

    ints = integers(node_count)
    reals = jnp.concatenate([gamma, coeff.reshape(4), jnp.sqrt(jnp.arange(ROOTS, dtype=F32))])
    vhi, vlo, hhi, hlo = weights_call(hamiltonian, couplings)
    sent, x = lax.optimization_barrier((own_call(densities.reshape(128, 256)), densities))
    got = exchange(sent)
    p1 = lax.ppermute(x, hier, near)
    own, first, last = edge_call(ints, got)
    below = lax.ppermute(last, hier, onward)
    above = lax.ppermute(first, hier, backward)
    own, p1, x = lax.optimization_barrier((own, p1, x))
    pair, edge = pair_call(ints, x, p1)
    own, pair, edge = lax.optimization_barrier((own, pair, edge))
    back_sent = column_call(ints, reals, own, below, above, vhi, vlo)
    back_sent, pair, edge = lax.optimization_barrier((back_sent, pair, edge))
    back_got = exchange(back_sent)
    p2 = lax.ppermute(edge, hier, far)
    pair = lax.ppermute(pair, hier, inner)
    base = row_call(ints, reals, x, p1, p2, pair, vhi, vlo)
    out = finish_call(ints, back_got, base, hhi, hlo)
    return out.reshape(4, 2, 16, 256)


def solution(mesh):
    devices = mesh.devices
    inside = Mesh(devices.reshape(devices.shape[0] // 2, 2, devices.shape[1]), ("team", "r", "col"))
    spec = P(("team", "r"), None, "col", None)
    return jax.shard_map(
        on_device,
        mesh=inside,
        in_specs=(spec, P(), P(), P(), P(), P()),
        out_specs=spec,
        check_vma=False,
    )
```

```python
import jax
import jax.numpy as jnp
from jax import lax
from jax.experimental import pallas as pl
from jax.experimental.pallas import tpu as pltpu
from jax.sharding import Mesh, PartitionSpec as P

STEP = 0.2
HALF2 = 0.5 * STEP * STEP
SLOTS = 4
TOTAL, TEAM_BEGIN, HERE_BEGIN, SIDE, COUNTS, ODD = 0, 1, 2, 3, 4, 9
ROOTS = 72
BF = jnp.bfloat16
F32 = jnp.float32


def split(v):
    hi = v.astype(BF)
    return hi, (v - hi.astype(F32)).astype(BF)


def dot(a, b):
    return jnp.dot(a, b, preferred_element_type=F32)


def granules(vs):
    lane = lax.broadcasted_iota(jnp.int32, vs[0].shape, 1) // 16
    turned = [vs[0]] + [pltpu.roll(vs[k], 16 * k, 1) for k in range(1, 8)]
    cur = [turned[-k % 8] for k in range(8)]
    for bit in (1, 2, 4):
        pick = (lane & bit) != 0
        cur = [jnp.where(pick, cur[(m - bit) % 8], cur[m]) for m in range(8)]
    return [cur[0]] + [pltpu.roll(cur[m], 128 - 16 * m, 1) for m in range(1, 8)]


def once(method):
    def cached(self, p):
        key = (method.__name__, p)
        if key not in self.memo:
            self.memo[key] = method(self, p)
        return self.memo[key]

    return cached


class Nodes:
    def __init__(self, total, begin, reals, root):
        self.memo = {}
        self.live = (total >> 1) << 1
        self.begin = begin
        self.base = begin - 4
        self.gamma = (reals[0], reals[1])
        self.re = (reals[2], reals[4])
        self.im = (reals[3], reals[5])
        self.root = root

    @once
    def up(self, p):
        g = self.base + p
        return self.root((g >> 1) + 1) * jnp.where((g >= 0) & (g + 2 < self.live), 1.0, 0.0)

    @once
    def down(self, p):
        g = self.base + p
        return self.root(g >> 1) * jnp.where((g >= 2) & (g < self.live), 1.0, 0.0)

    @once
    def middle(self, p):
        g = self.base + p
        n = (g >> 1).astype(F32)
        ok = (g >= 0) & (g < self.live)
        upper = jnp.where(ok & (g + 2 < self.live), n + 1.0, 0.0)
        return upper + jnp.where(ok & (g >= 2), n, 0.0)

    @once
    def even(self, p):
        g = self.base + p
        return jnp.where((g >= 0) & (g < self.live) & ((g & 1) == 0), 1.0, 0.0).astype(F32)

    @once
    def odd(self, p):
        g = self.base + p
        return jnp.where((g >= 0) & (g < self.live) & ((g & 1) == 1), 1.0, 0.0).astype(F32)

    @once
    def damp(self, p):
        g = self.base + p
        n0 = (g >> 1).astype(F32)
        n1 = (g & 1).astype(F32)
        return n0 * self.gamma[0] + n1 * self.gamma[1]


def scaled(s, v):
    return (s * v[0], s * v[1])


def plus(a, b):
    return (a[0] + b[0], a[1] + b[1])


def times(re, im, v):
    return (re * v[0] - im * v[1], re * v[1] + im * v[0])


def both(nodes, x, p, re, im):
    r = plus(scaled(nodes.up(p), x[p + 2]), scaled(re * nodes.down(p), x[p - 2]))
    t = scaled(im * nodes.down(p), x[p - 2])
    return (r[0] - t[1], r[1] + t[0]), (r[0] + t[1], r[1] - t[0])


def both1(nodes, x, p, re, im):
    r = plus(scaled(nodes.even(p), x[p + 1]), scaled(re * nodes.odd(p), x[p - 1]))
    t = scaled(im * nodes.odd(p), x[p - 1])
    return (r[0] - t[1], r[1] + t[0]), (r[0] + t[1], r[1] - t[0])


def first_order(nodes, x, p, re, im):
    here = nodes.damp(p)

    def w(q):
        return STEP - HALF2 * (here + nodes.damp(q))

    zero = scaled(w(p), x[p])
    up, down = scaled(w(p + 2) * nodes.up(p), x[p + 2]), scaled(w(p - 2) * nodes.down(p), x[p - 2])
    one = plus(up, times(re[0], im[0], down))
    up, down = scaled(w(p + 1) * nodes.even(p), x[p + 1]), scaled(w(p - 1) * nodes.odd(p), x[p - 1])
    two = plus(up, times(re[1], im[1], down))
    return zero, one, two


def put(hi_ref, lo_ref, block, col, j, rows, v):
    hi, lo = split(jnp.concatenate([v[0], v[1]], axis=0))
    at = pl.ds(block * 128 + j * rows, rows)
    hi_ref[at, 256 * col : 256 * col + 256] = hi
    lo_ref[at, 256 * col : 256 * col + 256] = lo


def times_weights(hi_ref, lo_ref, ghi_ref, glo_ref):
    hi, g = hi_ref[...], ghi_ref[...]
    return dot(hi, g) + dot(lo_ref[...], g) + dot(hi, glo_ref[...])


def weights_kernel(h_ref, q_ref, vhi, vlo, hhi, hlo):
    for b in range(3):
        hi, lo = split(h_ref[...] if b == 0 else q_ref[b - 1])
        vhi[256 * b : 256 * b + 256, :] = hi
        vlo[256 * b : 256 * b + 256, :] = lo
        hhi[:, 256 * b : 256 * b + 256] = hi
        hlo[:, 256 * b : 256 * b + 256] = lo


def own_kernel(x_ref, o_ref):
    o_ref[...] = x_ref[...].T.reshape(32, 8, 128)


def fetch(pairs, sem):
    copies = [pltpu.make_async_copy(source, target, sem.at[i]) for i, (source, target) in enumerate(pairs)]
    for copy in copies:
        copy.start()
    return copies


def team_counts(ints_ref):
    side = ints_ref[SIDE]
    return ints_ref[COUNTS + 2 - side], ints_ref[COUNTS + 3 - side]


def edge_kernel(ints_in, got_ref, own_ref, first_ref, last_ref, y_ref, ints_ref, sem):
    fetched = fetch([(ints_in, ints_ref)], sem)
    for place in range(2):
        vs = []
        for low in range(8):
            vs.append(jnp.concatenate([got_ref[(8 * high + low) * 2 + place] for high in range(2)], axis=0))
        for m, v in enumerate(granules(vs)):
            y_ref[SLOTS * place + m // 2, m % 2] = jnp.concatenate([v[:8], v[8:]], axis=1)
    for copy in fetched:
        copy.wait()
    own, other = team_counts(ints_ref)
    odd = ints_ref[ODD]

    def node(j):
        return y_ref[jnp.where(j < own, SLOTS * odd + j, SLOTS * (1 - odd) + jnp.minimum(j - own, SLOTS - 1))]

    for j in range(8):
        own_ref[j] = node(j)
    for j in range(4):
        first_ref[j] = own_ref[j]
        last_ref[j] = own_ref[own + other - 4 + j]


def pair_kernel(ints_ref, x_ref, near_ref, o_ref, far_ref):
    far_ref[...] = x_ref[pl.ds(jnp.where(ints_ref[SIDE] == 0, ints_ref[COUNTS + 2] - 2, 0), 2)]
    o_ref[0:4] = x_ref[...]
    o_ref[4:6] = near_ref[pl.ds(jnp.where(ints_ref[SIDE] == 0, ints_ref[COUNTS + 1] - 2, 0), 2)]


def column_kernel(
    wide_ref, reals_ref, own_ref, below_ref, above_ref, ghi_ref, glo_ref, o_ref, y_ref, hi_ref, lo_ref, hi2_ref, lo2_ref, z_ref, send_ref, out_sem
):
    total, begin, side, before, here, after, odd = (
        wide_ref[i : i + 1, 0:1][0, 0] for i in (TOTAL, TEAM_BEGIN, SIDE, COUNTS + 1, COUNTS + 2, COUNTS + 3, ODD)
    )
    reals = [reals_ref[i : i + 1, 0:1][0, 0] for i in range(6)]
    own, other = jnp.where(side == 0, here, before), jnp.where(side == 0, after, here)

    def root(n):
        return jnp.sqrt(jnp.full((8, 256), jnp.maximum(n, 0).astype(F32)))

    nodes = Nodes(total, begin, reals, root)
    re, im = nodes.re, nodes.im
    y_ref[0:4] = below_ref[...]
    y_ref[4:12] = own_ref[...]
    y_ref[12:16] = above_ref[...]
    y_ref[pl.ds(4 + own + other, 4)] = above_ref[...]
    x = []
    for p in range(16):
        v = y_ref[p]
        x.append((v[0], v[1]))
    a2, b2 = {}, {}
    for p in range(2, 14):
        a2[p], b2[p] = both1(nodes, x, p, re[1], im[1])
    for j in range(8):
        p = j + 4
        a1, b1 = both(nodes, x, p, re[0], im[0])
        a12, b1a2 = both(nodes, a2, p, re[0], im[0])
        a1b2, _ = both(nodes, b2, p, re[0], im[0])
        far = scaled(nodes.up(p) * nodes.up(p + 2), x[p + 4])
        low = scaled(nodes.down(p) * nodes.down(p - 2), x[p - 4])
        mid = nodes.middle(p)
        here = scaled(mid, x[p])
        a11 = plus(plus(far, times(re[0], im[0], here)), times(re[0] * re[0] - im[0] * im[0], 2.0 * re[0] * im[0], low))
        s11 = plus(plus(scaled(2.0, far), scaled(2.0 * re[0], here)), scaled(2.0 * (re[0] * re[0] + im[0] * im[0]), low))
        rows = (
            (x[p], a1, a2[p]),
            (a1, a11, a12),
            (a2[p], a12, times(re[1], im[1], x[p])),
            (scaled(2.0, b1), s11, scaled(2.0, b1a2)),
            (scaled(2.0, b2[p]), scaled(2.0, a1b2), scaled(2.0 * re[1], x[p])),
        )
        for block, row in enumerate(rows):
            for col, v in enumerate(row):
                put(hi_ref, lo_ref, block, col, j, 16, v)
    sums = times_weights(hi_ref, lo_ref, ghi_ref, glo_ref)
    for j in range(8):
        p = j + 4
        for block, v in enumerate(first_order(nodes, x, p, re, im)):
            s = sums[block * 128 + 16 * j : block * 128 + 16 * j + 16]
            put(hi2_ref, lo2_ref, 0, block, j, 16, (v[1] - HALF2 * s[:8], -v[0] - HALF2 * s[8:]))
        z_ref[1, j] = (2.0 * HALF2) * sums[16 * j : 16 * j + 16].reshape(2, 8, 256)
        z_ref[2, j] = HALF2 * sums[384 + 16 * j : 400 + 16 * j].reshape(2, 8, 256)
        z_ref[3, j] = HALF2 * sums[512 + 16 * j : 528 + 16 * j].reshape(2, 8, 256)

    def send(z):
        for r in range(2):
            vs = []
            for m in range(8):
                v = z_ref[z, m // 2 if r == 0 else own + m // 2, m % 2]
                vs.append(jnp.concatenate([v[:, :128], v[:, 128:]], axis=0))
            for low, v in enumerate(granules(vs)):
                for high in range(2):
                    send_ref[z, (8 * high + low) * 2 + (odd if r == 0 else 1 - odd)] = v[8 * high : 8 * high + 8]
        copy = pltpu.make_async_copy(send_ref.at[z], o_ref.at[:, 8 * z : 8 * z + 8], out_sem.at[z])
        copy.start()
        return copy

    last = times_weights(hi2_ref, lo2_ref, ghi_ref, glo_ref)
    copies = [send(z) for z in range(1, 4)]
    z_ref[0] = last.reshape(8, 2, 8, 256)
    for copy in [*copies, send(0)]:
        copy.wait()


def row_kernel(
    ints_ref, reals_ref, x_ref, p1_ref, p2_ref, pair_ref, ghi_ref, glo_ref, o_ref, w_ref, hi_ref, lo_ref, hi2_ref, lo2_ref
):

    def root(n):
        return reals_ref[jnp.clip(n, 0, ROOTS - 1) + 6]

    nodes = Nodes(ints_ref[TOTAL], ints_ref[HERE_BEGIN], [reals_ref[i] for i in range(6)], root)
    re, im = nodes.re, (-nodes.im[0], -nodes.im[1])
    up = ints_ref[SIDE]
    farther, below, own, above = (ints_ref[COUNTS + i] for i in range(4))
    w_ref[8:12] = x_ref[...]
    w_ref[pl.ds(4 + 8 * up, 4)] = p1_ref[...]
    w_ref[pl.ds(jnp.where(up == 0, farther - 2, 16), 2)] = p2_ref[...]
    w_ref[pl.ds(12 - 8 * up, 4)] = pair_ref[0:4]
    w_ref[pl.ds(jnp.where(up == 0, 16, farther - 2), 2)] = pair_ref[4:6]

    def slot(p):
        j = p - 4
        if j < 0:
            return jnp.where(j + below >= 0, 4 + j + below, farther + j + below)
        return jnp.where(j < own, 8 + j, jnp.where(j < own + above, 12 + j - own, jnp.minimum(16 + j - own - above, 19)))

    x = []
    for p in range(12):
        v = w_ref[slot(p)]
        x.append((v[0], v[1]))
    b2 = {}
    for p in range(2, 10):
        b2[p], _ = both1(nodes, x, p, re[1], im[1])
    for j in range(4):
        p = j + 4
        b1, _ = both(nodes, x, p, re[0], im[0])
        b12, _ = both(nodes, b2, p, re[0], im[0])
        far = scaled(nodes.up(p) * nodes.up(p + 2), x[p + 4])
        low = scaled(nodes.down(p) * nodes.down(p - 2), x[p - 4])
        here = scaled(nodes.middle(p), x[p])
        b11 = plus(plus(far, times(re[0], im[0], here)), times(re[0] * re[0] - im[0] * im[0], 2.0 * re[0] * im[0], low))
        rows = ((x[p], b1, b2[p]), (b1, b11, b12), (b2[p], b12, times(re[1], im[1], x[p])))
        for block, row in enumerate(rows):
            for col, v in enumerate(row):
                put(hi_ref, lo_ref, block, col, j, 32, v)
    sums = times_weights(hi_ref, lo_ref, ghi_ref, glo_ref)
    for j in range(4):
        p = j + 4
        for block, v in enumerate(first_order(nodes, x, p, re, im)):
            s = sums[block * 128 + 32 * j : block * 128 + 32 * j + 32]
            put(hi2_ref, lo2_ref, 0, block, j, 32, (-v[1] - HALF2 * s[:16], v[0] - HALF2 * s[16:]))
    right = times_weights(hi2_ref, lo2_ref, ghi_ref, glo_ref)
    for j in range(4):
        d = nodes.damp(j + 4)
        keep = 1.0 - STEP * d + HALF2 * d * d
        old = x_ref[j].reshape(32, 256)
        live = (j < own) & (nodes.begin + j < nodes.live)
        o_ref[32 * j : 32 * j + 32, :] = jnp.where(live, keep * old + right[32 * j : 32 * j + 32], old)


def finish_kernel(ints_in, got_ref, base_ref, ghi_ref, glo_ref, o_ref, ints_ref, sem):
    fetched = fetch([(ints_in, ints_ref)], sem)
    his, los = [], []
    for z in range(1, 4):
        hi, lo = split(got_ref[:, 8 * z : 8 * z + 8, :].reshape(256, 128))
        his.append(hi)
        los.append(lo)
    hi, lo = jnp.concatenate(his, axis=0), jnp.concatenate(los, axis=0)
    g = ghi_ref[...]
    out = dot(g, hi) + dot(g, lo) + dot(glo_ref[...], hi) + got_ref[:, :8, :].reshape(256, 128)
    out = out.T
    for copy in fetched:
        copy.wait()
    own, begin, limit = ints_ref[COUNTS + 2], ints_ref[HERE_BEGIN], (ints_ref[TOTAL] >> 1) << 1
    for j in range(4):
        live = (j < own) & (begin + j < limit)
        rows = slice(32 * j, 32 * j + 32)
        o_ref[rows, :] = base_ref[rows, :] + jnp.where(live, out[rows], 0.0)


SMEM = pl.BlockSpec(memory_space=pltpu.SMEM)
VMEM = pl.BlockSpec(memory_space=pltpu.VMEM)
ANY = pl.BlockSpec(memory_space=pl.ANY)


def call(kernel, outs, specs, scratch=(), flops=1_000_000, name=None, out_specs=None, aliases=None):
    return pl.pallas_call(
        kernel,
        out_shape=outs,
        in_specs=specs,
        out_specs=out_specs or jax.tree.map(lambda _: VMEM, outs),
        input_output_aliases=aliases or {},
        scratch_shapes=list(scratch),
        compiler_params=pltpu.CompilerParams(vmem_limit_bytes=48 * 1024 * 1024),
        cost_estimate=pl.CostEstimate(flops=flops, bytes_accessed=4_000_000, transcendentals=0),
        name=name,
    )


def struct(shape, dtype=F32):
    return jax.ShapeDtypeStruct(shape, dtype)


weights_call = call(
    weights_kernel,
    (struct((768, 256), BF), struct((768, 256), BF), struct((256, 768), BF), struct((256, 768), BF)),
    [VMEM] * 2,
    name="weights",
)
own_call = call(own_kernel, struct((32, 8, 128)), [VMEM], name="own")
INTS = pltpu.SMEM((16,), jnp.int32)
edge_call = call(
    edge_kernel,
    (struct((8, 2, 8, 256)), struct((4, 2, 8, 256)), struct((4, 2, 8, 256))),
    [ANY, VMEM],
    [pltpu.VMEM((8, 2, 8, 256), F32), INTS, pltpu.SemaphoreType.DMA((1,))],
    name="edge",
)
pair_call = call(pair_kernel, (struct((6, 2, 16, 256)), struct((2, 2, 16, 256))), [SMEM] + [VMEM] * 2, name="pair")
column_call = call(
    column_kernel,
    struct((32, 32, 128)),
    [VMEM] * 7,
    [
        pltpu.VMEM((16, 2, 8, 256), F32),
        pltpu.VMEM((640, 768), BF),
        pltpu.VMEM((640, 768), BF),
        pltpu.VMEM((128, 768), BF),
        pltpu.VMEM((128, 768), BF),
        pltpu.VMEM((4, 8, 2, 8, 256), F32),
        pltpu.VMEM((4, 32, 8, 128), F32),
        pltpu.SemaphoreType.DMA((4,)),
    ],
    flops=1_000_000_000,
    out_specs=ANY,
    name="columns",
)
row_call = call(
    row_kernel,
    struct((128, 256)),
    [SMEM] * 2 + [VMEM] * 6,
    [
        pltpu.VMEM((20, 2, 16, 256), F32),
        pltpu.VMEM((384, 768), BF),
        pltpu.VMEM((384, 768), BF),
        pltpu.VMEM((128, 768), BF),
        pltpu.VMEM((128, 768), BF),
    ],
    flops=1_000_000_000,
    name="rows",
)
finish_call = call(
    finish_kernel, struct((128, 256)), [ANY] + [VMEM] * 4, [INTS, pltpu.SemaphoreType.DMA((1,))], flops=300_000_000, name="finish"
)


def routes(shards):
    pairs = [(i, i + 1) for i in range(1, shards - 1, 2)]
    near = pairs + [(b, a) for a, b in pairs]
    far = [(i, i + 2) for i in range(0, shards - 2, 2)] + [(i, i - 2) for i in range(3, shards, 2)]
    pairs = [(i, i + 1) for i in range(0, shards, 2)]
    inner = pairs + [(b, a) for a, b in pairs]
    onward = [(i, (i // 2 + 1) * 2 + 1 - i % 2) for i in range(shards - 2)]
    return near, far, inner, onward, [(b, a) for a, b in onward]


def groups(shards, columns):
    return [
        [(2 * team + (side ^ team % 2)) * columns + c for c in range(columns) for side in range(2)] for team in range(shards // 2)
    ]


def integers(node_count):
    shards = node_count.shape[0]
    team, side = lax.axis_index("team"), lax.axis_index("r")
    here = 2 * team + side
    row = jnp.arange(16, dtype=jnp.int32)[:, None]
    column = jnp.arange(shards, dtype=jnp.int32)[None, :]
    near = jnp.clip(here + row - (COUNTS + 2), 0, shards - 1)
    wanted = (
        (row == TOTAL)
        | ((row == TEAM_BEGIN) & (column < 2 * team))
        | ((row == HERE_BEGIN) & (column < here))
        | ((row >= COUNTS) & (row < ODD) & (column == near))
    )
    sums = jnp.sum(jnp.where(wanted, node_count[None, :], 0), axis=1)
    return sums + jnp.where(row[:, 0] == SIDE, side, 0) + jnp.where(row[:, 0] == ODD, team & 1, 0)


def on_device(densities, hamiltonian, couplings, gamma, coeff, node_count):
    hier = ("team", "r")
    shards = node_count.shape[0]
    everyone = ("team", "r", "col")
    lists = groups(shards, lax.axis_size("col"))
    near, far, inner, onward, backward = routes(shards)

    def exchange(v):
        return lax.all_to_all(v, everyone, 0, 0, axis_index_groups=lists, tiled=True)

    ints = integers(node_count)
    reals = jnp.concatenate([gamma, coeff.reshape(4), jnp.sqrt(jnp.arange(ROOTS, dtype=F32))])
    sent, x = lax.optimization_barrier((own_call(densities.reshape(128, 256)), densities))
    got = exchange(sent)
    p1 = lax.ppermute(x, hier, near)
    own, first, last = edge_call(ints, got)
    below = lax.ppermute(last, hier, onward)
    above = lax.ppermute(first, hier, backward)
    own, p1, x, hamiltonian, couplings = lax.optimization_barrier((own, p1, x, hamiltonian, couplings))
    vhi, vlo, hhi, hlo = weights_call(hamiltonian, couplings)
    wide = jnp.broadcast_to(ints[:, None], (16, 128))
    wide_reals = jnp.broadcast_to(reals[:8, None], (8, 128))
    pair, edge = pair_call(ints, x, p1)
    own, pair, edge = lax.optimization_barrier((own, pair, edge))
    back_sent = column_call(wide, wide_reals, own, below, above, vhi, vlo)
    back_sent, pair, edge = lax.optimization_barrier((back_sent, pair, edge))
    back_got = exchange(back_sent)
    p2 = lax.ppermute(edge, hier, far)
    pair = lax.ppermute(pair, hier, inner)
    base = row_call(ints, reals, x, p1, p2, pair, vhi, vlo)
    out = finish_call(ints, back_got, base, hhi, hlo)
    return out.reshape(4, 2, 16, 256)


def solution(mesh):
    devices = mesh.devices
    inside = Mesh(devices.reshape(devices.shape[0] // 2, 2, devices.shape[1]), ("team", "r", "col"))
    spec = P(("team", "r"), None, "col", None)
    return jax.shard_map(
        on_device,
        mesh=inside,
        in_specs=(spec, P(), P(), P(), P(), P()),
        out_specs=spec,
        check_vma=False,
    )
```

```python
import jax
import jax.numpy as jnp
from jax import lax
from jax.experimental import pallas as pl
from jax.experimental.pallas import tpu as pltpu
from jax.sharding import Mesh, PartitionSpec as P

STEP = 0.2
HALF2 = 0.5 * STEP * STEP
SLOTS = 4
TOTAL, TEAM_BEGIN, HERE_BEGIN, SIDE, COUNTS, ODD = 0, 1, 2, 3, 4, 9
ROOTS = 72
BF = jnp.bfloat16
F32 = jnp.float32


def split(v):
    hi = v.astype(BF)
    return hi, (v - hi.astype(F32)).astype(BF)


def dot(a, b):
    return jnp.dot(a, b, preferred_element_type=F32)


def granules(vs):
    lane = lax.broadcasted_iota(jnp.int32, vs[0].shape, 1) // 16
    turned = [vs[0]] + [pltpu.roll(vs[k], 16 * k, 1) for k in range(1, 8)]
    cur = [turned[-k % 8] for k in range(8)]
    for bit in (1, 2, 4):
        pick = (lane & bit) != 0
        cur = [jnp.where(pick, cur[(m - bit) % 8], cur[m]) for m in range(8)]
    return [cur[0]] + [pltpu.roll(cur[m], 128 - 16 * m, 1) for m in range(1, 8)]


def once(method):
    def cached(self, p):
        key = (method.__name__, p)
        if key not in self.memo:
            self.memo[key] = method(self, p)
        return self.memo[key]

    return cached


class Nodes:
    def __init__(self, total, begin, reals, root):
        self.memo = {}
        self.live = (total >> 1) << 1
        self.begin = begin
        self.base = begin - 4
        self.gamma = (reals[0], reals[1])
        self.re = (reals[2], reals[4])
        self.im = (reals[3], reals[5])
        self.root = root

    @once
    def up(self, p):
        g = self.base + p
        return self.root((g >> 1) + 1) * jnp.where((g >= 0) & (g + 2 < self.live), 1.0, 0.0)

    @once
    def down(self, p):
        g = self.base + p
        return self.root(g >> 1) * jnp.where((g >= 2) & (g < self.live), 1.0, 0.0)

    @once
    def twist(self, p):
        g = self.base + p
        n = (g >> 1).astype(F32)
        ok = (g >= 0) & (g < self.live)
        return jnp.where(ok & (g + 2 < self.live), n + 1.0, 0.0) - jnp.where(ok & (g >= 2), n, 0.0)

    @once
    def even(self, p):
        g = self.base + p
        return jnp.where((g >= 0) & (g < self.live) & ((g & 1) == 0), 1.0, 0.0).astype(F32)

    @once
    def odd(self, p):
        g = self.base + p
        return jnp.where((g >= 0) & (g < self.live) & ((g & 1) == 1), 1.0, 0.0).astype(F32)

    @once
    def damp(self, p):
        g = self.base + p
        n0 = (g >> 1).astype(F32)
        n1 = (g & 1).astype(F32)
        return n0 * self.gamma[0] + n1 * self.gamma[1]


def scaled(s, v):
    return (s * v[0], s * v[1])


def plus(a, b):
    return (a[0] + b[0], a[1] + b[1])


def times(re, im, v):
    return (re * v[0] - im * v[1], re * v[1] + im * v[0])


def both(nodes, x, p, re, im):
    r = plus(scaled(nodes.up(p), x[p + 2]), scaled(re * nodes.down(p), x[p - 2]))
    t = scaled(im * nodes.down(p), x[p - 2])
    return (r[0] - t[1], r[1] + t[0]), (r[0] + t[1], r[1] - t[0])


def both1(nodes, x, p, re, im):
    r = plus(scaled(nodes.even(p), x[p + 1]), scaled(re * nodes.odd(p), x[p - 1]))
    t = scaled(im * nodes.odd(p), x[p - 1])
    return (r[0] - t[1], r[1] + t[0]), (r[0] + t[1], r[1] - t[0])


def first_order(nodes, x, p, re, im):
    here = nodes.damp(p)

    def w(q):
        return STEP - HALF2 * (here + nodes.damp(q))

    zero = scaled(w(p), x[p])
    up, down = scaled(w(p + 2) * nodes.up(p), x[p + 2]), scaled(w(p - 2) * nodes.down(p), x[p - 2])
    one = plus(up, times(re[0], im[0], down))
    up, down = scaled(w(p + 1) * nodes.even(p), x[p + 1]), scaled(w(p - 1) * nodes.odd(p), x[p - 1])
    two = plus(up, times(re[1], im[1], down))
    return zero, one, two


def put(hi_ref, lo_ref, col, j, rows, v):
    hi, lo = split(jnp.concatenate([v[0], v[1]], axis=0))
    at = pl.ds(j * rows, rows)
    hi_ref[at, 256 * col : 256 * col + 256] = hi
    lo_ref[at, 256 * col : 256 * col + 256] = lo


def product(hi, lo, ghi, glo):
    return dot(hi, ghi) + dot(lo, ghi) + dot(hi, glo)


def times_weights(hi_ref, lo_ref, ghi_ref, glo_ref):
    return product(hi_ref[...], lo_ref[...], ghi_ref[...], glo_ref[...])


def weights_kernel(h_ref, q_ref, vhi, vlo, hhi, hlo):
    for b in range(3):
        hi, lo = split(h_ref[...] if b == 0 else q_ref[b - 1])
        vhi[256 * b : 256 * b + 256, :] = hi
        vlo[256 * b : 256 * b + 256, :] = lo
        hhi[:, 256 * b : 256 * b + 256] = hi
        hlo[:, 256 * b : 256 * b + 256] = lo


def own_kernel(x_ref, o_ref):
    o_ref[...] = x_ref[...].T.reshape(32, 8, 128)


def fetch(pairs, sem):
    copies = [pltpu.make_async_copy(source, target, sem.at[i]) for i, (source, target) in enumerate(pairs)]
    for copy in copies:
        copy.start()
    return copies


def taken(ref, i):
    return ref[i : i + 1, 0:1][0, 0]


def edge_kernel(wide_ref, got_ref, own_ref, first_ref, last_ref, y_ref):
    side, before, here, after, odd = (taken(wide_ref, i) for i in (SIDE, COUNTS + 1, COUNTS + 2, COUNTS + 3, ODD))
    own, other = jnp.where(side == 0, here, before), jnp.where(side == 0, after, here)
    for place in range(2):
        vs = []
        for low in range(8):
            vs.append(jnp.concatenate([got_ref[(8 * high + low) * 2 + place] for high in range(2)], axis=0))
        for m, v in enumerate(granules(vs)):
            y_ref[SLOTS * place + m // 2, m % 2] = jnp.concatenate([v[:8], v[8:]], axis=1)

    def node(j):
        return y_ref[jnp.where(j < own, SLOTS * odd + j, SLOTS * (1 - odd) + jnp.clip(j - own, 0, SLOTS - 1))]

    for j in range(8):
        own_ref[j] = node(j)
    for j in range(4):
        first_ref[j] = node(j)
        last_ref[j] = node(own + other - 4 + j)


def pair_kernel(ints_ref, x_ref, near_ref, o_ref, far_ref):
    far_ref[...] = x_ref[pl.ds(jnp.where(ints_ref[SIDE] == 0, ints_ref[COUNTS + 2] - 2, 0), 2)]
    o_ref[0:4] = x_ref[...]
    o_ref[4:6] = near_ref[pl.ds(jnp.where(ints_ref[SIDE] == 0, ints_ref[COUNTS + 1] - 2, 0), 2)]


def column_kernel(
    wide_ref, reals_ref, own_ref, below_ref, above_ref, ghi_ref, glo_ref, o_ref, y_ref, hi_ref, lo_ref, hi2_ref, lo2_ref, z_ref, send_ref, out_sem
):
    total, begin, side, before, here, after, odd = (
        taken(wide_ref, i) for i in (TOTAL, TEAM_BEGIN, SIDE, COUNTS + 1, COUNTS + 2, COUNTS + 3, ODD)
    )
    reals = [taken(reals_ref, i) for i in range(6)]
    own, other = jnp.where(side == 0, here, before), jnp.where(side == 0, after, here)

    def root(n):
        return jnp.sqrt(jnp.full((8, 256), jnp.maximum(n, 0).astype(F32)))

    nodes = Nodes(total, begin, reals, root)
    re, im = nodes.re, nodes.im
    y_ref[0:4] = below_ref[...]
    y_ref[4:12] = own_ref[...]
    y_ref[12:16] = above_ref[...]
    y_ref[pl.ds(4 + own + other, 4)] = above_ref[...]
    x = []
    for p in range(16):
        v = y_ref[p]
        x.append((v[0], v[1]))
    for p in range(2, 14):
        put(hi_ref, lo_ref, 0, p - 2, 16, x[p])
        put(hi_ref, lo_ref, 1, p - 2, 16, both(nodes, x, p, re[0], im[0])[0])
        put(hi_ref, lo_ref, 2, p - 2, 16, both1(nodes, x, p, re[1], im[1])[0])
    sums = times_weights(hi_ref, lo_ref, ghi_ref, glo_ref)
    hi, lo = hi_ref[32:160, :256], lo_ref[32:160, :256]
    alone = [product(hi, lo, ghi_ref[256 * b : 256 * b + 256, :], glo_ref[256 * b : 256 * b + 256, :]) for b in (1, 2)]
    s = {p: (sums[16 * p - 32 : 16 * p - 24], sums[16 * p - 24 : 16 * p - 16]) for p in range(2, 14)}
    for j in range(8):
        p = j + 4
        left, right = zip(both(nodes, s, p, re[0], im[0]), both1(nodes, s, p, re[1], im[1]))
        for col, (v, t) in enumerate(zip(first_order(nodes, x, p, re, im), (s[p], *left))):
            put(hi2_ref, lo2_ref, col, j, 16, (v[1] - HALF2 * t[0], -v[0] - HALF2 * t[1]))
        z_ref[1, j] = (2.0 * HALF2) * sums[16 * j + 32 : 16 * j + 48].reshape(2, 8, 256)
        for b, twist in enumerate((nodes.twist(p), nodes.even(p) - nodes.odd(p))):
            by = im[b] * twist
            z_ref[2 + b, j, 0] = (2.0 * HALF2) * (right[b][0] + by * alone[b][16 * j + 8 : 16 * j + 16])
            z_ref[2 + b, j, 1] = (2.0 * HALF2) * (right[b][1] - by * alone[b][16 * j : 16 * j + 8])

    def send(z):
        for r in range(2):
            vs = []
            for m in range(8):
                v = z_ref[z, m // 2 if r == 0 else own + m // 2, m % 2]
                vs.append(jnp.concatenate([v[:, :128], v[:, 128:]], axis=0))
            for low, v in enumerate(granules(vs)):
                for high in range(2):
                    send_ref[z, (8 * high + low) * 2 + (odd if r == 0 else 1 - odd)] = v[8 * high : 8 * high + 8]
        copy = pltpu.make_async_copy(send_ref.at[z], o_ref.at[:, 8 * z : 8 * z + 8], out_sem.at[z])
        copy.start()
        return copy

    last = times_weights(hi2_ref, lo2_ref, ghi_ref, glo_ref)
    copies = [send(z) for z in range(1, 4)]
    z_ref[0] = last.reshape(8, 2, 8, 256)
    for copy in [*copies, send(0)]:
        copy.wait()


def row_kernel(
    ints_ref, reals_ref, x_ref, p1_ref, p2_ref, pair_ref, ghi_ref, glo_ref, o_ref, w_ref, hi_ref, lo_ref, hi2_ref, lo2_ref
):

    def root(n):
        return reals_ref[jnp.clip(n, 0, ROOTS - 1) + 6]

    nodes = Nodes(ints_ref[TOTAL], ints_ref[HERE_BEGIN], [reals_ref[i] for i in range(6)], root)
    re, im = nodes.re, (-nodes.im[0], -nodes.im[1])
    up = ints_ref[SIDE]
    farther, below, own, above = (ints_ref[COUNTS + i] for i in range(4))
    w_ref[8:12] = x_ref[...]
    w_ref[pl.ds(4 + 8 * up, 4)] = p1_ref[...]
    w_ref[pl.ds(jnp.where(up == 0, farther - 2, 16), 2)] = p2_ref[...]
    w_ref[pl.ds(12 - 8 * up, 4)] = pair_ref[0:4]
    w_ref[pl.ds(jnp.where(up == 0, 16, farther - 2), 2)] = pair_ref[4:6]

    def slot(p):
        j = p - 4
        if j < 0:
            return jnp.where(j + below >= 0, 4 + j + below, farther + j + below)
        return jnp.where(j < own, 8 + j, jnp.where(j < own + above, 12 + j - own, jnp.minimum(16 + j - own - above, 19)))

    x = []
    for p in range(12):
        v = w_ref[slot(p)]
        x.append((v[0], v[1]))
    for p in range(2, 10):
        put(hi_ref, lo_ref, 0, p - 2, 32, x[p])
        put(hi_ref, lo_ref, 1, p - 2, 32, both(nodes, x, p, re[0], im[0])[0])
        put(hi_ref, lo_ref, 2, p - 2, 32, both1(nodes, x, p, re[1], im[1])[0])
    sums = times_weights(hi_ref, lo_ref, ghi_ref, glo_ref)
    s = {p: (sums[32 * p - 64 : 32 * p - 48], sums[32 * p - 48 : 32 * p - 32]) for p in range(2, 10)}
    for j in range(4):
        p = j + 4
        mixed = (s[p], both(nodes, s, p, re[0], im[0])[0], both1(nodes, s, p, re[1], im[1])[0])
        for col, (v, t) in enumerate(zip(first_order(nodes, x, p, re, im), mixed)):
            put(hi2_ref, lo2_ref, col, j, 32, (-v[1] - HALF2 * t[0], v[0] - HALF2 * t[1]))
    right = times_weights(hi2_ref, lo2_ref, ghi_ref, glo_ref)
    for j in range(4):
        d = nodes.damp(j + 4)
        keep = 1.0 - STEP * d + HALF2 * d * d
        old = x_ref[j].reshape(32, 256)
        live = (j < own) & (nodes.begin + j < nodes.live)
        o_ref[32 * j : 32 * j + 32, :] = jnp.where(live, keep * old + right[32 * j : 32 * j + 32], old)


def finish_kernel(ints_in, got_ref, base_ref, ghi_ref, glo_ref, o_ref, ints_ref, sem):
    fetched = fetch([(ints_in, ints_ref)], sem)
    his, los = [], []
    for z in range(1, 4):
        hi, lo = split(got_ref[:, 8 * z : 8 * z + 8, :].reshape(256, 128))
        his.append(hi)
        los.append(lo)
    hi, lo = jnp.concatenate(his, axis=0), jnp.concatenate(los, axis=0)
    g = ghi_ref[...]
    out = dot(g, hi) + dot(g, lo) + dot(glo_ref[...], hi) + got_ref[:, :8, :].reshape(256, 128)
    out = out.T
    for copy in fetched:
        copy.wait()
    own, begin, limit = ints_ref[COUNTS + 2], ints_ref[HERE_BEGIN], (ints_ref[TOTAL] >> 1) << 1
    for j in range(4):
        live = (j < own) & (begin + j < limit)
        rows = slice(32 * j, 32 * j + 32)
        o_ref[rows, :] = base_ref[rows, :] + jnp.where(live, out[rows], 0.0)


SMEM = pl.BlockSpec(memory_space=pltpu.SMEM)
VMEM = pl.BlockSpec(memory_space=pltpu.VMEM)
ANY = pl.BlockSpec(memory_space=pl.ANY)


def call(kernel, outs, specs, scratch=(), flops=1_000_000, name=None, out_specs=None, aliases=None):
    return pl.pallas_call(
        kernel,
        out_shape=outs,
        in_specs=specs,
        out_specs=out_specs or jax.tree.map(lambda _: VMEM, outs),
        input_output_aliases=aliases or {},
        scratch_shapes=list(scratch),
        compiler_params=pltpu.CompilerParams(vmem_limit_bytes=48 * 1024 * 1024),
        cost_estimate=pl.CostEstimate(flops=flops, bytes_accessed=4_000_000, transcendentals=0),
        name=name,
    )


def struct(shape, dtype=F32):
    return jax.ShapeDtypeStruct(shape, dtype)


weights_call = call(
    weights_kernel,
    (struct((768, 256), BF), struct((768, 256), BF), struct((256, 768), BF), struct((256, 768), BF)),
    [VMEM] * 2,
    name="weights",
)
own_call = call(own_kernel, struct((32, 8, 128)), [VMEM], name="own")
INTS = pltpu.SMEM((16,), jnp.int32)
edge_call = call(
    edge_kernel,
    (struct((8, 2, 8, 256)), struct((4, 2, 8, 256)), struct((4, 2, 8, 256))),
    [VMEM] * 2,
    [pltpu.VMEM((8, 2, 8, 256), F32)],
    name="edge",
)
pair_call = call(pair_kernel, (struct((6, 2, 16, 256)), struct((2, 2, 16, 256))), [SMEM] + [VMEM] * 2, name="pair")
column_call = call(
    column_kernel,
    struct((32, 32, 128)),
    [VMEM] * 7,
    [
        pltpu.VMEM((16, 2, 8, 256), F32),
        pltpu.VMEM((192, 768), BF),
        pltpu.VMEM((192, 768), BF),
        pltpu.VMEM((128, 768), BF),
        pltpu.VMEM((128, 768), BF),
        pltpu.VMEM((4, 8, 2, 8, 256), F32),
        pltpu.VMEM((4, 32, 8, 128), F32),
        pltpu.SemaphoreType.DMA((4,)),
    ],
    flops=1_000_000_000,
    out_specs=ANY,
    name="columns",
)
row_call = call(
    row_kernel,
    struct((128, 256)),
    [SMEM] * 2 + [VMEM] * 6,
    [
        pltpu.VMEM((20, 2, 16, 256), F32),
        pltpu.VMEM((256, 768), BF),
        pltpu.VMEM((256, 768), BF),
        pltpu.VMEM((128, 768), BF),
        pltpu.VMEM((128, 768), BF),
    ],
    flops=1_000_000_000,
    name="rows",
)
finish_call = call(
    finish_kernel, struct((128, 256)), [ANY] + [VMEM] * 4, [INTS, pltpu.SemaphoreType.DMA((1,))], flops=300_000_000, name="finish"
)


def routes(shards):
    pairs = [(i, i + 1) for i in range(1, shards - 1, 2)]
    near = pairs + [(b, a) for a, b in pairs]
    far = [(i, i + 2) for i in range(0, shards - 2, 2)] + [(i, i - 2) for i in range(3, shards, 2)]
    pairs = [(i, i + 1) for i in range(0, shards, 2)]
    inner = pairs + [(b, a) for a, b in pairs]
    onward = [(i, (i // 2 + 1) * 2 + 1 - i % 2) for i in range(shards - 2)]
    return near, far, inner, onward, [(b, a) for a, b in onward]


def groups(shards, columns):
    return [
        [(2 * team + (side ^ team % 2)) * columns + c for c in range(columns) for side in range(2)] for team in range(shards // 2)
    ]


def integers(node_count):
    shards = node_count.shape[0]
    team, side = lax.axis_index("team"), lax.axis_index("r")
    here = 2 * team + side
    row = jnp.arange(16, dtype=jnp.int32)[:, None]
    column = jnp.arange(shards, dtype=jnp.int32)[None, :]
    near = jnp.clip(here + row - (COUNTS + 2), 0, shards - 1)
    wanted = (
        (row == TOTAL)
        | ((row == TEAM_BEGIN) & (column < 2 * team))
        | ((row == HERE_BEGIN) & (column < here))
        | ((row >= COUNTS) & (row < ODD) & (column == near))
    )
    sums = jnp.sum(jnp.where(wanted, node_count[None, :], 0), axis=1)
    return sums + jnp.where(row[:, 0] == SIDE, side, 0) + jnp.where(row[:, 0] == ODD, team & 1, 0)


def on_device(densities, hamiltonian, couplings, gamma, coeff, node_count):
    hier = ("team", "r")
    shards = node_count.shape[0]
    everyone = ("team", "r", "col")
    lists = groups(shards, lax.axis_size("col"))
    near, far, inner, onward, backward = routes(shards)

    def exchange(v):
        return lax.all_to_all(v, everyone, 0, 0, axis_index_groups=lists, tiled=True)

    ints = integers(node_count)
    wide = jnp.broadcast_to(ints[:, None], (16, 128))
    reals = jnp.concatenate([gamma, coeff.reshape(4), jnp.sqrt(jnp.arange(ROOTS, dtype=F32))])
    sent, x = lax.optimization_barrier((own_call(densities.reshape(128, 256)), densities))
    got = exchange(sent)
    p1 = lax.ppermute(x, hier, near)
    own, first, last = edge_call(wide, got)
    below = lax.ppermute(last, hier, onward)
    above = lax.ppermute(first, hier, backward)
    own, p1, x, hamiltonian, couplings = lax.optimization_barrier((own, p1, x, hamiltonian, couplings))
    vhi, vlo, hhi, hlo = weights_call(hamiltonian, couplings)
    wide_reals = jnp.broadcast_to(reals[:8, None], (8, 128))
    pair, edge = pair_call(ints, x, p1)
    own, pair, edge = lax.optimization_barrier((own, pair, edge))
    back_sent = column_call(wide, wide_reals, own, below, above, vhi, vlo)
    back_sent, pair, edge = lax.optimization_barrier((back_sent, pair, edge))
    back_got = exchange(back_sent)
    p2 = lax.ppermute(edge, hier, far)
    pair = lax.ppermute(pair, hier, inner)
    base = row_call(ints, reals, x, p1, p2, pair, vhi, vlo)
    out = finish_call(ints, back_got, base, hhi, hlo)
    return out.reshape(4, 2, 16, 256)


def solution(mesh):
    devices = mesh.devices
    inside = Mesh(devices.reshape(devices.shape[0] // 2, 2, devices.shape[1]), ("team", "r", "col"))
    spec = P(("team", "r"), None, "col", None)
    return jax.shard_map(
        on_device,
        mesh=inside,
        in_specs=(spec, P(), P(), P(), P(), P()),
        out_specs=spec,
        check_vma=False,
    )
```

```python
import jax
import jax.numpy as jnp
from jax import lax
from jax.experimental import pallas as pl
from jax.experimental.pallas import tpu as pltpu
from jax.sharding import Mesh, PartitionSpec as P

STEP = 0.2
HALF2 = 0.5 * STEP * STEP
SLOTS = 4
TOTAL, TEAM_BEGIN, HERE_BEGIN, SIDE, COUNTS, ODD = 0, 1, 2, 3, 4, 9
ROOTS = 72
BF = jnp.bfloat16
F32 = jnp.float32


def split(v):
    hi = v.astype(BF)
    return hi, (v - hi.astype(F32)).astype(BF)


def dot(a, b):
    return jnp.dot(a, b, preferred_element_type=F32)


def granules(vs):
    lane = lax.broadcasted_iota(jnp.int32, vs[0].shape, 1) // 16
    turned = [vs[0]] + [pltpu.roll(vs[k], 16 * k, 1) for k in range(1, 8)]
    cur = [turned[-k % 8] for k in range(8)]
    for bit in (1, 2, 4):
        pick = (lane & bit) != 0
        cur = [jnp.where(pick, cur[(m - bit) % 8], cur[m]) for m in range(8)]
    return [cur[0]] + [pltpu.roll(cur[m], 128 - 16 * m, 1) for m in range(1, 8)]


def once(method):
    def cached(self, p):
        key = (method.__name__, p)
        if key not in self.memo:
            self.memo[key] = method(self, p)
        return self.memo[key]

    return cached


class Nodes:
    def __init__(self, total, begin, reals, root):
        self.memo = {}
        self.live = (total >> 1) << 1
        self.begin = begin
        self.base = begin - 4
        self.gamma = (reals[0], reals[1])
        self.re = (reals[2], reals[4])
        self.im = (reals[3], reals[5])
        self.root = root

    @once
    def up(self, p):
        g = self.base + p
        return self.root((g >> 1) + 1) * jnp.where((g >= 0) & (g + 2 < self.live), 1.0, 0.0)

    @once
    def down(self, p):
        g = self.base + p
        return self.root(g >> 1) * jnp.where((g >= 2) & (g < self.live), 1.0, 0.0)

    @once
    def twist(self, p):
        g = self.base + p
        n = (g >> 1).astype(F32)
        ok = (g >= 0) & (g < self.live)
        return jnp.where(ok & (g + 2 < self.live), n + 1.0, 0.0) - jnp.where(ok & (g >= 2), n, 0.0)

    @once
    def even(self, p):
        g = self.base + p
        return jnp.where((g >= 0) & (g < self.live) & ((g & 1) == 0), 1.0, 0.0).astype(F32)

    @once
    def odd(self, p):
        g = self.base + p
        return jnp.where((g >= 0) & (g < self.live) & ((g & 1) == 1), 1.0, 0.0).astype(F32)

    @once
    def damp(self, p):
        g = self.base + p
        n0 = (g >> 1).astype(F32)
        n1 = (g & 1).astype(F32)
        return n0 * self.gamma[0] + n1 * self.gamma[1]


def scaled(s, v):
    return (s * v[0], s * v[1])


def plus(a, b):
    return (a[0] + b[0], a[1] + b[1])


def times(re, im, v):
    return (re * v[0] - im * v[1], re * v[1] + im * v[0])


def both(nodes, x, p, re, im):
    r = plus(scaled(nodes.up(p), x[p + 2]), scaled(re * nodes.down(p), x[p - 2]))
    t = scaled(im * nodes.down(p), x[p - 2])
    return (r[0] - t[1], r[1] + t[0]), (r[0] + t[1], r[1] - t[0])


def both1(nodes, x, p, re, im):
    r = plus(scaled(nodes.even(p), x[p + 1]), scaled(re * nodes.odd(p), x[p - 1]))
    t = scaled(im * nodes.odd(p), x[p - 1])
    return (r[0] - t[1], r[1] + t[0]), (r[0] + t[1], r[1] - t[0])


def first_order(nodes, x, p, re, im):
    here = nodes.damp(p)

    def w(q):
        return STEP - HALF2 * (here + nodes.damp(q))

    zero = scaled(w(p), x[p])
    up, down = scaled(w(p + 2) * nodes.up(p), x[p + 2]), scaled(w(p - 2) * nodes.down(p), x[p - 2])
    one = plus(up, times(re[0], im[0], down))
    up, down = scaled(w(p + 1) * nodes.even(p), x[p + 1]), scaled(w(p - 1) * nodes.odd(p), x[p - 1])
    two = plus(up, times(re[1], im[1], down))
    return zero, one, two


def put(hi_ref, lo_ref, col, j, rows, v):
    hi, lo = split(jnp.concatenate([v[0], v[1]], axis=0))
    at = pl.ds(j * rows, rows)
    hi_ref[at, 256 * col : 256 * col + 256] = hi
    lo_ref[at, 256 * col : 256 * col + 256] = lo


def product(hi, lo, ghi, glo):
    return dot(hi, ghi) + dot(lo, ghi) + dot(hi, glo)


def times_weights(hi_ref, lo_ref, ghi_ref, glo_ref):
    return product(hi_ref[...], lo_ref[...], ghi_ref[...], glo_ref[...])


def weights_kernel(h_ref, q_ref, vhi, vlo, hhi, hlo):
    for b in range(3):
        hi, lo = split(h_ref[...] if b == 0 else q_ref[b - 1])
        vhi[256 * b : 256 * b + 256, :] = hi
        vlo[256 * b : 256 * b + 256, :] = lo
        hhi[:, 256 * b : 256 * b + 256] = hi
        hlo[:, 256 * b : 256 * b + 256] = lo


def own_kernel(x_ref, o_ref):
    o_ref[...] = x_ref[...].T.reshape(32, 8, 128)


def fetch(pairs, sem):
    copies = [pltpu.make_async_copy(source, target, sem.at[i]) for i, (source, target) in enumerate(pairs)]
    for copy in copies:
        copy.start()
    return copies


def taken(ref, i):
    return ref[i : i + 1, 0:1][0, 0]


def edge_kernel(wide_ref, got_ref, own_ref, ring_ref, cross_ref, y_ref):
    side, before, here, after, odd = (taken(wide_ref, i) for i in (SIDE, COUNTS + 1, COUNTS + 2, COUNTS + 3, ODD))
    own, other = jnp.where(side == 0, here, before), jnp.where(side == 0, after, here)
    for place in range(2):
        vs = []
        for low in range(8):
            vs.append(jnp.concatenate([got_ref[(8 * high + low) * 2 + place] for high in range(2)], axis=0))
        for m, v in enumerate(granules(vs)):
            y_ref[SLOTS * place + m // 2, m % 2] = jnp.concatenate([v[:8], v[8:]], axis=1)

    def node(j):
        return y_ref[jnp.where(j < own, SLOTS * odd + j, SLOTS * (1 - odd) + jnp.clip(j - own, 0, SLOTS - 1))]

    for j in range(8):
        own_ref[j] = node(j)
    behind, ahead = jnp.where(odd == 0, own + other - 4, 0), jnp.where(odd == 0, 0, own + other - 4)
    for j in range(4):
        ring_ref[j] = node(behind + j)
        cross_ref[j] = node(ahead + j)


def pair_kernel(ints_ref, x_ref, near_ref, o_ref, far_ref):
    far_ref[...] = x_ref[pl.ds(jnp.where(ints_ref[SIDE] == 0, ints_ref[COUNTS + 2] - 2, 0), 2)]
    o_ref[0:4] = x_ref[...]
    o_ref[4:6] = near_ref[pl.ds(jnp.where(ints_ref[SIDE] == 0, ints_ref[COUNTS + 1] - 2, 0), 2)]


def column_kernel(
    wide_ref, reals_ref, own_ref, cross_ref, ring_ref, ghi_ref, glo_ref, o_ref, y_ref, hi_ref, lo_ref, hi2_ref, lo2_ref, z_ref, send_ref, out_sem
):
    total, begin, side, before, here, after, odd = (
        taken(wide_ref, i) for i in (TOTAL, TEAM_BEGIN, SIDE, COUNTS + 1, COUNTS + 2, COUNTS + 3, ODD)
    )
    reals = [taken(reals_ref, i) for i in range(6)]
    own, other = jnp.where(side == 0, here, before), jnp.where(side == 0, after, here)

    def root(n):
        return jnp.sqrt(jnp.full((8, 256), jnp.maximum(n, 0).astype(F32)))

    nodes = Nodes(total, begin, reals, root)
    re, im = nodes.re, nodes.im
    y_ref[4:12] = own_ref[...]
    y_ref[12:16] = ring_ref[...]
    y_ref[pl.ds(jnp.where(odd == 0, 4 + own + other, 0), 4)] = ring_ref[...]
    y_ref[pl.ds(jnp.where(odd == 0, 0, 4 + own + other), 4)] = cross_ref[...]
    x = []
    for p in range(16):
        v = y_ref[p]
        x.append((v[0], v[1]))
    for p in range(2, 14):
        put(hi_ref, lo_ref, 0, p - 2, 16, x[p])
        put(hi_ref, lo_ref, 1, p - 2, 16, both(nodes, x, p, re[0], im[0])[0])
        put(hi_ref, lo_ref, 2, p - 2, 16, both1(nodes, x, p, re[1], im[1])[0])
    sums = times_weights(hi_ref, lo_ref, ghi_ref, glo_ref)
    hi, lo = hi_ref[32:160, :256], lo_ref[32:160, :256]
    alone = [product(hi, lo, ghi_ref[256 * b : 256 * b + 256, :], glo_ref[256 * b : 256 * b + 256, :]) for b in (1, 2)]
    s = {p: (sums[16 * p - 32 : 16 * p - 24], sums[16 * p - 24 : 16 * p - 16]) for p in range(2, 14)}
    for j in range(8):
        p = j + 4
        left, right = zip(both(nodes, s, p, re[0], im[0]), both1(nodes, s, p, re[1], im[1]))
        for col, (v, t) in enumerate(zip(first_order(nodes, x, p, re, im), (s[p], *left))):
            put(hi2_ref, lo2_ref, col, j, 16, (v[1] - HALF2 * t[0], -v[0] - HALF2 * t[1]))
        z_ref[1, j] = (2.0 * HALF2) * sums[16 * j + 32 : 16 * j + 48].reshape(2, 8, 256)
        for b, twist in enumerate((nodes.twist(p), nodes.even(p) - nodes.odd(p))):
            by = im[b] * twist
            z_ref[2 + b, j, 0] = (2.0 * HALF2) * (right[b][0] + by * alone[b][16 * j + 8 : 16 * j + 16])
            z_ref[2 + b, j, 1] = (2.0 * HALF2) * (right[b][1] - by * alone[b][16 * j : 16 * j + 8])

    def send(z):
        for r in range(2):
            vs = []
            for m in range(8):
                v = z_ref[z, m // 2 if r == 0 else own + m // 2, m % 2]
                vs.append(jnp.concatenate([v[:, :128], v[:, 128:]], axis=0))
            for low, v in enumerate(granules(vs)):
                for high in range(2):
                    send_ref[z, (8 * high + low) * 2 + (odd if r == 0 else 1 - odd)] = v[8 * high : 8 * high + 8]
        copy = pltpu.make_async_copy(send_ref.at[z], o_ref.at[:, 8 * z : 8 * z + 8], out_sem.at[z])
        copy.start()
        return copy

    last = times_weights(hi2_ref, lo2_ref, ghi_ref, glo_ref)
    copies = [send(z) for z in range(1, 4)]
    z_ref[0] = last.reshape(8, 2, 8, 256)
    for copy in [*copies, send(0)]:
        copy.wait()


def row_kernel(
    ints_ref, reals_ref, x_ref, p1_ref, p2_ref, pair_ref, ghi_ref, glo_ref, o_ref, w_ref, hi_ref, lo_ref, hi2_ref, lo2_ref
):

    def root(n):
        return reals_ref[jnp.clip(n, 0, ROOTS - 1) + 6]

    nodes = Nodes(ints_ref[TOTAL], ints_ref[HERE_BEGIN], [reals_ref[i] for i in range(6)], root)
    re, im = nodes.re, (-nodes.im[0], -nodes.im[1])
    up = ints_ref[SIDE]
    farther, below, own, above = (ints_ref[COUNTS + i] for i in range(4))
    w_ref[8:12] = x_ref[...]
    w_ref[pl.ds(4 + 8 * up, 4)] = p1_ref[...]
    w_ref[pl.ds(jnp.where(up == 0, farther - 2, 16), 2)] = p2_ref[...]
    w_ref[pl.ds(12 - 8 * up, 4)] = pair_ref[0:4]
    w_ref[pl.ds(jnp.where(up == 0, 16, farther - 2), 2)] = pair_ref[4:6]

    def slot(p):
        j = p - 4
        if j < 0:
            return jnp.where(j + below >= 0, 4 + j + below, farther + j + below)
        return jnp.where(j < own, 8 + j, jnp.where(j < own + above, 12 + j - own, jnp.minimum(16 + j - own - above, 19)))

    x = []
    for p in range(12):
        v = w_ref[slot(p)]
        x.append((v[0], v[1]))
    for p in range(2, 10):
        put(hi_ref, lo_ref, 0, p - 2, 32, x[p])
        put(hi_ref, lo_ref, 1, p - 2, 32, both(nodes, x, p, re[0], im[0])[0])
        put(hi_ref, lo_ref, 2, p - 2, 32, both1(nodes, x, p, re[1], im[1])[0])
    sums = times_weights(hi_ref, lo_ref, ghi_ref, glo_ref)
    s = {p: (sums[32 * p - 64 : 32 * p - 48], sums[32 * p - 48 : 32 * p - 32]) for p in range(2, 10)}
    for j in range(4):
        p = j + 4
        mixed = (s[p], both(nodes, s, p, re[0], im[0])[0], both1(nodes, s, p, re[1], im[1])[0])
        for col, (v, t) in enumerate(zip(first_order(nodes, x, p, re, im), mixed)):
            put(hi2_ref, lo2_ref, col, j, 32, (-v[1] - HALF2 * t[0], v[0] - HALF2 * t[1]))
    right = times_weights(hi2_ref, lo2_ref, ghi_ref, glo_ref)
    for j in range(4):
        d = nodes.damp(j + 4)
        keep = 1.0 - STEP * d + HALF2 * d * d
        old = x_ref[j].reshape(32, 256)
        live = (j < own) & (nodes.begin + j < nodes.live)
        o_ref[32 * j : 32 * j + 32, :] = jnp.where(live, keep * old + right[32 * j : 32 * j + 32], old)


def finish_kernel(ints_in, got_ref, base_ref, ghi_ref, glo_ref, o_ref, ints_ref, sem):
    fetched = fetch([(ints_in, ints_ref)], sem)
    his, los = [], []
    for z in range(1, 4):
        hi, lo = split(got_ref[:, 8 * z : 8 * z + 8, :].reshape(256, 128))
        his.append(hi)
        los.append(lo)
    hi, lo = jnp.concatenate(his, axis=0), jnp.concatenate(los, axis=0)
    g = ghi_ref[...]
    out = dot(g, hi) + dot(g, lo) + dot(glo_ref[...], hi) + got_ref[:, :8, :].reshape(256, 128)
    out = out.T
    for copy in fetched:
        copy.wait()
    own, begin, limit = ints_ref[COUNTS + 2], ints_ref[HERE_BEGIN], (ints_ref[TOTAL] >> 1) << 1
    for j in range(4):
        live = (j < own) & (begin + j < limit)
        rows = slice(32 * j, 32 * j + 32)
        o_ref[rows, :] = base_ref[rows, :] + jnp.where(live, out[rows], 0.0)


SMEM = pl.BlockSpec(memory_space=pltpu.SMEM)
VMEM = pl.BlockSpec(memory_space=pltpu.VMEM)
ANY = pl.BlockSpec(memory_space=pl.ANY)


def call(kernel, outs, specs, scratch=(), flops=1_000_000, name=None, out_specs=None, aliases=None):
    return pl.pallas_call(
        kernel,
        out_shape=outs,
        in_specs=specs,
        out_specs=out_specs or jax.tree.map(lambda _: VMEM, outs),
        input_output_aliases=aliases or {},
        scratch_shapes=list(scratch),
        compiler_params=pltpu.CompilerParams(vmem_limit_bytes=48 * 1024 * 1024),
        cost_estimate=pl.CostEstimate(flops=flops, bytes_accessed=4_000_000, transcendentals=0),
        name=name,
    )


def struct(shape, dtype=F32):
    return jax.ShapeDtypeStruct(shape, dtype)


weights_call = call(
    weights_kernel,
    (struct((768, 256), BF), struct((768, 256), BF), struct((256, 768), BF), struct((256, 768), BF)),
    [VMEM] * 2,
    name="weights",
)
own_call = call(own_kernel, struct((32, 8, 128)), [VMEM], name="own")
INTS = pltpu.SMEM((16,), jnp.int32)
edge_call = call(
    edge_kernel,
    (struct((8, 2, 8, 256)), struct((4, 2, 8, 256)), struct((4, 2, 8, 256))),
    [VMEM] * 2,
    [pltpu.VMEM((8, 2, 8, 256), F32)],
    name="edge",
)
pair_call = call(pair_kernel, (struct((6, 2, 16, 256)), struct((2, 2, 16, 256))), [SMEM] + [VMEM] * 2, name="pair")
column_call = call(
    column_kernel,
    struct((32, 32, 128)),
    [VMEM] * 7,
    [
        pltpu.VMEM((16, 2, 8, 256), F32),
        pltpu.VMEM((192, 768), BF),
        pltpu.VMEM((192, 768), BF),
        pltpu.VMEM((128, 768), BF),
        pltpu.VMEM((128, 768), BF),
        pltpu.VMEM((4, 8, 2, 8, 256), F32),
        pltpu.VMEM((4, 32, 8, 128), F32),
        pltpu.SemaphoreType.DMA((4,)),
    ],
    flops=1_000_000_000,
    out_specs=ANY,
    name="columns",
)
row_call = call(
    row_kernel,
    struct((128, 256)),
    [SMEM] * 2 + [VMEM] * 6,
    [
        pltpu.VMEM((20, 2, 16, 256), F32),
        pltpu.VMEM((256, 768), BF),
        pltpu.VMEM((256, 768), BF),
        pltpu.VMEM((128, 768), BF),
        pltpu.VMEM((128, 768), BF),
    ],
    flops=1_000_000_000,
    name="rows",
)
finish_call = call(
    finish_kernel, struct((128, 256)), [ANY] + [VMEM] * 4, [INTS, pltpu.SemaphoreType.DMA((1,))], flops=300_000_000, name="finish"
)


def routes(shards):
    pairs = [(i, i + 1) for i in range(1, shards - 1, 2)]
    near = pairs + [(b, a) for a, b in pairs]
    far = [(i, i + 2) for i in range(0, shards - 2, 2)] + [(i, i - 2) for i in range(3, shards, 2)]
    pairs = [(i, i + 1) for i in range(0, shards, 2)]
    inner = pairs + [(b, a) for a, b in pairs]
    onward = [(i, (i // 2 + 1) * 2 + 1 - i % 2) for i in range(shards - 2)]
    ring = [(a, b) for a, b in onward if a // 2 % 2 == 0]
    cross = [(a, b) for a, b in onward if a // 2 % 2 == 1]
    return near, far, inner, ring + [(b, a) for a, b in ring], cross + [(b, a) for a, b in cross]


def groups(shards, columns):
    return [
        [(2 * team + (side ^ team % 2)) * columns + c for c in range(columns) for side in range(2)] for team in range(shards // 2)
    ]


def integers(node_count):
    shards = node_count.shape[0]
    team, side = lax.axis_index("team"), lax.axis_index("r")
    here = 2 * team + side
    row = jnp.arange(16, dtype=jnp.int32)[:, None]
    column = jnp.arange(shards, dtype=jnp.int32)[None, :]
    near = jnp.clip(here + row - (COUNTS + 2), 0, shards - 1)
    wanted = (
        (row == TOTAL)
        | ((row == TEAM_BEGIN) & (column < 2 * team))
        | ((row == HERE_BEGIN) & (column < here))
        | ((row >= COUNTS) & (row < ODD) & (column == near))
    )
    sums = jnp.sum(jnp.where(wanted, node_count[None, :], 0), axis=1)
    return sums + jnp.where(row[:, 0] == SIDE, side, 0) + jnp.where(row[:, 0] == ODD, team & 1, 0)


def on_device(densities, hamiltonian, couplings, gamma, coeff, node_count):
    hier = ("team", "r")
    shards = node_count.shape[0]
    everyone = ("team", "r", "col")
    lists = groups(shards, lax.axis_size("col"))
    near, far, inner, ring, cross = routes(shards)

    def exchange(v):
        return lax.all_to_all(v, everyone, 0, 0, axis_index_groups=lists, tiled=True)

    ints = integers(node_count)
    wide = jnp.broadcast_to(ints[:, None], (16, 128))
    reals = jnp.concatenate([gamma, coeff.reshape(4), jnp.sqrt(jnp.arange(ROOTS, dtype=F32))])
    sent, x = lax.optimization_barrier((own_call(densities.reshape(128, 256)), densities))
    got = exchange(sent)
    p1 = lax.ppermute(x, hier, near)
    own, ring_edge, cross_edge = edge_call(wide, got)
    cross_got = lax.ppermute(cross_edge, hier, cross)
    ring_got = lax.ppermute(ring_edge, hier, ring)
    own, p1, x, hamiltonian, couplings = lax.optimization_barrier((own, p1, x, hamiltonian, couplings))
    vhi, vlo, hhi, hlo = weights_call(hamiltonian, couplings)
    wide_reals = jnp.broadcast_to(reals[:8, None], (8, 128))
    pair, edge = pair_call(ints, x, p1)
    own, pair, edge = lax.optimization_barrier((own, pair, edge))
    back_sent = column_call(wide, wide_reals, own, cross_got, ring_got, vhi, vlo)
    back_sent, pair, edge = lax.optimization_barrier((back_sent, pair, edge))
    back_got = exchange(back_sent)
    p2 = lax.ppermute(edge, hier, far)
    pair = lax.ppermute(pair, hier, inner)
    base = row_call(ints, reals, x, p1, p2, pair, vhi, vlo)
    out = finish_call(ints, back_got, base, hhi, hlo)
    return out.reshape(4, 2, 16, 256)


def solution(mesh):
    devices = mesh.devices
    inside = Mesh(devices.reshape(devices.shape[0] // 2, 2, devices.shape[1]), ("team", "r", "col"))
    spec = P(("team", "r"), None, "col", None)
    return jax.shard_map(
        on_device,
        mesh=inside,
        in_specs=(spec, P(), P(), P(), P(), P()),
        out_specs=spec,
        check_vma=False,
    )
```

```python
import jax
import jax.numpy as jnp
from jax import lax
from jax.experimental import pallas as pl
from jax.experimental.pallas import tpu as pltpu
from jax.sharding import Mesh, PartitionSpec as P

STEP = 0.2
HALF2 = 0.5 * STEP * STEP
SLOTS = 4
TOTAL, TEAM_BEGIN, HERE_BEGIN, SIDE, COUNTS, ODD = 0, 1, 2, 3, 4, 9
ROOTS = 72
BF = jnp.bfloat16
F32 = jnp.float32


def split(v):
    hi = v.astype(BF)
    return hi, (v - hi.astype(F32)).astype(BF)


def dot(a, b):
    return jnp.dot(a, b, preferred_element_type=F32)


def granules(vs):
    lane = lax.broadcasted_iota(jnp.int32, vs[0].shape, 1) // 16
    turned = [vs[0]] + [pltpu.roll(vs[k], 16 * k, 1) for k in range(1, 8)]
    cur = [turned[-k % 8] for k in range(8)]
    for bit in (1, 2, 4):
        pick = (lane & bit) != 0
        cur = [jnp.where(pick, cur[(m - bit) % 8], cur[m]) for m in range(8)]
    return [cur[0]] + [pltpu.roll(cur[m], 128 - 16 * m, 1) for m in range(1, 8)]


def once(method):
    def cached(self, p):
        key = (method.__name__, p)
        if key not in self.memo:
            self.memo[key] = method(self, p)
        return self.memo[key]

    return cached


class Nodes:
    def __init__(self, total, begin, reals, root):
        self.memo = {}
        self.live = (total >> 1) << 1
        self.begin = begin
        self.base = begin - 4
        self.gamma = (reals[0], reals[1])
        self.re = (reals[2], reals[4])
        self.im = (reals[3], reals[5])
        self.root = root

    @once
    def up(self, p):
        g = self.base + p
        return self.root((g >> 1) + 1) * jnp.where((g >= 0) & (g + 2 < self.live), 1.0, 0.0)

    @once
    def down(self, p):
        g = self.base + p
        return self.root(g >> 1) * jnp.where((g >= 2) & (g < self.live), 1.0, 0.0)

    @once
    def twist(self, p):
        g = self.base + p
        n = (g >> 1).astype(F32)
        ok = (g >= 0) & (g < self.live)
        return jnp.where(ok & (g + 2 < self.live), n + 1.0, 0.0) - jnp.where(ok & (g >= 2), n, 0.0)

    @once
    def even(self, p):
        g = self.base + p
        return jnp.where((g >= 0) & (g < self.live) & ((g & 1) == 0), 1.0, 0.0).astype(F32)

    @once
    def odd(self, p):
        g = self.base + p
        return jnp.where((g >= 0) & (g < self.live) & ((g & 1) == 1), 1.0, 0.0).astype(F32)

    @once
    def damp(self, p):
        g = self.base + p
        n0 = (g >> 1).astype(F32)
        n1 = (g & 1).astype(F32)
        return n0 * self.gamma[0] + n1 * self.gamma[1]


def scaled(s, v):
    return (s * v[0], s * v[1])


def plus(a, b):
    return (a[0] + b[0], a[1] + b[1])


def times(re, im, v):
    return (re * v[0] - im * v[1], re * v[1] + im * v[0])


def both(nodes, x, p, re, im):
    r = plus(scaled(nodes.up(p), x[p + 2]), scaled(re * nodes.down(p), x[p - 2]))
    t = scaled(im * nodes.down(p), x[p - 2])
    return (r[0] - t[1], r[1] + t[0]), (r[0] + t[1], r[1] - t[0])


def both1(nodes, x, p, re, im):
    r = plus(scaled(nodes.even(p), x[p + 1]), scaled(re * nodes.odd(p), x[p - 1]))
    t = scaled(im * nodes.odd(p), x[p - 1])
    return (r[0] - t[1], r[1] + t[0]), (r[0] + t[1], r[1] - t[0])


def first_order(nodes, x, p, re, im):
    here = nodes.damp(p)

    def w(q):
        return STEP - HALF2 * (here + nodes.damp(q))

    zero = scaled(w(p), x[p])
    up, down = scaled(w(p + 2) * nodes.up(p), x[p + 2]), scaled(w(p - 2) * nodes.down(p), x[p - 2])
    one = plus(up, times(re[0], im[0], down))
    up, down = scaled(w(p + 1) * nodes.even(p), x[p + 1]), scaled(w(p - 1) * nodes.odd(p), x[p - 1])
    two = plus(up, times(re[1], im[1], down))
    return zero, one, two


def put(hi_ref, lo_ref, col, j, rows, v):
    hi, lo = split(jnp.concatenate([v[0], v[1]], axis=0))
    at = pl.ds(j * rows, rows)
    hi_ref[at, 256 * col : 256 * col + 256] = hi
    lo_ref[at, 256 * col : 256 * col + 256] = lo


def product(hi, lo, ghi, glo):
    return dot(hi, ghi) + dot(lo, ghi) + dot(hi, glo)


def times_weights(hi_ref, lo_ref, ghi_ref, glo_ref):
    return product(hi_ref[...], lo_ref[...], ghi_ref[...], glo_ref[...])


def weights_kernel(h_ref, q_ref, vhi, vlo, hhi, hlo):
    for b in range(3):
        hi, lo = split(h_ref[...] if b == 0 else q_ref[b - 1])
        vhi[256 * b : 256 * b + 256, :] = hi
        vlo[256 * b : 256 * b + 256, :] = lo
        hhi[:, 256 * b : 256 * b + 256] = hi
        hlo[:, 256 * b : 256 * b + 256] = lo


def own_kernel(x_ref, o_ref):
    o_ref[...] = x_ref[...].T.reshape(32, 8, 128)


def fetch(pairs, sem):
    copies = [pltpu.make_async_copy(source, target, sem.at[i]) for i, (source, target) in enumerate(pairs)]
    for copy in copies:
        copy.start()
    return copies


def taken(ref, i):
    return ref[i : i + 1, 0:1][0, 0]


def edge_kernel(wide_ref, got_ref, own_ref, ring_ref, cross_ref, y_ref):
    side, before, here, after, odd = (taken(wide_ref, i) for i in (SIDE, COUNTS + 1, COUNTS + 2, COUNTS + 3, ODD))
    own, other = jnp.where(side == 0, here, before), jnp.where(side == 0, after, here)
    for place in range(2):
        vs = []
        for low in range(8):
            vs.append(jnp.concatenate([got_ref[(8 * high + low) * 2 + place] for high in range(2)], axis=0))
        for m, v in enumerate(granules(vs)):
            y_ref[SLOTS * place + m // 2, m % 2] = jnp.concatenate([v[:8], v[8:]], axis=1)

    def node(j):
        return y_ref[jnp.where(j < own, SLOTS * odd + j, SLOTS * (1 - odd) + jnp.clip(j - own, 0, SLOTS - 1))]

    for j in range(8):
        own_ref[j] = node(j)
    behind, ahead = jnp.where(odd == 0, own + other - 4, 0), jnp.where(odd == 0, 0, own + other - 4)
    for j in range(4):
        ring_ref[j] = node(behind + j)
        cross_ref[j] = node(ahead + j)


def pair_kernel(ints_ref, x_ref, near_ref, o_ref, far_ref):
    far_ref[...] = x_ref[pl.ds(jnp.where(ints_ref[SIDE] == 0, ints_ref[COUNTS + 2] - 2, 0), 2)]
    o_ref[0:4] = x_ref[...]
    o_ref[4:6] = near_ref[pl.ds(jnp.where(ints_ref[SIDE] == 0, ints_ref[COUNTS + 1] - 2, 0), 2)]


def column_kernel(
    wide_ref, reals_ref, own_ref, ring_ref, cross_ref, ghi_ref, glo_ref, o_ref, y_ref, hi_ref, lo_ref, hi2_ref, lo2_ref, z_ref, send_ref, out_sem
):
    total, begin, side, before, here, after, odd = (
        taken(wide_ref, i) for i in (TOTAL, TEAM_BEGIN, SIDE, COUNTS + 1, COUNTS + 2, COUNTS + 3, ODD)
    )
    reals = [taken(reals_ref, i) for i in range(6)]
    own, other = jnp.where(side == 0, here, before), jnp.where(side == 0, after, here)

    def root(n):
        return jnp.sqrt(jnp.full((8, 256), jnp.maximum(n, 0).astype(F32)))

    nodes = Nodes(total, begin, reals, root)
    re, im = nodes.re, nodes.im
    y_ref[4:12] = own_ref[...]
    y_ref[12:16] = ring_ref[...]
    y_ref[pl.ds(jnp.where(odd == 0, 4 + own + other, 0), 4)] = ring_ref[...]
    y_ref[pl.ds(jnp.where(odd == 0, 0, 4 + own + other), 4)] = cross_ref[...]
    x = []
    for p in range(16):
        v = y_ref[p]
        x.append((v[0], v[1]))
    for p in range(2, 14):
        put(hi_ref, lo_ref, 0, p - 2, 16, x[p])
        put(hi_ref, lo_ref, 1, p - 2, 16, both(nodes, x, p, re[0], im[0])[0])
        put(hi_ref, lo_ref, 2, p - 2, 16, both1(nodes, x, p, re[1], im[1])[0])
    sums = times_weights(hi_ref, lo_ref, ghi_ref, glo_ref)
    hi, lo = hi_ref[32:160, :256], lo_ref[32:160, :256]
    alone = [product(hi, lo, ghi_ref[256 * b : 256 * b + 256, :], glo_ref[256 * b : 256 * b + 256, :]) for b in (1, 2)]
    s = {p: (sums[16 * p - 32 : 16 * p - 24], sums[16 * p - 24 : 16 * p - 16]) for p in range(2, 14)}
    for j in range(8):
        p = j + 4
        left, right = zip(both(nodes, s, p, re[0], im[0]), both1(nodes, s, p, re[1], im[1]))
        for col, (v, t) in enumerate(zip(first_order(nodes, x, p, re, im), (s[p], *left))):
            put(hi2_ref, lo2_ref, col, j, 16, (v[1] - HALF2 * t[0], -v[0] - HALF2 * t[1]))
        z_ref[1, j] = (2.0 * HALF2) * sums[16 * j + 32 : 16 * j + 48].reshape(2, 8, 256)
        for b, twist in enumerate((nodes.twist(p), nodes.even(p) - nodes.odd(p))):
            by = im[b] * twist
            z_ref[2 + b, j, 0] = (2.0 * HALF2) * (right[b][0] + by * alone[b][16 * j + 8 : 16 * j + 16])
            z_ref[2 + b, j, 1] = (2.0 * HALF2) * (right[b][1] - by * alone[b][16 * j : 16 * j + 8])

    def send(z):
        for r in range(2):
            vs = []
            for m in range(8):
                v = z_ref[z, m // 2 if r == 0 else own + m // 2, m % 2]
                vs.append(jnp.concatenate([v[:, :128], v[:, 128:]], axis=0))
            for low, v in enumerate(granules(vs)):
                for high in range(2):
                    send_ref[z, (8 * high + low) * 2 + (odd if r == 0 else 1 - odd)] = v[8 * high : 8 * high + 8]
        copy = pltpu.make_async_copy(send_ref.at[z], o_ref.at[:, 8 * z : 8 * z + 8], out_sem.at[z])
        copy.start()
        return copy

    last = times_weights(hi2_ref, lo2_ref, ghi_ref, glo_ref)
    copies = [send(z) for z in range(1, 4)]
    z_ref[0] = last.reshape(8, 2, 8, 256)
    for copy in [*copies, send(0)]:
        copy.wait()


def row_kernel(
    ints_ref, reals_ref, x_ref, p1_ref, p2_ref, pair_ref, ghi_ref, glo_ref, o_ref, w_ref, hi_ref, lo_ref, hi2_ref, lo2_ref
):

    def root(n):
        return reals_ref[jnp.clip(n, 0, ROOTS - 1) + 6]

    nodes = Nodes(ints_ref[TOTAL], ints_ref[HERE_BEGIN], [reals_ref[i] for i in range(6)], root)
    re, im = nodes.re, (-nodes.im[0], -nodes.im[1])
    up = ints_ref[SIDE]
    farther, below, own, above = (ints_ref[COUNTS + i] for i in range(4))
    w_ref[8:12] = x_ref[...]
    w_ref[pl.ds(4 + 8 * up, 4)] = p1_ref[...]
    w_ref[pl.ds(jnp.where(up == 0, farther - 2, 16), 2)] = p2_ref[...]
    w_ref[pl.ds(12 - 8 * up, 4)] = pair_ref[0:4]
    w_ref[pl.ds(jnp.where(up == 0, 16, farther - 2), 2)] = pair_ref[4:6]

    def slot(p):
        j = p - 4
        if j < 0:
            return jnp.where(j + below >= 0, 4 + j + below, farther + j + below)
        return jnp.where(j < own, 8 + j, jnp.where(j < own + above, 12 + j - own, jnp.minimum(16 + j - own - above, 19)))

    x = []
    for p in range(12):
        v = w_ref[slot(p)]
        x.append((v[0], v[1]))
    for p in range(2, 10):
        put(hi_ref, lo_ref, 0, p - 2, 32, x[p])
        put(hi_ref, lo_ref, 1, p - 2, 32, both(nodes, x, p, re[0], im[0])[0])
        put(hi_ref, lo_ref, 2, p - 2, 32, both1(nodes, x, p, re[1], im[1])[0])
    sums = times_weights(hi_ref, lo_ref, ghi_ref, glo_ref)
    s = {p: (sums[32 * p - 64 : 32 * p - 48], sums[32 * p - 48 : 32 * p - 32]) for p in range(2, 10)}
    for j in range(4):
        p = j + 4
        mixed = (s[p], both(nodes, s, p, re[0], im[0])[0], both1(nodes, s, p, re[1], im[1])[0])
        for col, (v, t) in enumerate(zip(first_order(nodes, x, p, re, im), mixed)):
            put(hi2_ref, lo2_ref, col, j, 32, (-v[1] - HALF2 * t[0], v[0] - HALF2 * t[1]))
    right = times_weights(hi2_ref, lo2_ref, ghi_ref, glo_ref)
    for j in range(4):
        d = nodes.damp(j + 4)
        keep = 1.0 - STEP * d + HALF2 * d * d
        old = x_ref[j].reshape(32, 256)
        live = (j < own) & (nodes.begin + j < nodes.live)
        o_ref[32 * j : 32 * j + 32, :] = jnp.where(live, keep * old + right[32 * j : 32 * j + 32], old)


def finish_kernel(ints_in, got_ref, base_ref, ghi_ref, glo_ref, o_ref, ints_ref, sem):
    fetched = fetch([(ints_in, ints_ref)], sem)
    his, los = [], []
    for z in range(1, 4):
        hi, lo = split(got_ref[:, 8 * z : 8 * z + 8, :].reshape(256, 128))
        his.append(hi)
        los.append(lo)
    hi, lo = jnp.concatenate(his, axis=0), jnp.concatenate(los, axis=0)
    g = ghi_ref[...]
    out = dot(g, hi) + dot(g, lo) + dot(glo_ref[...], hi) + got_ref[:, :8, :].reshape(256, 128)
    out = out.T
    for copy in fetched:
        copy.wait()
    own, begin, limit = ints_ref[COUNTS + 2], ints_ref[HERE_BEGIN], (ints_ref[TOTAL] >> 1) << 1
    for j in range(4):
        live = (j < own) & (begin + j < limit)
        rows = slice(32 * j, 32 * j + 32)
        o_ref[rows, :] = base_ref[rows, :] + jnp.where(live, out[rows], 0.0)


SMEM = pl.BlockSpec(memory_space=pltpu.SMEM)
VMEM = pl.BlockSpec(memory_space=pltpu.VMEM)
ANY = pl.BlockSpec(memory_space=pl.ANY)


def call(kernel, outs, specs, scratch=(), flops=1_000_000, name=None, out_specs=None, aliases=None):
    return pl.pallas_call(
        kernel,
        out_shape=outs,
        in_specs=specs,
        out_specs=out_specs or jax.tree.map(lambda _: VMEM, outs),
        input_output_aliases=aliases or {},
        scratch_shapes=list(scratch),
        compiler_params=pltpu.CompilerParams(vmem_limit_bytes=48 * 1024 * 1024),
        cost_estimate=pl.CostEstimate(flops=flops, bytes_accessed=4_000_000, transcendentals=0),
        name=name,
    )


def struct(shape, dtype=F32):
    return jax.ShapeDtypeStruct(shape, dtype)


weights_call = call(
    weights_kernel,
    (struct((768, 256), BF), struct((768, 256), BF), struct((256, 768), BF), struct((256, 768), BF)),
    [VMEM] * 2,
    name="weights",
)
own_call = call(own_kernel, struct((32, 8, 128)), [VMEM], name="own")
INTS = pltpu.SMEM((16,), jnp.int32)
edge_call = call(
    edge_kernel,
    (struct((8, 2, 8, 256)), struct((4, 2, 8, 256)), struct((4, 2, 8, 256))),
    [VMEM] * 2,
    [pltpu.VMEM((8, 2, 8, 256), F32)],
    name="edge",
)
pair_call = call(pair_kernel, (struct((6, 2, 16, 256)), struct((2, 2, 16, 256))), [SMEM] + [VMEM] * 2, name="pair")
column_call = call(
    column_kernel,
    struct((32, 32, 128)),
    [VMEM] * 7,
    [
        pltpu.VMEM((16, 2, 8, 256), F32),
        pltpu.VMEM((192, 768), BF),
        pltpu.VMEM((192, 768), BF),
        pltpu.VMEM((128, 768), BF),
        pltpu.VMEM((128, 768), BF),
        pltpu.VMEM((4, 8, 2, 8, 256), F32),
        pltpu.VMEM((4, 32, 8, 128), F32),
        pltpu.SemaphoreType.DMA((4,)),
    ],
    flops=1_000_000_000,
    out_specs=ANY,
    name="columns",
)
row_call = call(
    row_kernel,
    struct((128, 256)),
    [SMEM] * 2 + [VMEM] * 6,
    [
        pltpu.VMEM((20, 2, 16, 256), F32),
        pltpu.VMEM((256, 768), BF),
        pltpu.VMEM((256, 768), BF),
        pltpu.VMEM((128, 768), BF),
        pltpu.VMEM((128, 768), BF),
    ],
    flops=1_000_000_000,
    name="rows",
)
finish_call = call(
    finish_kernel, struct((128, 256)), [ANY] + [VMEM] * 4, [INTS, pltpu.SemaphoreType.DMA((1,))], flops=300_000_000, name="finish"
)


def routes(shards):
    pairs = [(i, i + 1) for i in range(1, shards - 1, 2)]
    near = pairs + [(b, a) for a, b in pairs]
    far = [(i, i + 2) for i in range(0, shards - 2, 2)] + [(i, i - 2) for i in range(3, shards, 2)]
    pairs = [(i, i + 1) for i in range(0, shards, 2)]
    inner = pairs + [(b, a) for a, b in pairs]
    onward = [(i, (i // 2 + 1) * 2 + 1 - i % 2) for i in range(shards - 2)]
    ring = [(a, b) for a, b in onward if a // 2 % 2 == 0]
    cross = [(a, b) for a, b in onward if a // 2 % 2 == 1]
    return near, far, inner, ring + [(b, a) for a, b in ring], cross + [(b, a) for a, b in cross]


def groups(shards, columns):
    return [
        [(2 * team + (side ^ team % 2)) * columns + c for c in range(columns) for side in range(2)] for team in range(shards // 2)
    ]


def integers(node_count):
    shards = node_count.shape[0]
    team, side = lax.axis_index("team"), lax.axis_index("r")
    here = 2 * team + side
    row = jnp.arange(16, dtype=jnp.int32)[:, None]
    column = jnp.arange(shards, dtype=jnp.int32)[None, :]
    near = jnp.clip(here + row - (COUNTS + 2), 0, shards - 1)
    wanted = (
        (row == TOTAL)
        | ((row == TEAM_BEGIN) & (column < 2 * team))
        | ((row == HERE_BEGIN) & (column < here))
        | ((row >= COUNTS) & (row < ODD) & (column == near))
    )
    sums = jnp.sum(jnp.where(wanted, node_count[None, :], 0), axis=1)
    return sums + jnp.where(row[:, 0] == SIDE, side, 0) + jnp.where(row[:, 0] == ODD, team & 1, 0)


def on_device(densities, hamiltonian, couplings, gamma, coeff, node_count):
    hier = ("team", "r")
    shards = node_count.shape[0]
    everyone = ("team", "r", "col")
    lists = groups(shards, lax.axis_size("col"))
    near, far, inner, ring, cross = routes(shards)

    def exchange(v):
        return lax.all_to_all(v, everyone, 0, 0, axis_index_groups=lists, tiled=True)

    ints = integers(node_count)
    wide = jnp.broadcast_to(ints[:, None], (16, 128))
    reals = jnp.concatenate([gamma, coeff.reshape(4), jnp.sqrt(jnp.arange(ROOTS, dtype=F32))])
    sent, x = lax.optimization_barrier((own_call(densities.reshape(128, 256)), densities))
    got = exchange(sent)
    p1 = lax.ppermute(x, hier, near)
    own, ring_edge, cross_edge = edge_call(wide, got)
    cross_got = lax.ppermute(cross_edge, hier, cross)
    ring_got = lax.ppermute(ring_edge, hier, ring)
    own, p1, x, hamiltonian, couplings = lax.optimization_barrier((own, p1, x, hamiltonian, couplings))
    vhi, vlo, hhi, hlo = weights_call(hamiltonian, couplings)
    wide_reals = jnp.broadcast_to(reals[:8, None], (8, 128))
    pair, edge = pair_call(ints, x, p1)
    own, pair, edge = lax.optimization_barrier((own, pair, edge))
    back_sent = column_call(wide, wide_reals, own, ring_got, cross_got, vhi, vlo)
    back_sent, pair, edge = lax.optimization_barrier((back_sent, pair, edge))
    back_got = exchange(back_sent)
    p2 = lax.ppermute(edge, hier, far)
    pair = lax.ppermute(pair, hier, inner)
    base = row_call(ints, reals, x, p1, p2, pair, vhi, vlo)
    out = finish_call(ints, back_got, base, hhi, hlo)
    return out.reshape(4, 2, 16, 256)


def solution(mesh):
    devices = mesh.devices
    inside = Mesh(devices.reshape(devices.shape[0] // 2, 2, devices.shape[1]), ("team", "r", "col"))
    spec = P(("team", "r"), None, "col", None)
    return jax.shard_map(
        on_device,
        mesh=inside,
        in_specs=(spec, P(), P(), P(), P(), P()),
        out_specs=spec,
        check_vma=False,
    )
```

```python
import jax
import jax.numpy as jnp
from jax import lax
from jax.experimental import pallas as pl
from jax.experimental.pallas import tpu as pltpu
from jax.sharding import Mesh, PartitionSpec as P

STEP = 0.2
HALF2 = 0.5 * STEP * STEP
SLOTS = 4
TOTAL, TEAM_BEGIN, HERE_BEGIN, SIDE, COUNTS, ODD = 0, 1, 2, 3, 4, 9
ROOTS = 72
BF = jnp.bfloat16
F32 = jnp.float32


def split(v):
    hi = v.astype(BF)
    return hi, (v - hi.astype(F32)).astype(BF)


def dot(a, b):
    return jnp.dot(a, b, preferred_element_type=F32)


def granules(vs):
    lane = lax.broadcasted_iota(jnp.int32, vs[0].shape, 1) // 16
    turned = [vs[0]] + [pltpu.roll(vs[k], 16 * k, 1) for k in range(1, 8)]
    cur = [turned[-k % 8] for k in range(8)]
    for bit in (1, 2, 4):
        pick = (lane & bit) != 0
        cur = [jnp.where(pick, cur[(m - bit) % 8], cur[m]) for m in range(8)]
    return [cur[0]] + [pltpu.roll(cur[m], 128 - 16 * m, 1) for m in range(1, 8)]


def once(method):
    def cached(self, p):
        key = (method.__name__, p)
        if key not in self.memo:
            self.memo[key] = method(self, p)
        return self.memo[key]

    return cached


class Nodes:
    def __init__(self, total, begin, reals, root):
        self.memo = {}
        self.live = (total >> 1) << 1
        self.begin = begin
        self.base = begin - 4
        self.gamma = (reals[0], reals[1])
        self.re = (reals[2], reals[4])
        self.im = (reals[3], reals[5])
        self.root = root

    @once
    def up(self, p):
        g = self.base + p
        return self.root((g >> 1) + 1) * jnp.where((g >= 0) & (g + 2 < self.live), 1.0, 0.0)

    @once
    def down(self, p):
        g = self.base + p
        return self.root(g >> 1) * jnp.where((g >= 2) & (g < self.live), 1.0, 0.0)

    @once
    def twist(self, p):
        g = self.base + p
        n = (g >> 1).astype(F32)
        ok = (g >= 0) & (g < self.live)
        return jnp.where(ok & (g + 2 < self.live), n + 1.0, 0.0) - jnp.where(ok & (g >= 2), n, 0.0)

    @once
    def even(self, p):
        g = self.base + p
        return jnp.where((g >= 0) & (g < self.live) & ((g & 1) == 0), 1.0, 0.0).astype(F32)

    @once
    def odd(self, p):
        g = self.base + p
        return jnp.where((g >= 0) & (g < self.live) & ((g & 1) == 1), 1.0, 0.0).astype(F32)

    @once
    def damp(self, p):
        g = self.base + p
        n0 = (g >> 1).astype(F32)
        n1 = (g & 1).astype(F32)
        return n0 * self.gamma[0] + n1 * self.gamma[1]


def scaled(s, v):
    return (s * v[0], s * v[1])


def plus(a, b):
    return (a[0] + b[0], a[1] + b[1])


def times(re, im, v):
    return (re * v[0] - im * v[1], re * v[1] + im * v[0])


def both(nodes, x, p, re, im):
    r = plus(scaled(nodes.up(p), x[p + 2]), scaled(re * nodes.down(p), x[p - 2]))
    t = scaled(im * nodes.down(p), x[p - 2])
    return (r[0] - t[1], r[1] + t[0]), (r[0] + t[1], r[1] - t[0])


def both1(nodes, x, p, re, im):
    r = plus(scaled(nodes.even(p), x[p + 1]), scaled(re * nodes.odd(p), x[p - 1]))
    t = scaled(im * nodes.odd(p), x[p - 1])
    return (r[0] - t[1], r[1] + t[0]), (r[0] + t[1], r[1] - t[0])


def first_order(nodes, x, p, re, im):
    here = nodes.damp(p)

    def w(q):
        return STEP - HALF2 * (here + nodes.damp(q))

    zero = scaled(w(p), x[p])
    up, down = scaled(w(p + 2) * nodes.up(p), x[p + 2]), scaled(w(p - 2) * nodes.down(p), x[p - 2])
    one = plus(up, times(re[0], im[0], down))
    up, down = scaled(w(p + 1) * nodes.even(p), x[p + 1]), scaled(w(p - 1) * nodes.odd(p), x[p - 1])
    two = plus(up, times(re[1], im[1], down))
    return zero, one, two


def put(hi_ref, lo_ref, col, j, rows, v):
    hi, lo = split(jnp.concatenate([v[0], v[1]], axis=0))
    at = pl.ds(j * rows, rows)
    hi_ref[at, 256 * col : 256 * col + 256] = hi
    lo_ref[at, 256 * col : 256 * col + 256] = lo


def product(hi, lo, ghi, glo):
    rows = hi.shape[0]
    both_parts = dot(jnp.concatenate([hi, lo], axis=0), ghi)
    return both_parts[:rows] + both_parts[rows:] + dot(hi, glo)


def times_weights(hi_ref, lo_ref, ghi_ref, glo_ref):
    return product(hi_ref[...], lo_ref[...], ghi_ref[...], glo_ref[...])


def weights_kernel(h_ref, q_ref, vhi, vlo, hhi, hlo):
    for b in range(3):
        hi, lo = split(h_ref[...] if b == 0 else q_ref[b - 1])
        vhi[256 * b : 256 * b + 256, :] = hi
        vlo[256 * b : 256 * b + 256, :] = lo
        hhi[:, 256 * b : 256 * b + 256] = hi
        hlo[:, 256 * b : 256 * b + 256] = lo


def own_kernel(x_ref, o_ref, v_ref, t_ref, in_sem, out_sem):
    copies = [pltpu.make_async_copy(x_ref.at[i], v_ref.at[i], in_sem.at[i]) for i in range(4)]
    for copy in copies:
        copy.start()
    for copy in copies:
        copy.wait()
    t_ref[...] = v_ref[...].reshape(128, 256).T.reshape(32, 8, 128)
    copies = [pltpu.make_async_copy(t_ref.at[pl.ds(8 * i, 8)], o_ref.at[pl.ds(8 * i, 8)], out_sem.at[i]) for i in range(4)]
    for copy in copies:
        copy.start()
    for copy in copies:
        copy.wait()


def fetch(pairs, sem):
    copies = [pltpu.make_async_copy(source, target, sem.at[i]) for i, (source, target) in enumerate(pairs)]
    for copy in copies:
        copy.start()
    return copies


def taken(ref, i):
    return ref[i : i + 1, 0:1][0, 0]


def edge_kernel(wide_ref, got_ref, own_ref, ring_ref, cross_ref, y_ref):
    side, before, here, after, odd = (taken(wide_ref, i) for i in (SIDE, COUNTS + 1, COUNTS + 2, COUNTS + 3, ODD))
    own, other = jnp.where(side == 0, here, before), jnp.where(side == 0, after, here)
    for place in range(2):
        vs = []
        for low in range(8):
            vs.append(jnp.concatenate([got_ref[(8 * high + low) * 2 + place] for high in range(2)], axis=0))
        for m, v in enumerate(granules(vs)):
            y_ref[SLOTS * place + m // 2, m % 2] = jnp.concatenate([v[:8], v[8:]], axis=1)

    def node(j):
        return y_ref[jnp.where(j < own, SLOTS * odd + j, SLOTS * (1 - odd) + jnp.clip(j - own, 0, SLOTS - 1))]

    for j in range(8):
        own_ref[j] = node(j)
    behind, ahead = jnp.where(odd == 0, own + other - 4, 0), jnp.where(odd == 0, 0, own + other - 4)
    for j in range(4):
        ring_ref[j] = node(behind + j)
        cross_ref[j] = node(ahead + j)


def pair_kernel(ints_ref, x_ref, near_ref, o_ref, far_ref):
    far_ref[...] = x_ref[pl.ds(jnp.where(ints_ref[SIDE] == 0, ints_ref[COUNTS + 2] - 2, 0), 2)]
    o_ref[0:4] = x_ref[...]
    o_ref[4:6] = near_ref[pl.ds(jnp.where(ints_ref[SIDE] == 0, ints_ref[COUNTS + 1] - 2, 0), 2)]


def column_kernel(
    wide_ref, reals_ref, own_ref, cross_ref, ring_ref, ghi_ref, glo_ref, o_ref, y_ref, hi_ref, lo_ref, hi2_ref, lo2_ref, z_ref, send_ref, out_sem
):
    total, begin, side, before, here, after, odd = (
        taken(wide_ref, i) for i in (TOTAL, TEAM_BEGIN, SIDE, COUNTS + 1, COUNTS + 2, COUNTS + 3, ODD)
    )
    reals = [taken(reals_ref, i) for i in range(6)]
    own, other = jnp.where(side == 0, here, before), jnp.where(side == 0, after, here)

    def root(n):
        return jnp.sqrt(jnp.full((8, 256), jnp.maximum(n, 0).astype(F32)))

    nodes = Nodes(total, begin, reals, root)
    re, im = nodes.re, nodes.im
    y_ref[4:12] = own_ref[...]
    y_ref[12:16] = ring_ref[...]
    y_ref[pl.ds(jnp.where(odd == 0, 4 + own + other, 0), 4)] = ring_ref[...]
    y_ref[pl.ds(jnp.where(odd == 0, 0, 4 + own + other), 4)] = cross_ref[...]
    x = []
    for p in range(16):
        v = y_ref[p]
        x.append((v[0], v[1]))
    for p in range(2, 14):
        put(hi_ref, lo_ref, 0, p - 2, 16, x[p])
        put(hi_ref, lo_ref, 1, p - 2, 16, both(nodes, x, p, re[0], im[0])[0])
        put(hi_ref, lo_ref, 2, p - 2, 16, both1(nodes, x, p, re[1], im[1])[0])
    sums = times_weights(hi_ref, lo_ref, ghi_ref, glo_ref)
    hi, lo = hi_ref[32:160, :256], lo_ref[32:160, :256]
    alone = [product(hi, lo, ghi_ref[256 * b : 256 * b + 256, :], glo_ref[256 * b : 256 * b + 256, :]) for b in (1, 2)]
    s = {p: (sums[16 * p - 32 : 16 * p - 24], sums[16 * p - 24 : 16 * p - 16]) for p in range(2, 14)}
    for j in range(8):
        p = j + 4
        left, right = zip(both(nodes, s, p, re[0], im[0]), both1(nodes, s, p, re[1], im[1]))
        for col, (v, t) in enumerate(zip(first_order(nodes, x, p, re, im), (s[p], *left))):
            put(hi2_ref, lo2_ref, col, j, 16, (v[1] - HALF2 * t[0], -v[0] - HALF2 * t[1]))
        z_ref[1, j] = (2.0 * HALF2) * sums[16 * j + 32 : 16 * j + 48].reshape(2, 8, 256)
        for b, twist in enumerate((nodes.twist(p), nodes.even(p) - nodes.odd(p))):
            by = im[b] * twist
            z_ref[2 + b, j, 0] = (2.0 * HALF2) * (right[b][0] + by * alone[b][16 * j + 8 : 16 * j + 16])
            z_ref[2 + b, j, 1] = (2.0 * HALF2) * (right[b][1] - by * alone[b][16 * j : 16 * j + 8])

    def send(z):
        for r in range(2):
            vs = []
            for m in range(8):
                v = z_ref[z, m // 2 if r == 0 else own + m // 2, m % 2]
                vs.append(jnp.concatenate([v[:, :128], v[:, 128:]], axis=0))
            for low, v in enumerate(granules(vs)):
                for high in range(2):
                    send_ref[z, (8 * high + low) * 2 + (odd if r == 0 else 1 - odd)] = v[8 * high : 8 * high + 8]
        copy = pltpu.make_async_copy(send_ref.at[z], o_ref.at[:, 8 * z : 8 * z + 8], out_sem.at[z])
        copy.start()
        return copy

    copies = [send(z) for z in range(1, 4)]
    last = times_weights(hi2_ref, lo2_ref, ghi_ref, glo_ref)
    z_ref[0] = last.reshape(8, 2, 8, 256)
    for copy in [*copies, send(0)]:
        copy.wait()


def row_kernel(
    ints_ref, reals_ref, x_ref, p1_ref, p2_ref, pair_ref, ghi_ref, glo_ref, o_ref, w_ref, hi_ref, lo_ref, hi2_ref, lo2_ref
):

    def root(n):
        return reals_ref[jnp.clip(n, 0, ROOTS - 1) + 6]

    nodes = Nodes(ints_ref[TOTAL], ints_ref[HERE_BEGIN], [reals_ref[i] for i in range(6)], root)
    re, im = nodes.re, (-nodes.im[0], -nodes.im[1])
    up = ints_ref[SIDE]
    farther, below, own, above = (ints_ref[COUNTS + i] for i in range(4))
    w_ref[8:12] = x_ref[...]
    w_ref[pl.ds(4 + 8 * up, 4)] = p1_ref[...]
    w_ref[pl.ds(jnp.where(up == 0, farther - 2, 16), 2)] = p2_ref[...]
    w_ref[pl.ds(12 - 8 * up, 4)] = pair_ref[0:4]
    w_ref[pl.ds(jnp.where(up == 0, 16, farther - 2), 2)] = pair_ref[4:6]

    def slot(p):
        j = p - 4
        if j < 0:
            return jnp.where(j + below >= 0, 4 + j + below, farther + j + below)
        return jnp.where(j < own, 8 + j, jnp.where(j < own + above, 12 + j - own, jnp.minimum(16 + j - own - above, 19)))

    x = []
    for p in range(12):
        v = w_ref[slot(p)]
        x.append((v[0], v[1]))
    for p in range(2, 10):
        put(hi_ref, lo_ref, 0, p - 2, 32, x[p])
        put(hi_ref, lo_ref, 1, p - 2, 32, both(nodes, x, p, re[0], im[0])[0])
        put(hi_ref, lo_ref, 2, p - 2, 32, both1(nodes, x, p, re[1], im[1])[0])
    sums = times_weights(hi_ref, lo_ref, ghi_ref, glo_ref)
    s = {p: (sums[32 * p - 64 : 32 * p - 48], sums[32 * p - 48 : 32 * p - 32]) for p in range(2, 10)}
    for j in range(4):
        p = j + 4
        mixed = (s[p], both(nodes, s, p, re[0], im[0])[0], both1(nodes, s, p, re[1], im[1])[0])
        for col, (v, t) in enumerate(zip(first_order(nodes, x, p, re, im), mixed)):
            put(hi2_ref, lo2_ref, col, j, 32, (-v[1] - HALF2 * t[0], v[0] - HALF2 * t[1]))
    right = times_weights(hi2_ref, lo2_ref, ghi_ref, glo_ref)
    for j in range(4):
        d = nodes.damp(j + 4)
        keep = 1.0 - STEP * d + HALF2 * d * d
        old = x_ref[j].reshape(32, 256)
        live = (j < own) & (nodes.begin + j < nodes.live)
        o_ref[32 * j : 32 * j + 32, :] = jnp.where(live, keep * old + right[32 * j : 32 * j + 32], old)


def finish_kernel(ints_in, got_ref, base_ref, ghi_ref, glo_ref, o_ref, ints_ref, sem):
    fetched = fetch([(ints_in, ints_ref)], sem)
    his, los = [], []
    for z in range(1, 4):
        hi, lo = split(got_ref[:, 8 * z : 8 * z + 8, :].reshape(256, 128))
        his.append(hi)
        los.append(lo)
    hi, lo = jnp.concatenate(his, axis=0), jnp.concatenate(los, axis=0)
    g = ghi_ref[...]
    out = dot(g, hi) + dot(g, lo) + dot(glo_ref[...], hi) + got_ref[:, :8, :].reshape(256, 128)
    out = out.T
    for copy in fetched:
        copy.wait()
    own, begin, limit = ints_ref[COUNTS + 2], ints_ref[HERE_BEGIN], (ints_ref[TOTAL] >> 1) << 1
    for j in range(4):
        live = (j < own) & (begin + j < limit)
        rows = slice(32 * j, 32 * j + 32)
        o_ref[rows, :] = base_ref[rows, :] + jnp.where(live, out[rows], 0.0)


SMEM = pl.BlockSpec(memory_space=pltpu.SMEM)
VMEM = pl.BlockSpec(memory_space=pltpu.VMEM)
ANY = pl.BlockSpec(memory_space=pl.ANY)


def call(kernel, outs, specs, scratch=(), flops=1_000_000, name=None, out_specs=None, aliases=None):
    return pl.pallas_call(
        kernel,
        out_shape=outs,
        in_specs=specs,
        out_specs=out_specs or jax.tree.map(lambda _: VMEM, outs),
        input_output_aliases=aliases or {},
        scratch_shapes=list(scratch),
        compiler_params=pltpu.CompilerParams(vmem_limit_bytes=48 * 1024 * 1024),
        cost_estimate=pl.CostEstimate(flops=flops, bytes_accessed=4_000_000, transcendentals=0),
        name=name,
    )


def struct(shape, dtype=F32):
    return jax.ShapeDtypeStruct(shape, dtype)


weights_call = call(
    weights_kernel,
    (struct((768, 256), BF), struct((768, 256), BF), struct((256, 768), BF), struct((256, 768), BF)),
    [VMEM] * 2,
    name="weights",
)
own_call = call(
    own_kernel,
    struct((32, 8, 128)),
    [ANY],
    [
        pltpu.VMEM((4, 2, 16, 256), F32),
        pltpu.VMEM((32, 8, 128), F32),
        pltpu.SemaphoreType.DMA((4,)),
        pltpu.SemaphoreType.DMA((4,)),
    ],
    out_specs=ANY,
    name="own",
)
INTS = pltpu.SMEM((16,), jnp.int32)
edge_call = call(
    edge_kernel,
    (struct((8, 2, 8, 256)), struct((4, 2, 8, 256)), struct((4, 2, 8, 256))),
    [VMEM] * 2,
    [pltpu.VMEM((8, 2, 8, 256), F32)],
    name="edge",
)
pair_call = call(pair_kernel, (struct((6, 2, 16, 256)), struct((2, 2, 16, 256))), [SMEM] + [VMEM] * 2, name="pair")
column_call = call(
    column_kernel,
    struct((32, 32, 128)),
    [VMEM] * 7,
    [
        pltpu.VMEM((16, 2, 8, 256), F32),
        pltpu.VMEM((192, 768), BF),
        pltpu.VMEM((192, 768), BF),
        pltpu.VMEM((128, 768), BF),
        pltpu.VMEM((128, 768), BF),
        pltpu.VMEM((4, 8, 2, 8, 256), F32),
        pltpu.VMEM((4, 32, 8, 128), F32),
        pltpu.SemaphoreType.DMA((4,)),
    ],
    flops=1_000_000_000,
    out_specs=ANY,
    name="columns",
)
row_call = call(
    row_kernel,
    struct((128, 256)),
    [SMEM] * 2 + [VMEM] * 6,
    [
        pltpu.VMEM((20, 2, 16, 256), F32),
        pltpu.VMEM((256, 768), BF),
        pltpu.VMEM((256, 768), BF),
        pltpu.VMEM((128, 768), BF),
        pltpu.VMEM((128, 768), BF),
    ],
    flops=1_000_000_000,
    name="rows",
)
finish_call = call(
    finish_kernel, struct((128, 256)), [ANY] + [VMEM] * 4, [INTS, pltpu.SemaphoreType.DMA((1,))], flops=300_000_000, name="finish"
)


def routes(shards):
    pairs = [(i, i + 1) for i in range(1, shards - 1, 2)]
    near = pairs + [(b, a) for a, b in pairs]
    far = [(i, i + 2) for i in range(0, shards - 2, 2)] + [(i, i - 2) for i in range(3, shards, 2)]
    pairs = [(i, i + 1) for i in range(0, shards, 2)]
    inner = pairs + [(b, a) for a, b in pairs]
    onward = [(i, (i // 2 + 1) * 2 + 1 - i % 2) for i in range(shards - 2)]
    ring = [(a, b) for a, b in onward if a // 2 % 2 == 0]
    cross = [(a, b) for a, b in onward if a // 2 % 2 == 1]
    return near, far, inner, ring + [(b, a) for a, b in ring], cross + [(b, a) for a, b in cross]


def groups(shards, columns):
    return [
        [(2 * team + (side ^ team % 2)) * columns + c for c in range(columns) for side in range(2)] for team in range(shards // 2)
    ]


def integers(node_count):
    shards = node_count.shape[0]
    team, side = lax.axis_index("team"), lax.axis_index("r")
    here = 2 * team + side
    row = jnp.arange(16, dtype=jnp.int32)[:, None]
    column = jnp.arange(shards, dtype=jnp.int32)[None, :]
    near = jnp.clip(here + row - (COUNTS + 2), 0, shards - 1)
    wanted = (
        (row == TOTAL)
        | ((row == TEAM_BEGIN) & (column < 2 * team))
        | ((row == HERE_BEGIN) & (column < here))
        | ((row >= COUNTS) & (row < ODD) & (column == near))
    )
    sums = jnp.sum(jnp.where(wanted, node_count[None, :], 0), axis=1)
    return sums + jnp.where(row[:, 0] == SIDE, side, 0) + jnp.where(row[:, 0] == ODD, team & 1, 0)


def on_device(densities, hamiltonian, couplings, gamma, coeff, node_count):
    hier = ("team", "r")
    shards = node_count.shape[0]
    everyone = ("team", "r", "col")
    lists = groups(shards, lax.axis_size("col"))
    near, far, inner, ring, cross = routes(shards)

    def exchange(v):
        return lax.all_to_all(v, everyone, 0, 0, axis_index_groups=lists, tiled=True)

    ints = integers(node_count)
    wide = jnp.broadcast_to(ints[:, None], (16, 128))
    reals = jnp.concatenate([gamma, coeff.reshape(4), jnp.sqrt(jnp.arange(ROOTS, dtype=F32))])
    sent, x = lax.optimization_barrier((own_call(densities), densities))
    got = exchange(sent)
    p1 = lax.ppermute(x, hier, near)
    own, ring_edge, cross_edge = edge_call(wide, got)
    cross_got = lax.ppermute(cross_edge, hier, cross)
    ring_got = lax.ppermute(ring_edge, hier, ring)
    own, p1, x, hamiltonian, couplings = lax.optimization_barrier((own, p1, x, hamiltonian, couplings))
    vhi, vlo, hhi, hlo = weights_call(hamiltonian, couplings)
    wide_reals = jnp.broadcast_to(reals[:8, None], (8, 128))
    pair, edge = pair_call(ints, x, p1)
    own, pair, edge = lax.optimization_barrier((own, pair, edge))
    back_sent = column_call(wide, wide_reals, own, cross_got, ring_got, vhi, vlo)
    back_sent, pair, edge = lax.optimization_barrier((back_sent, pair, edge))
    back_got = exchange(back_sent)
    p2 = lax.ppermute(edge, hier, far)
    pair = lax.ppermute(pair, hier, inner)
    base = row_call(ints, reals, x, p1, p2, pair, vhi, vlo)
    out = finish_call(ints, back_got, base, hhi, hlo)
    return out.reshape(4, 2, 16, 256)


def solution(mesh):
    devices = mesh.devices
    inside = Mesh(devices.reshape(devices.shape[0] // 2, 2, devices.shape[1]), ("team", "r", "col"))
    spec = P(("team", "r"), None, "col", None)
    return jax.shard_map(
        on_device,
        mesh=inside,
        in_specs=(spec, P(), P(), P(), P(), P()),
        out_specs=spec,
        check_vma=False,
    )
```

```python
import jax
import jax.numpy as jnp
from jax import lax
from jax.experimental import pallas as pl
from jax.experimental.pallas import tpu as pltpu
from jax.sharding import Mesh, PartitionSpec as P

STEP = 0.2
HALF2 = 0.5 * STEP * STEP
SLOTS = 4
TOTAL, TEAM_BEGIN, HERE_BEGIN, SIDE, COUNTS, ODD = 0, 1, 2, 3, 4, 9
ROOTS = 72
BF = jnp.bfloat16
F32 = jnp.float32


def split(v):
    hi = v.astype(BF)
    return hi, (v - hi.astype(F32)).astype(BF)


def dot(a, b):
    return jnp.dot(a, b, preferred_element_type=F32)


def granules(vs):
    lane = lax.broadcasted_iota(jnp.int32, vs[0].shape, 1) // 16
    turned = [vs[0]] + [pltpu.roll(vs[k], 16 * k, 1) for k in range(1, 8)]
    cur = [turned[-k % 8] for k in range(8)]
    for bit in (1, 2, 4):
        pick = (lane & bit) != 0
        cur = [jnp.where(pick, cur[(m - bit) % 8], cur[m]) for m in range(8)]
    return [cur[0]] + [pltpu.roll(cur[m], 128 - 16 * m, 1) for m in range(1, 8)]


def once(method):
    def cached(self, p):
        key = (method.__name__, p)
        if key not in self.memo:
            self.memo[key] = method(self, p)
        return self.memo[key]

    return cached


class Nodes:
    def __init__(self, total, begin, reals, root):
        self.memo = {}
        self.live = (total >> 1) << 1
        self.begin = begin
        self.base = begin - 4
        self.gamma = (reals[0], reals[1])
        self.re = (reals[2], reals[4])
        self.im = (reals[3], reals[5])
        self.root = root

    @once
    def up(self, p):
        g = self.base + p
        return self.root((g >> 1) + 1) * jnp.where((g >= 0) & (g + 2 < self.live), 1.0, 0.0)

    @once
    def down(self, p):
        g = self.base + p
        return self.root(g >> 1) * jnp.where((g >= 2) & (g < self.live), 1.0, 0.0)

    @once
    def twist(self, p):
        g = self.base + p
        n = (g >> 1).astype(F32)
        ok = (g >= 0) & (g < self.live)
        return jnp.where(ok & (g + 2 < self.live), n + 1.0, 0.0) - jnp.where(ok & (g >= 2), n, 0.0)

    @once
    def even(self, p):
        g = self.base + p
        return jnp.where((g >= 0) & (g < self.live) & ((g & 1) == 0), 1.0, 0.0).astype(F32)

    @once
    def odd(self, p):
        g = self.base + p
        return jnp.where((g >= 0) & (g < self.live) & ((g & 1) == 1), 1.0, 0.0).astype(F32)

    @once
    def damp(self, p):
        g = self.base + p
        n0 = (g >> 1).astype(F32)
        n1 = (g & 1).astype(F32)
        return n0 * self.gamma[0] + n1 * self.gamma[1]


def scaled(s, v):
    return (s * v[0], s * v[1])


def plus(a, b):
    return (a[0] + b[0], a[1] + b[1])


def times(re, im, v):
    return (re * v[0] - im * v[1], re * v[1] + im * v[0])


def both(nodes, x, p, re, im):
    r = plus(scaled(nodes.up(p), x[p + 2]), scaled(re * nodes.down(p), x[p - 2]))
    t = scaled(im * nodes.down(p), x[p - 2])
    return (r[0] - t[1], r[1] + t[0]), (r[0] + t[1], r[1] - t[0])


def both1(nodes, x, p, re, im):
    r = plus(scaled(nodes.even(p), x[p + 1]), scaled(re * nodes.odd(p), x[p - 1]))
    t = scaled(im * nodes.odd(p), x[p - 1])
    return (r[0] - t[1], r[1] + t[0]), (r[0] + t[1], r[1] - t[0])


def first_order(nodes, x, p, re, im):
    here = nodes.damp(p)

    def w(q):
        return STEP - HALF2 * (here + nodes.damp(q))

    zero = scaled(w(p), x[p])
    up, down = scaled(w(p + 2) * nodes.up(p), x[p + 2]), scaled(w(p - 2) * nodes.down(p), x[p - 2])
    one = plus(up, times(re[0], im[0], down))
    up, down = scaled(w(p + 1) * nodes.even(p), x[p + 1]), scaled(w(p - 1) * nodes.odd(p), x[p - 1])
    two = plus(up, times(re[1], im[1], down))
    return zero, one, two


def put(hi_ref, lo_ref, col, j, rows, v):
    hi, lo = split(jnp.concatenate([v[0], v[1]], axis=0))
    at = pl.ds(j * rows, rows)
    hi_ref[at, 256 * col : 256 * col + 256] = hi
    lo_ref[at, 256 * col : 256 * col + 256] = lo


def product(hi, lo, ghi, glo):
    rows = hi.shape[0]
    both_parts = dot(jnp.concatenate([hi, lo], axis=0), ghi)
    return both_parts[:rows] + both_parts[rows:] + dot(hi, glo)


def times_weights(hi_ref, lo_ref, ghi_ref, glo_ref):
    return product(hi_ref[...], lo_ref[...], ghi_ref[...], glo_ref[...])


def weights_kernel(h_ref, q_ref, vhi, vlo, hhi, hlo):
    for b in range(3):
        hi, lo = split(h_ref[...] if b == 0 else q_ref[b - 1])
        vhi[256 * b : 256 * b + 256, :] = hi
        vlo[256 * b : 256 * b + 256, :] = lo
        hhi[:, 256 * b : 256 * b + 256] = hi
        hlo[:, 256 * b : 256 * b + 256] = lo


def own_kernel(x_ref, o_ref):
    o_ref[...] = x_ref[...].T.reshape(32, 8, 128)


def fetch(pairs, sem):
    copies = [pltpu.make_async_copy(source, target, sem.at[i]) for i, (source, target) in enumerate(pairs)]
    for copy in copies:
        copy.start()
    return copies


def taken(ref, i):
    return ref[i : i + 1, 0:1][0, 0]


def edge_kernel(wide_ref, got_ref, own_ref, ring_ref, cross_ref, y_ref):
    side, before, here, after, odd = (taken(wide_ref, i) for i in (SIDE, COUNTS + 1, COUNTS + 2, COUNTS + 3, ODD))
    own, other = jnp.where(side == 0, here, before), jnp.where(side == 0, after, here)
    for place in range(2):
        vs = []
        for low in range(8):
            vs.append(jnp.concatenate([got_ref[(8 * high + low) * 2 + place] for high in range(2)], axis=0))
        for m, v in enumerate(granules(vs)):
            y_ref[SLOTS * place + m // 2, m % 2] = jnp.concatenate([v[:8], v[8:]], axis=1)

    def node(j):
        return y_ref[jnp.where(j < own, SLOTS * odd + j, SLOTS * (1 - odd) + jnp.clip(j - own, 0, SLOTS - 1))]

    for j in range(8):
        own_ref[j] = node(j)
    behind, ahead = jnp.where(odd == 0, own + other - 4, 0), jnp.where(odd == 0, 0, own + other - 4)
    for j in range(4):
        ring_ref[j] = node(behind + j)
        cross_ref[j] = node(ahead + j)


def pair_kernel(ints_ref, x_ref, near_ref, o_ref, far_ref):
    far_ref[...] = x_ref[pl.ds(jnp.where(ints_ref[SIDE] == 0, ints_ref[COUNTS + 2] - 2, 0), 2)]
    o_ref[0:4] = x_ref[...]
    o_ref[4:6] = near_ref[pl.ds(jnp.where(ints_ref[SIDE] == 0, ints_ref[COUNTS + 1] - 2, 0), 2)]


def column_kernel(
    wide_ref, reals_ref, own_ref, cross_ref, ring_ref, ghi_ref, glo_ref, o_ref, y_ref, hi_ref, lo_ref, hi2_ref, lo2_ref, z_ref, send_ref, out_sem
):
    total, begin, side, before, here, after, odd = (
        taken(wide_ref, i) for i in (TOTAL, TEAM_BEGIN, SIDE, COUNTS + 1, COUNTS + 2, COUNTS + 3, ODD)
    )
    reals = [taken(reals_ref, i) for i in range(6)]
    own, other = jnp.where(side == 0, here, before), jnp.where(side == 0, after, here)

    def root(n):
        return jnp.sqrt(jnp.full((8, 256), jnp.maximum(n, 0).astype(F32)))

    nodes = Nodes(total, begin, reals, root)
    re, im = nodes.re, nodes.im
    y_ref[4:12] = own_ref[...]
    y_ref[12:16] = ring_ref[...]
    y_ref[pl.ds(jnp.where(odd == 0, 4 + own + other, 0), 4)] = ring_ref[...]
    y_ref[pl.ds(jnp.where(odd == 0, 0, 4 + own + other), 4)] = cross_ref[...]
    x = []
    for p in range(16):
        v = y_ref[p]
        x.append((v[0], v[1]))
    for p in range(2, 14):
        put(hi_ref, lo_ref, 0, p - 2, 16, x[p])
        put(hi_ref, lo_ref, 1, p - 2, 16, both(nodes, x, p, re[0], im[0])[0])
        put(hi_ref, lo_ref, 2, p - 2, 16, both1(nodes, x, p, re[1], im[1])[0])
    sums = times_weights(hi_ref, lo_ref, ghi_ref, glo_ref)
    hi, lo = hi_ref[32:160, :256], lo_ref[32:160, :256]
    alone = [product(hi, lo, ghi_ref[256 * b : 256 * b + 256, :], glo_ref[256 * b : 256 * b + 256, :]) for b in (1, 2)]
    s = {p: (sums[16 * p - 32 : 16 * p - 24], sums[16 * p - 24 : 16 * p - 16]) for p in range(2, 14)}
    for j in range(8):
        p = j + 4
        left, right = zip(both(nodes, s, p, re[0], im[0]), both1(nodes, s, p, re[1], im[1]))
        for col, (v, t) in enumerate(zip(first_order(nodes, x, p, re, im), (s[p], *left))):
            put(hi2_ref, lo2_ref, col, j, 16, (v[1] - HALF2 * t[0], -v[0] - HALF2 * t[1]))
        z_ref[1, j] = (2.0 * HALF2) * sums[16 * j + 32 : 16 * j + 48].reshape(2, 8, 256)
        for b, twist in enumerate((nodes.twist(p), nodes.even(p) - nodes.odd(p))):
            by = im[b] * twist
            z_ref[2 + b, j, 0] = (2.0 * HALF2) * (right[b][0] + by * alone[b][16 * j + 8 : 16 * j + 16])
            z_ref[2 + b, j, 1] = (2.0 * HALF2) * (right[b][1] - by * alone[b][16 * j : 16 * j + 8])

    def send(z):
        for r in range(2):
            vs = []
            for m in range(8):
                v = z_ref[z, m // 2 if r == 0 else own + m // 2, m % 2]
                vs.append(jnp.concatenate([v[:, :128], v[:, 128:]], axis=0))
            for low, v in enumerate(granules(vs)):
                for high in range(2):
                    send_ref[z, (8 * high + low) * 2 + (odd if r == 0 else 1 - odd)] = v[8 * high : 8 * high + 8]
        copy = pltpu.make_async_copy(send_ref.at[z], o_ref.at[:, 8 * z : 8 * z + 8], out_sem.at[z])
        copy.start()
        return copy

    copies = [send(z) for z in range(1, 4)]
    last = times_weights(hi2_ref, lo2_ref, ghi_ref, glo_ref)
    z_ref[0] = last.reshape(8, 2, 8, 256)
    for copy in [*copies, send(0)]:
        copy.wait()


def row_kernel(
    ints_ref, reals_ref, x_ref, p1_ref, p2_ref, pair_ref, ghi_ref, glo_ref, o_ref, w_ref, hi_ref, lo_ref, hi2_ref, lo2_ref
):

    def root(n):
        return reals_ref[jnp.clip(n, 0, ROOTS - 1) + 6]

    nodes = Nodes(ints_ref[TOTAL], ints_ref[HERE_BEGIN], [reals_ref[i] for i in range(6)], root)
    re, im = nodes.re, (-nodes.im[0], -nodes.im[1])
    up = ints_ref[SIDE]
    farther, below, own, above = (ints_ref[COUNTS + i] for i in range(4))
    w_ref[8:12] = x_ref[...]
    w_ref[pl.ds(4 + 8 * up, 4)] = p1_ref[...]
    w_ref[pl.ds(jnp.where(up == 0, farther - 2, 16), 2)] = p2_ref[...]
    w_ref[pl.ds(12 - 8 * up, 4)] = pair_ref[0:4]
    w_ref[pl.ds(jnp.where(up == 0, 16, farther - 2), 2)] = pair_ref[4:6]

    def slot(p):
        j = p - 4
        if j < 0:
            return jnp.where(j + below >= 0, 4 + j + below, farther + j + below)
        return jnp.where(j < own, 8 + j, jnp.where(j < own + above, 12 + j - own, jnp.minimum(16 + j - own - above, 19)))

    x = []
    for p in range(12):
        v = w_ref[slot(p)]
        x.append((v[0], v[1]))
    for p in range(2, 10):
        put(hi_ref, lo_ref, 0, p - 2, 32, x[p])
        put(hi_ref, lo_ref, 1, p - 2, 32, both(nodes, x, p, re[0], im[0])[0])
        put(hi_ref, lo_ref, 2, p - 2, 32, both1(nodes, x, p, re[1], im[1])[0])
    sums = times_weights(hi_ref, lo_ref, ghi_ref, glo_ref)
    s = {p: (sums[32 * p - 64 : 32 * p - 48], sums[32 * p - 48 : 32 * p - 32]) for p in range(2, 10)}
    for j in range(4):
        p = j + 4
        mixed = (s[p], both(nodes, s, p, re[0], im[0])[0], both1(nodes, s, p, re[1], im[1])[0])
        for col, (v, t) in enumerate(zip(first_order(nodes, x, p, re, im), mixed)):
            put(hi2_ref, lo2_ref, col, j, 32, (-v[1] - HALF2 * t[0], v[0] - HALF2 * t[1]))
    right = times_weights(hi2_ref, lo2_ref, ghi_ref, glo_ref)
    for j in range(4):
        d = nodes.damp(j + 4)
        keep = 1.0 - STEP * d + HALF2 * d * d
        old = x_ref[j].reshape(32, 256)
        live = (j < own) & (nodes.begin + j < nodes.live)
        o_ref[32 * j : 32 * j + 32, :] = jnp.where(live, keep * old + right[32 * j : 32 * j + 32], old)


def finish_kernel(ints_in, got_ref, base_ref, ghi_ref, glo_ref, o_ref, ints_ref, sem):
    fetched = fetch([(ints_in, ints_ref)], sem)
    his, los = [], []
    for z in range(1, 4):
        hi, lo = split(got_ref[:, 8 * z : 8 * z + 8, :].reshape(256, 128))
        his.append(hi)
        los.append(lo)
    hi, lo = jnp.concatenate(his, axis=0), jnp.concatenate(los, axis=0)
    g = ghi_ref[...]
    out = dot(g, hi) + dot(g, lo) + dot(glo_ref[...], hi) + got_ref[:, :8, :].reshape(256, 128)
    out = out.T
    for copy in fetched:
        copy.wait()
    own, begin, limit = ints_ref[COUNTS + 2], ints_ref[HERE_BEGIN], (ints_ref[TOTAL] >> 1) << 1
    for j in range(4):
        live = (j < own) & (begin + j < limit)
        rows = slice(32 * j, 32 * j + 32)
        o_ref[rows, :] = base_ref[rows, :] + jnp.where(live, out[rows], 0.0)


SMEM = pl.BlockSpec(memory_space=pltpu.SMEM)
VMEM = pl.BlockSpec(memory_space=pltpu.VMEM)
ANY = pl.BlockSpec(memory_space=pl.ANY)


def call(kernel, outs, specs, scratch=(), flops=1_000_000, name=None, out_specs=None, aliases=None):
    return pl.pallas_call(
        kernel,
        out_shape=outs,
        in_specs=specs,
        out_specs=out_specs or jax.tree.map(lambda _: VMEM, outs),
        input_output_aliases=aliases or {},
        scratch_shapes=list(scratch),
        compiler_params=pltpu.CompilerParams(vmem_limit_bytes=48 * 1024 * 1024),
        cost_estimate=pl.CostEstimate(flops=flops, bytes_accessed=4_000_000, transcendentals=0),
        name=name,
    )


def struct(shape, dtype=F32):
    return jax.ShapeDtypeStruct(shape, dtype)


weights_call = call(
    weights_kernel,
    (struct((768, 256), BF), struct((768, 256), BF), struct((256, 768), BF), struct((256, 768), BF)),
    [VMEM] * 2,
    name="weights",
)
own_call = call(own_kernel, struct((32, 8, 128)), [VMEM], name="own")
INTS = pltpu.SMEM((16,), jnp.int32)
edge_call = call(
    edge_kernel,
    (struct((8, 2, 8, 256)), struct((4, 2, 8, 256)), struct((4, 2, 8, 256))),
    [VMEM] * 2,
    [pltpu.VMEM((8, 2, 8, 256), F32)],
    name="edge",
)
pair_call = call(pair_kernel, (struct((6, 2, 16, 256)), struct((2, 2, 16, 256))), [SMEM] + [VMEM] * 2, name="pair")
column_call = call(
    column_kernel,
    struct((32, 32, 128)),
    [VMEM] * 7,
    [
        pltpu.VMEM((16, 2, 8, 256), F32),
        pltpu.VMEM((192, 768), BF),
        pltpu.VMEM((192, 768), BF),
        pltpu.VMEM((128, 768), BF),
        pltpu.VMEM((128, 768), BF),
        pltpu.VMEM((4, 8, 2, 8, 256), F32),
        pltpu.VMEM((4, 32, 8, 128), F32),
        pltpu.SemaphoreType.DMA((4,)),
    ],
    flops=1_000_000_000,
    out_specs=ANY,
    name="columns",
)
row_call = call(
    row_kernel,
    struct((128, 256)),
    [SMEM] * 2 + [VMEM] * 6,
    [
        pltpu.VMEM((20, 2, 16, 256), F32),
        pltpu.VMEM((256, 768), BF),
        pltpu.VMEM((256, 768), BF),
        pltpu.VMEM((128, 768), BF),
        pltpu.VMEM((128, 768), BF),
    ],
    flops=1_000_000_000,
    name="rows",
)
finish_call = call(
    finish_kernel, struct((128, 256)), [ANY] + [VMEM] * 4, [INTS, pltpu.SemaphoreType.DMA((1,))], flops=300_000_000, name="finish"
)


def routes(shards):
    pairs = [(i, i + 1) for i in range(1, shards - 1, 2)]
    near = pairs + [(b, a) for a, b in pairs]
    far = [(i, i + 2) for i in range(0, shards - 2, 2)] + [(i, i - 2) for i in range(3, shards, 2)]
    pairs = [(i, i + 1) for i in range(0, shards, 2)]
    inner = pairs + [(b, a) for a, b in pairs]
    onward = [(i, (i // 2 + 1) * 2 + 1 - i % 2) for i in range(shards - 2)]
    ring = [(a, b) for a, b in onward if a // 2 % 2 == 0]
    cross = [(a, b) for a, b in onward if a // 2 % 2 == 1]
    return near, far, inner, ring + [(b, a) for a, b in ring], cross + [(b, a) for a, b in cross]


def groups(shards, columns):
    return [
        [(2 * team + (side ^ team % 2)) * columns + c for c in range(columns) for side in range(2)] for team in range(shards // 2)
    ]


def integers(node_count):
    shards = node_count.shape[0]
    team, side = lax.axis_index("team"), lax.axis_index("r")
    here = 2 * team + side
    row = jnp.arange(16, dtype=jnp.int32)[:, None]
    column = jnp.arange(shards, dtype=jnp.int32)[None, :]
    near = jnp.clip(here + row - (COUNTS + 2), 0, shards - 1)
    wanted = (
        (row == TOTAL)
        | ((row == TEAM_BEGIN) & (column < 2 * team))
        | ((row == HERE_BEGIN) & (column < here))
        | ((row >= COUNTS) & (row < ODD) & (column == near))
    )
    sums = jnp.sum(jnp.where(wanted, node_count[None, :], 0), axis=1)
    return sums + jnp.where(row[:, 0] == SIDE, side, 0) + jnp.where(row[:, 0] == ODD, team & 1, 0)


def on_device(densities, hamiltonian, couplings, gamma, coeff, node_count):
    hier = ("team", "r")
    shards = node_count.shape[0]
    everyone = ("team", "r", "col")
    lists = groups(shards, lax.axis_size("col"))
    near, far, inner, ring, cross = routes(shards)

    def exchange(v):
        return lax.all_to_all(v, everyone, 0, 0, axis_index_groups=lists, tiled=True)

    ints = integers(node_count)
    wide = jnp.broadcast_to(ints[:, None], (16, 128))
    reals = jnp.concatenate([gamma, coeff.reshape(4), jnp.sqrt(jnp.arange(ROOTS, dtype=F32))])
    sent, x = lax.optimization_barrier((own_call(densities.reshape(128, 256)), densities))
    got = exchange(sent)
    p1 = lax.ppermute(x, hier, near)
    own, ring_edge, cross_edge = edge_call(wide, got)
    cross_got = lax.ppermute(cross_edge, hier, cross)
    ring_got = lax.ppermute(ring_edge, hier, ring)
    own, p1, x, hamiltonian, couplings = lax.optimization_barrier((own, p1, x, hamiltonian, couplings))
    vhi, vlo, hhi, hlo = weights_call(hamiltonian, couplings)
    wide_reals = jnp.broadcast_to(reals[:8, None], (8, 128))
    pair, edge = pair_call(ints, x, p1)
    own, pair, edge = lax.optimization_barrier((own, pair, edge))
    back_sent = column_call(wide, wide_reals, own, cross_got, ring_got, vhi, vlo)
    back_sent, pair, edge = lax.optimization_barrier((back_sent, pair, edge))
    back_got = exchange(back_sent)
    p2 = lax.ppermute(edge, hier, far)
    pair = lax.ppermute(pair, hier, inner)
    base = row_call(ints, reals, x, p1, p2, pair, vhi, vlo)
    out = finish_call(ints, back_got, base, hhi, hlo)
    return out.reshape(4, 2, 16, 256)


def solution(mesh):
    devices = mesh.devices
    inside = Mesh(devices.reshape(devices.shape[0] // 2, 2, devices.shape[1]), ("team", "r", "col"))
    spec = P(("team", "r"), None, "col", None)
    return jax.shard_map(
        on_device,
        mesh=inside,
        in_specs=(spec, P(), P(), P(), P(), P()),
        out_specs=spec,
        check_vma=False,
    )
```
